32 devices in a mesh: wide: 8 (over z, y), narrow: 4 (over x, core).
Axes of the slice: x: 2, y: 2, z: 4, core: 2. Of those that a mesh axis runs over, the one named last changes fastest.
Arguments:
- main_residual: bfloat16 [32768, 512], P(('wide', 'narrow')), may hold values from -6 to 6
- side_residual: bfloat16 [32768, 512], P(('wide', 'narrow')), may hold values from -6 to 6
- cotangent: bfloat16 [32768, 512], P(('wide', 'narrow')), may hold values from -6 to 6
- lengths: int32 [32, 4], P(('wide', 'narrow')), may hold values from 0 to 1024, as said below
- input_weight: bfloat16 [2, 512, 1536], P(None, ('wide', 'narrow')), may hold values from -0.375 to 0.375
- output_weight: bfloat16 [2, 512, 512], P(None, ('wide', 'narrow')), may hold values from -0.5 to 0.5
- expand_weight: bfloat16 [2, 512, 2048], P(None, ('wide', 'narrow')), may hold values from -0.25 to 0.25
- reduce_weight: bfloat16 [2, 2048, 512], P(None, ('wide', 'narrow')), may hold values from -0.1875 to 0.1875
- vectors: bfloat16 [2, 6144], P(None, ('wide', 'narrow')), may hold values from -0.9 to 1.5
- final_norm: bfloat16 [1024], P(('wide', 'narrow')), may hold values from -0.9 to 1.5
Outputs:
- layer_out: bfloat16 [32768, 512], P(('wide', 'narrow'))
- grad_main: float32 [32768, 512], P(('wide', 'narrow'))
- grad_side: float32 [32768, 512], P(('wide', 'narrow'))
- grad_input_weight: float32 [2, 512, 1536], P(None, ('wide', 'narrow'))
- grad_output_weight: float32 [2, 512, 512], P(None, ('wide', 'narrow'))
- grad_expand: float32 [2, 512, 2048], P(None, ('wide', 'narrow'))
- grad_reduce: float32 [2, 2048, 512], P(None, ('wide', 'narrow'))
- grad_vectors: float32 [2, 6144], P(None, ('wide', 'narrow'))
- grad_final: float32 [1024], P(('wide', 'narrow'))
The draws below stay inside these ranges and needn't reach their ends.
Inputs may be any that keep to these rules, and one draw needn't show every extreme that they name: Each row is either one sequence, with a length of half of 1024 to 1024 first and three zeros after it, or four sequences with lengths of 1 to 256. Both kinds occur in every draw, and a length of 1024 and one of 256 are reached.
All inputs are finite; a program needn't handle non-finite values.
Results may differ from the reference program's by a relative error of at most 0.024.
Values may be sent and summed in bfloat16 or wider, within the bound.
No kernel may reach another device: no remote copies, remote signals or barrier semaphores. Data moves between devices by JAX's collectives and lax.ppermute only.
A program may use at most 192 MiB of HBM per device.

```python
import jax
import jax.numpy as jnp
from jax import lax

MODEL_WIDTH = 512
HEADS = 8
HEAD_DIM = 64
FF = 2048
LAYERS = 2
LONG_LENGTH = 1024
SHORT_LENGTH = 256
SLOT_TOTAL = 32
TOKENS = 32768


def draw_lengths(key, part):
    key = jax.random.fold_in(key, 5)
    key_collection = jax.random.split(key, 5)
    slot_numbers = jnp.arange(SLOT_TOTAL, dtype=jnp.int32)
    sequence_kinds = jax.random.randint(key_collection[0], (SLOT_TOTAL,), 0, 2)
    leading_long = jax.random.randint(key_collection[1], (), 0, SLOT_TOTAL)
    leading_short = (leading_long + jax.random.randint(key_collection[2], (), 1, SLOT_TOTAL)) % SLOT_TOTAL
    sequence_kinds = jnp.where(slot_numbers == leading_long, 1, jnp.where(slot_numbers == leading_short, 0, sequence_kinds))
    long_sequence_lengths = jax.random.randint(key_collection[3], (SLOT_TOTAL,), LONG_LENGTH // 2, LONG_LENGTH + 1)
    long_sequence_lengths = jnp.where(slot_numbers == leading_long, LONG_LENGTH, long_sequence_lengths)
    short_sequence_lengths = jax.random.randint(key_collection[4], (SLOT_TOTAL, 4), 1, SHORT_LENGTH + 1)
    corner = (slot_numbers == leading_short)[:, None] & (jnp.arange(4)[None, :] == 0)
    short_sequence_lengths = jnp.where(corner, SHORT_LENGTH, short_sequence_lengths)
    long_token_rows = jnp.concatenate([long_sequence_lengths[:, None], jnp.zeros((SLOT_TOTAL, 3), jnp.int32)], axis=1)
    return jnp.where(sequence_kinds[:, None] == 1, long_token_rows, short_sequence_lengths).astype(jnp.int32)


def gains_and_shifts(gain_key, shift_key, shape_out, gain_spread, shift_spread):
    gains = 1.0 + gain_spread * jax.random.truncated_normal(gain_key, -3.0, 3.0, shape_out, jnp.float32)
    shifts = shift_spread * jax.random.truncated_normal(shift_key, -3.0, 3.0, shape_out, jnp.float32)
    return (gains, shifts)


def draw_vectors(key, part):
    key = jax.random.fold_in(key, 7)
    gain_key, shift_key = jax.random.split(key)
    shape_out = (LAYERS, 8 * MODEL_WIDTH + FF)
    gains, shifts = gains_and_shifts(gain_key, shift_key, shape_out, 0.15, 0.3)
    block_ids = jnp.arange(8 * MODEL_WIDTH + FF)[None, :] // MODEL_WIDTH
    is_gain = (block_ids == 3) | (block_ids == 6)
    return jnp.where(is_gain, gains, shifts).astype(jnp.bfloat16)


def draw_final_norm(key, part):
    key = jax.random.fold_in(key, 9)
    gain_key, shift_key = jax.random.split(key)
    shape_out = (2 * MODEL_WIDTH,)
    gains, shifts = gains_and_shifts(gain_key, shift_key, shape_out, 0.15, 0.3)
    return jnp.where(jnp.arange(2 * MODEL_WIDTH) < MODEL_WIDTH, gains, shifts).astype(jnp.bfloat16)


def steps_of(key, extent, cuts, least, top_value):
    loudness, own = 1.0, jax.random.fold_in(key, 6)
    for axis_at, shards_of in cuts:
        heights = jnp.exp(jax.random.uniform(jax.random.fold_in(own, axis_at), (shards_of,), jnp.float32, least / len(cuts), top_value / len(cuts)))
        loudness = loudness * jnp.repeat(heights, extent[axis_at] // shards_of).reshape([-1 if axis == axis_at else 1 for axis in range(len(extent))])
    return loudness


def normal_values(key, dims, spread, reach, cuts=(), held_as=jnp.bfloat16):
    values = jax.random.normal(key, dims, jnp.float32) * spread
    if len(cuts) > 0:
        values = steps_of(key, dims, cuts, -0.22, 0.18) * values
    return jnp.clip(values, min=-reach, max=reach).astype(held_as)


def setup_inputs(seed: int = 0) -> dict:
    arg_keys = jax.random.split(jax.random.key(seed), 11)
    main_residual = normal_values(arg_keys[0], (TOKENS, MODEL_WIDTH), 1.0, 6.0, ((0, 32),))
    side_residual = normal_values(arg_keys[1], (TOKENS, MODEL_WIDTH), 1.0, 6.0, ((0, 32),))
    cotangent = normal_values(arg_keys[2], (TOKENS, MODEL_WIDTH), 1.0, 6.0, ((0, 32),))
    lengths = draw_lengths(jax.random.fold_in(arg_keys[10], 71), 0)
    input_weight = normal_values(arg_keys[4], (LAYERS, MODEL_WIDTH, 3 * MODEL_WIDTH), (MODEL_WIDTH // 2) ** -0.5, 0.375, ((1, 32),))
    output_weight = normal_values(arg_keys[5], (LAYERS, MODEL_WIDTH, MODEL_WIDTH), (MODEL_WIDTH // 4) ** -0.5, 0.5, ((1, 32),))
    expand_weight = normal_values(arg_keys[6], (LAYERS, MODEL_WIDTH, FF), MODEL_WIDTH ** -0.5, 0.25, ((1, 32),))
    reduce_weight = normal_values(arg_keys[7], (LAYERS, FF, MODEL_WIDTH), (FF // 2) ** -0.5, 0.1875, ((1, 32),))
    vectors = draw_vectors(jax.random.fold_in(arg_keys[10], 71), 0)
    final_norm = draw_final_norm(jax.random.fold_in(arg_keys[10], 71), 0)
    return {"main_residual": main_residual, "side_residual": side_residual, "cotangent": cotangent, "lengths": lengths, "input_weight": input_weight, "output_weight": output_weight, "expand_weight": expand_weight, "reduce_weight": reduce_weight, "vectors": vectors, "final_norm": final_norm}


@jax.custom_vjp
def low(v):
    return lax.optimization_barrier(v.astype(jnp.bfloat16)).astype(jnp.float32)

@jax.custom_vjp
def low_back(v):
    return v

def low_keep(v):
    return (low(v), None)

def low_pass(kept, grad):
    return (grad,)

def back_keep(v):
    return (v, None)

def back_low(kept, grad):
    return (low(grad),)
low.defvjp(low_keep, low_pass)
low_back.defvjp(back_keep, back_low)
HIGHEST = lax.Precision.HIGHEST

def layer_norm(values, gain, shift):
    centered = values - lax.optimization_barrier(jnp.mean(values, axis=-1, keepdims=True))
    variance = lax.optimization_barrier(jnp.mean(centered * centered, axis=-1, keepdims=True))
    return centered * lax.rsqrt(variance + 1e-05) * gain + shift

def exact_dot(left, right):
    return jnp.dot(left, right, precision=HIGHEST, preferred_element_type=jnp.float32)

def allowed_pairs(bounds):
    position = jnp.arange(LONG_LENGTH, dtype=jnp.int32)
    single = bounds[1] == 0
    segment = jnp.where(single, 0, position // SHORT_LENGTH).astype(jnp.int32)
    inside = jnp.where(single, position, position % SHORT_LENGTH)
    alive = inside < bounds[segment]
    return (segment[:, None] == segment[None, :]) & alive[None, :]

def slot_forward(main_rows, side_rows, allowed, weight_set):
    input_weight, output_weight, expand_weight, reduce_weight, vectors, final_norm = weight_set
    score_scale = HEAD_DIM ** (-0.5)
    for layer_index in range(LAYERS):
        layer_vectors = vectors[layer_index]
        pieces = [layer_vectors[block_index * MODEL_WIDTH:(block_index + 1) * MODEL_WIDTH] for block_index in range(8)]
        up_bias = layer_vectors[8 * MODEL_WIDTH:]
        bias_in = jnp.concatenate([pieces[0], jnp.zeros((MODEL_WIDTH,), jnp.float32), pieces[1]])
        packed = exact_dot(low(main_rows), input_weight[layer_index]) + bias_in
        packed = low(low_back(packed))
        queries = packed[:, :MODEL_WIDTH].reshape(LONG_LENGTH, HEADS, HEAD_DIM)
        key_rows = packed[:, MODEL_WIDTH:2 * MODEL_WIDTH].reshape(LONG_LENGTH, HEADS, HEAD_DIM)
        value_rows = packed[:, 2 * MODEL_WIDTH:].reshape(LONG_LENGTH, HEADS, HEAD_DIM)
        scores = jnp.einsum('qhd,khd->hqk', queries, key_rows, precision=HIGHEST) * score_scale
        scores = jnp.where(allowed[None], low_back(scores), -1000000000.0)
        probabilities = low(jax.nn.softmax(scores, axis=-1))
        context = jnp.einsum('hqk,khd->qhd', probabilities, value_rows, precision=HIGHEST).reshape(LONG_LENGTH, MODEL_WIDTH)
        context = low(low_back(context))
        branch = low_back(exact_dot(context, output_weight[layer_index]) + pieces[2])
        main_rows = layer_norm(main_rows + branch, pieces[3], pieces[4])
        side_rows = side_rows + branch
        hidden = low_back(exact_dot(low(main_rows), expand_weight[layer_index]) + up_bias)
        branch = low_back(exact_dot(low(jax.nn.gelu(hidden)), reduce_weight[layer_index]) + pieces[5])
        main_rows = layer_norm(main_rows + branch, pieces[6], pieces[7])
        side_rows = side_rows + branch
    return main_rows + layer_norm(side_rows, final_norm[:MODEL_WIDTH], final_norm[MODEL_WIDTH:])

def reference(main_residual, side_residual, cotangent, lengths, input_weight, output_weight, expand_weight, reduce_weight, vectors, final_norm):
    weight_set = (input_weight.astype(jnp.float32), output_weight.astype(jnp.float32), expand_weight.astype(jnp.float32), reduce_weight.astype(jnp.float32), vectors.astype(jnp.float32), final_norm.astype(jnp.float32))
    main_states = main_residual.astype(jnp.float32).reshape(SLOT_TOTAL, LONG_LENGTH, MODEL_WIDTH)
    side_states = side_residual.astype(jnp.float32).reshape(SLOT_TOTAL, LONG_LENGTH, MODEL_WIDTH)
    incoming_list = cotangent.astype(jnp.float32).reshape(SLOT_TOTAL, LONG_LENGTH, MODEL_WIDTH)

    def one_slot(totals, slot_items):
        main_rows, side_rows, incoming, bounds = slot_items
        allowed = allowed_pairs(bounds)

        def forward(main_in, side_in, weights_in):
            return slot_forward(main_in, side_in, allowed, weights_in)
        result, pullback = jax.vjp(forward, main_rows, side_rows, weight_set)
        grad_main, grad_side, grad_weights = pullback(incoming)
        totals = jax.tree.map(jnp.add, totals, grad_weights)
        return (totals, (result.astype(jnp.bfloat16), grad_main, grad_side))
    zero_grads = jax.tree.map(jnp.zeros_like, weight_set)
    totals, (results, grad_mains, grad_sides) = lax.scan(one_slot, zero_grads, (main_states, side_states, incoming_list, lengths))
    return (results.reshape(TOKENS, MODEL_WIDTH), grad_mains.reshape(TOKENS, MODEL_WIDTH), grad_sides.reshape(TOKENS, MODEL_WIDTH), totals[0], totals[1], totals[2], totals[3], totals[4], totals[5])
```

```python
import functools

import jax
import jax.numpy as jnp
from jax import lax
from jax.experimental import pallas as pl
from jax.experimental.pallas import tpu as pltpu
from jax.sharding import PartitionSpec as P

HEAD_DIM = 64
AXES = ("wide", "narrow")
F32 = jnp.float32
BF16 = jnp.bfloat16
NN = (((1,), (0,)), ((), ()))
NT = (((1,), (1,)), ((), ()))
TN = (((0,), (0,)), ((), ()))
MASKED = -1000000000.0
VMEM_LIMIT = 60 * 2**20
BLOCK = 16
VMEM = pltpu.VMEM
ANY = pl.ANY


def mm(left, right, dims):
    return lax.dot_general(left, right, dims, preferred_element_type=F32)


def whole(memory=VMEM):
    return pl.BlockSpec(memory_space=memory)


def fixed(shape):
    zeros = (0,) * len(shape)
    return pl.BlockSpec(shape, lambda step: zeros)


def rows_of(tile, width):
    return pl.BlockSpec((tile, width), lambda step: (step, 0))


def each_slot(order_ref, stream, refs, act):
    for index, ref in enumerate(refs):
        count = ref.shape[0]

        def one(slot, carry, ref=ref, base=index * count):
            act(ref, slot, order_ref[stream, base + slot])
            return carry

        lax.fori_loop(0, count, one, 0)


def wait_all(ref, sem):
    pltpu.make_async_copy(ref, ref, sem).wait()


def fetch_attn(order_ref, alpha, beta, w_ref, sem):
    def fetch_qk(ref, slot, owner):
        pltpu.make_async_copy(ref.at[slot], w_ref.at[pl.ds(0, 2), owner], sem).start()

    def fetch_v(ref, slot, owner):
        pltpu.make_async_copy(ref.at[slot, 0], w_ref.at[2, owner], sem).start()

    each_slot(order_ref, 0, alpha, fetch_qk)
    each_slot(order_ref, 1, beta, fetch_v)


def attn_forward_body(
    order_ref,
    bounds_ref,
    x_ref,
    vec_ref,
    *refs,
):
    alpha, beta = refs[:4], refs[4:8]
    e_ref, qkv_ref, ctx_ref, rinv_ref, w_ref, aux_ref, rows_ref, sem = refs[8:]
    pair = pl.program_id(0)
    tokens, features = x_ref.shape
    lane = lax.broadcasted_iota(jnp.int32, (tokens, 128), 1)
    low_half = lane < HEAD_DIM

    @pl.when(pair == 0)
    def _():
        fetch_attn(order_ref, alpha, beta, w_ref, sem)
        token = lax.broadcasted_iota(jnp.int32, (tokens, 128), 0)
        column = lane % HEAD_DIM
        single = bounds_ref[0, 1] == 0
        quarter = tokens // 4
        segment = jnp.where(single, 0, token // quarter)
        inside = jnp.where(single, token, token % quarter)
        own = column == segment
        bound = jnp.where(
            segment == 0,
            bounds_ref[0, 0],
            jnp.where(
                segment == 1,
                bounds_ref[0, 1],
                jnp.where(segment == 2, bounds_ref[0, 2], bounds_ref[0, 3]),
            ),
        )
        alive = own & (inside < bound)
        aux_ref[0] = jnp.where(own, 1.0, 0.0).astype(BF16)
        aux_ref[1] = jnp.where(alive | (column >= 4), 0.0, MASKED).astype(BF16)
        wait_all(w_ref, sem)
        x = x_ref[...]
        for part in range(3):
            packed = mm(x, w_ref[part].reshape(features, features), NN)
            if part == 0:
                packed = (packed + vec_ref[0:1]).astype(BF16) * BF16(0.125)
            elif part == 2:
                packed = (packed + vec_ref[1:2]).astype(BF16)
            else:
                packed = packed.astype(BF16)
            for index in range(features // 128):
                qkv_ref[part, index] = packed[:, index * 128 : (index + 1) * 128]

    query = qkv_ref[0, pair]
    key = qkv_ref[1, pair]
    value_t = qkv_ref[2, pair].T
    ones = jnp.ones((16, tokens), BF16)
    chunk = 256
    outs = []
    for head in range(2):
        inside_head = low_half if head == 0 else ~low_half
        query_aug = jnp.where(inside_head, query, aux_ref[0])
        key_aug = jnp.where(inside_head, key, aux_ref[1])
        value_aug = jnp.concatenate(
            [value_t[head * HEAD_DIM : (head + 1) * HEAD_DIM], ones], axis=0
        )
        parts = []
        for start in range(0, tokens, chunk):
            scores = mm(key_aug, query_aug[start : start + chunk], NT)
            top = jnp.max(scores, axis=0, keepdims=True)
            exponent = jnp.exp(scores - top).astype(BF16)
            e_ref[head, :, start : start + chunk] = exponent
            mixed = mm(value_aug, exponent, NN)
            inverse = 1.0 / mixed[HEAD_DIM : HEAD_DIM + 1]
            rows_ref[pl.ds(pair * 2 + head, 1), start : start + chunk] = inverse
            parts.append(mixed[:HEAD_DIM] * inverse)
        outs.append(jnp.concatenate(parts, axis=1))
    ctx_ref[...] = jnp.concatenate(outs, axis=0).T.astype(BF16)

    @pl.when(pair == pl.num_programs(0) - 1)
    def _():
        rinv_ref[...] = jnp.concatenate(
            [rows_ref[...], jnp.zeros((120, tokens), F32)], axis=0
        ).T


def attn_forward(order, bounds, x, vec, weights):
    tokens, features = x.shape
    pairs = features // 128
    out_shape = (
        jax.ShapeDtypeStruct((2 * pairs, tokens, tokens), BF16),
        jax.ShapeDtypeStruct((3, pairs, tokens, 128), BF16),
        jax.ShapeDtypeStruct((tokens, features), BF16),
        jax.ShapeDtypeStruct((tokens, 128), F32),
    )
    return pl.pallas_call(
        attn_forward_body,
        grid=(pairs,),
        out_shape=out_shape,
        in_specs=[
            whole(pltpu.SMEM),
            whole(pltpu.SMEM),
            fixed(x.shape),
            fixed(vec.shape),
        ]
        + [whole(ANY)] * len(weights),
        out_specs=(
            pl.BlockSpec((2, tokens, tokens), lambda step: (step, 0, 0)),
            fixed((3, pairs, tokens, 128)),
            pl.BlockSpec((tokens, 128), lambda step: (0, step)),
            fixed((tokens, 128)),
        ),
        scratch_shapes=[
            VMEM((3, features // BLOCK, BLOCK, features), BF16),
            VMEM((2, tokens, 128), BF16),
            VMEM((2 * pairs, tokens), F32),
            pltpu.SemaphoreType.DMA,
        ],
        compiler_params=pltpu.CompilerParams(vmem_limit_bytes=VMEM_LIMIT),
        cost_estimate=pl.CostEstimate(
            flops=14 * 10**9, bytes_accessed=24 * 10**6, transcendentals=0
        ),
        name="attn_forward",
    )(order, bounds, x, vec, *weights)


def normed(z):
    centered = z - jnp.mean(z, axis=-1, keepdims=True)
    variance = jnp.mean(centered * centered, axis=-1, keepdims=True)
    rstd = lax.rsqrt(variance + 1e-05)
    return centered * rstd, rstd


def norm_back(grad, gain, xhat, rstd):
    scaled = grad * gain
    first = jnp.mean(scaled, axis=-1, keepdims=True)
    second = jnp.mean(scaled * xhat, axis=-1, keepdims=True)
    return rstd * (scaled - first - xhat * second)


GELU_A = 0.7978845608028654
GELU_B = 0.044715


def gelu_tanh(hidden):
    square = hidden * hidden
    return jnp.tanh(hidden * (GELU_A + (GELU_A * GELU_B) * square)), square


def gelu(hidden):
    tanh, _ = gelu_tanh(hidden)
    half = 0.5 * hidden
    return half + half * tanh


def gelu_both(hidden):
    tanh, square = gelu_tanh(hidden)
    half = 0.5 * hidden
    cdf = 0.5 + 0.5 * tanh
    slope = GELU_A + (3.0 * GELU_A * GELU_B) * square
    return hidden * cdf, cdf + half * (1.0 - tanh * tanh) * slope


def column_sum(ref, row, values):
    ref[row : row + 1] += jnp.sum(values.astype(F32), axis=0, keepdims=True)


def ffn_body(forward, backward, last, *refs):
    refs = list(refs)
    take = lambda: refs.pop(0)
    order_ref, vec_ref = take(), take()
    alpha, beta = [take() for _ in range(4)], [take() for _ in range(4)]
    ctx_ref = take()
    if forward:
        x_ref, y_ref = take(), take()
    else:
        xh1_ref, xh2_ref, stat_ref, m1b_ref, hid_ref, gm_ref, gs_ref = [take() for _ in range(7)]
    if last:
        cot_ref = take()
    if backward:
        rinv_ref = take()
    if forward and not backward:
        xh1_out, xh2_out, stat_out, m1b_out, hid_out, m2_out, m2b_out, y_out = [
            take() for _ in range(8)
        ]
    if last:
        layer_out, gs_out = take(), take()
    if backward:
        dz1_out, do_out, dvec_out = [take() for _ in range(3)]
        galpha, gbeta = [take() for _ in range(2)], [take() for _ in range(2)]
    wo_ref, up_ref, down_ref, sem_o, sem_u, sem_d = [take() for _ in range(6)]
    if backward:
        act_s, dhid_s, m1b_s, df_s, da_s, ctx_s, gup_s, gdown_s, go_s = [
            take() for _ in range(9)
        ]
    assert not refs
    step = pl.program_id(0)
    tile, features = ctx_ref.shape
    groups = up_ref.shape[0]
    wo = lambda: wo_ref[...].reshape(features, features)
    up = lambda j: up_ref[j].reshape(features, features)
    per = features // BLOCK
    down = lambda j: down_ref[j * per : (j + 1) * per].reshape(features, features)

    @pl.when(step == 0)
    def _():
        def fetch_out(ref, slot, owner):
            pltpu.make_async_copy(ref.at[slot, groups], wo_ref.at[owner], sem_o).start()

        def fetch_up(ref, slot, owner):
            pltpu.make_async_copy(
                ref.at[slot, pl.ds(0, groups)], up_ref.at[:, owner], sem_u
            ).start()

        def fetch_down(ref, slot, owner):
            pltpu.make_async_copy(
                ref.at[slot], down_ref.at[pl.ds(owner * groups, groups)], sem_d
            ).start()

        each_slot(order_ref, 0, alpha, fetch_out)
        each_slot(order_ref, 0, alpha, fetch_up)
        each_slot(order_ref, 1, beta, fetch_down)
        if backward:
            dvec_out[...] = jnp.zeros_like(dvec_out)
        wait_all(wo_ref, sem_o)
        wait_all(up_ref, sem_u)
        wait_all(down_ref, sem_d)

    vec = lambda row: vec_ref[row : row + 1]
    ctx = ctx_ref[...]
    if forward:
        branch = mm(ctx, wo(), NN) + vec(2)
        xh1, rstd1 = normed(x_ref[...].astype(F32) + branch)
        m1 = xh1 * vec(3) + vec(4)
        y = y_ref[...].astype(F32) + branch
        m1b = m1.astype(BF16)
        hidden = [mm(m1b, up(j), NN) + vec(8 + j) for j in range(groups)]
        if backward:
            both = [gelu_both(h) for h in hidden]
            act = [pair[0].astype(BF16) for pair in both]
        else:
            act = [gelu(h).astype(BF16) for h in hidden]
        branch = vec(5)
        for j in range(groups):
            branch = branch + mm(act[j], down(j), NN)
        xh2, rstd2 = normed(m1 + branch)
        m2 = xh2 * vec(6) + vec(7)
        y = y + branch
        if not backward:
            xh1_out[...] = xh1.astype(BF16)
            xh2_out[...] = xh2.astype(BF16)
            stat_out[...] = jnp.where(
                lax.broadcasted_iota(jnp.int32, (tile, 128), 1) < 64, rstd1, rstd2
            )
            m1b_out[...] = m1b
            for j in range(groups):
                hid_out[:, j * features : (j + 1) * features] = hidden[j].astype(BF16)
            m2_out[...] = m2
            m2b_out[...] = m2.astype(BF16)
            y_out[...] = y
    else:
        xh1 = xh1_ref[...].astype(F32)
        xh2 = xh2_ref[...].astype(F32)
        stat = stat_ref[...]
        rstd1, rstd2 = stat[:, 0:1], stat[:, 64:65]
        m1b = m1b_ref[...]
        both = [
            gelu_both(hid_ref[:, j * features : (j + 1) * features].astype(F32))
            for j in range(groups)
        ]
        act = [pair[0].astype(BF16) for pair in both]
    if last:
        yh, rstdy = normed(y)
        layer_out[...] = (m2 + yh * vec(12) + vec(13)).astype(BF16)
        gm = cot_ref[...].astype(F32)
        gs = norm_back(gm, vec(12), yh, rstdy)
        gs_out[...] = gs
        column_sum(dvec_out, 12, gm * yh)
        column_sum(dvec_out, 13, gm)
    elif backward:
        gm = gm_ref[...]
        gs = gs_ref[...]
    if not backward:
        return
    rows = pl.ds(pl.multiple_of(step * tile, tile), tile)
    column_sum(dvec_out, 6, gm * xh2)
    column_sum(dvec_out, 7, gm)
    dz2 = norm_back(gm, vec(6), xh2, rstd2)
    df = (dz2 + gs).astype(BF16)
    column_sum(dvec_out, 5, df)
    df_s[rows] = df
    m1b_s[rows] = m1b
    ctx_s[rows] = ctx
    gm = dz2
    for j in range(groups):
        columns = slice(j * features, (j + 1) * features)
        dhid = (both[j][1] * mm(df, down(j), NT)).astype(BF16)
        column_sum(dvec_out, 8 + j, dhid)
        dhid_s[rows, columns] = dhid
        act_s[rows, columns] = act[j]
        gm = gm + mm(dhid, up(j), NT)
    column_sum(dvec_out, 3, gm * xh1)
    column_sum(dvec_out, 4, gm)
    dz1 = norm_back(gm, vec(3), xh1, rstd1)
    dz1_out[...] = dz1
    da = (dz1 + gs).astype(BF16)
    column_sum(dvec_out, 2, da)
    da_s[rows] = da
    dctx = mm(da, wo(), NT)
    lane = lax.broadcasted_iota(jnp.int32, (tile, 128), 1)
    low_half = lane < HEAD_DIM
    column = lane % HEAD_DIM
    for pair in range(features // 128):
        columns = slice(pair * 128, (pair + 1) * 128)
        dpair = dctx[:, columns]
        product = dpair * ctx[:, columns].astype(F32)
        for head in range(2):
            inside = low_half if head == 0 else ~low_half
            inverse = rinv_ref[:, 2 * pair + head : 2 * pair + head + 1]
            dot = -inverse * jnp.sum(jnp.where(inside, product, 0.0), axis=-1, keepdims=True)
            high = dot.astype(BF16).astype(F32)
            extra = jnp.where(column == 0, high, jnp.where(column == 1, dot - high, 0.0))
            do_out[2 * pair + head] = jnp.where(inside, dpair * inverse, extra).astype(BF16)

    @pl.when(step == pl.num_programs(0) - 1)
    def _():
        shape = (per, BLOCK, features)
        for j in range(groups):
            columns = slice(j * features, (j + 1) * features)
            gdown_s[j * per : (j + 1) * per] = (
                mm(act_s[:, columns], df_s[...], TN).astype(BF16).reshape(shape)
            )
            gup_s[j] = mm(m1b_s[...], dhid_s[:, columns], TN).astype(BF16).reshape(shape)
        go_s[...] = mm(ctx_s[...], da_s[...], TN).astype(BF16).reshape(shape)

        def send_alpha(ref, slot, owner):
            pltpu.make_async_copy(
                gup_s.at[:, owner], ref.at[slot, pl.ds(0, groups)], sem_u
            ).start()
            pltpu.make_async_copy(go_s.at[owner], ref.at[slot, groups], sem_o).start()

        def send_beta(ref, slot, owner):
            pltpu.make_async_copy(
                gdown_s.at[pl.ds(owner * groups, groups)], ref.at[slot], sem_d
            ).start()

        each_slot(order_ref, 0, galpha, send_alpha)
        each_slot(order_ref, 1, gbeta, send_beta)
        wait_all(gup_s, sem_u)
        wait_all(go_s, sem_o)
        wait_all(gdown_s, sem_d)


def ffn_call(forward, backward, last, order, vec, weights, ctx, tiled, rinv):
    tokens, features = ctx.shape
    tile = 256
    groups = 4
    width = groups * features
    per = features // BLOCK
    shapes = []
    if forward and not backward:
        shapes += [
            ((tokens, features), BF16),
            ((tokens, features), BF16),
            ((tokens, 128), F32),
            ((tokens, features), BF16),
            ((tokens, width), BF16),
            ((tokens, features), F32),
            ((tokens, features), BF16),
            ((tokens, features), F32),
        ]
    if last:
        shapes += [((tokens, features), BF16), ((tokens, features), F32)]
    out_specs = [rows_of(tile, shape[1]) for shape, _ in shapes]
    if backward:
        heads = features // HEAD_DIM
        shapes += [((tokens, features), F32), ((heads, tokens, 128), BF16), ((16, features), F32)]
        shapes += [((per // 2, groups + 1, BLOCK, features), BF16)] * 2
        shapes += [((per // 2, groups, BLOCK, features), BF16)] * 2
        out_specs += [
            rows_of(tile, features),
            pl.BlockSpec((heads, tile, 128), lambda step: (0, step, 0)),
            fixed((16, features)),
        ] + [whole(ANY)] * 4
    scratch = [
        VMEM((per, BLOCK, features), BF16),
        VMEM((groups, per, BLOCK, features), BF16),
        VMEM((groups * per, BLOCK, features), BF16),
        pltpu.SemaphoreType.DMA,
        pltpu.SemaphoreType.DMA,
        pltpu.SemaphoreType.DMA,
    ]
    if backward:
        scratch += [
            VMEM((tokens, width), BF16),
            VMEM((tokens, width), BF16),
            VMEM((tokens, features), BF16),
            VMEM((tokens, features), BF16),
            VMEM((tokens, features), BF16),
            VMEM((tokens, features), BF16),
            VMEM((groups, per, BLOCK, features), BF16),
            VMEM((groups * per, BLOCK, features), BF16),
            VMEM((per, BLOCK, features), BF16),
        ]
    operands = [ctx] + list(tiled) + ([rinv] if backward else [])
    return pl.pallas_call(
        functools.partial(ffn_body, forward, backward, last),
        grid=(tokens // tile,),
        out_shape=tuple(jax.ShapeDtypeStruct(shape, dtype) for shape, dtype in shapes),
        in_specs=[whole(pltpu.SMEM), fixed(vec.shape)]
        + [whole(ANY)] * len(weights)
        + [rows_of(tile, operand.shape[1]) for operand in operands],
        out_specs=tuple(out_specs),
        scratch_shapes=scratch,
        compiler_params=pltpu.CompilerParams(vmem_limit_bytes=VMEM_LIMIT),
        cost_estimate=pl.CostEstimate(
            flops=(6 * forward + 12 * backward) * 10**9, bytes_accessed=16 * 10**6, transcendentals=0
        ),
        name="ffn_" + ("f" if forward else "") + ("b" if backward else ""),
    )(order, vec, *weights, *operands)


def attn_backward_body(
    order_ref,
    e_ref,
    do_ref,
    qkv_ref,
    x_ref,
    dz_ref,
    *refs,
):
    alpha, beta = refs[:4], refs[4:8]
    gm_out, dvec_out = refs[8:10]
    galpha, gbeta = refs[10:12], refs[12:14]
    w_ref, dqkv_s, ds_s, g_s, sem, sem_a, sem_b = refs[14:]
    pair = pl.program_id(0)
    tokens, features = x_ref.shape
    lane = lax.broadcasted_iota(jnp.int32, (tokens, 128), 1)
    low_half = lane < HEAD_DIM
    column = lane % HEAD_DIM

    @pl.when(pair == 0)
    def _():
        fetch_attn(order_ref, alpha, beta, w_ref, sem)

    query = qkv_ref[0, 0]
    key_t = qkv_ref[1, 0].T
    value = qkv_ref[2, 0]
    ones = jnp.where(column < 2, 1.0, 0.0).astype(BF16)
    chunk = 256
    dquery, dkey, dvalue = [], [], []
    for head in range(2):
        inside = low_half if head == 0 else ~low_half
        value_aug = jnp.where(inside, value, ones)
        key_head = key_t[head * HEAD_DIM : (head + 1) * HEAD_DIM]
        parts = []
        for start in range(0, tokens, chunk):
            columns = slice(start, start + chunk)
            dchances = mm(value_aug, do_ref[head, columns], NT)
            dscores = (e_ref[head, :, columns].astype(F32) * dchances).astype(BF16)
            ds_s[head, :, columns] = dscores
            parts.append(mm(key_head, dscores, NN))
        dquery.append(jnp.concatenate(parts, axis=1))
        dkey.append(mm(ds_s[head], query, NN))
        dvalue.append(mm(e_ref[head], do_ref[head], NN))
    here = pl.ds(pl.multiple_of(pair * 128, 128), 128)
    dqkv_s[0, :, here] = (jnp.concatenate(dquery, axis=0).T * 0.125).astype(BF16)
    dqkv_s[1, :, here] = jnp.where(low_half, dkey[0], dkey[1]).astype(BF16)
    dqkv_s[2, :, here] = jnp.where(low_half, dvalue[0], dvalue[1]).astype(BF16)

    @pl.when(pair == pl.num_programs(0) - 1)
    def _():
        wait_all(w_ref, sem)
        x = x_ref[...]
        per = features // BLOCK
        for part in range(3):
            g_s[part] = (
                mm(x, dqkv_s[part], TN).astype(BF16).reshape((per, BLOCK, features))
            )

        def send_alpha(ref, slot, owner):
            pltpu.make_async_copy(g_s.at[pl.ds(0, 2), owner], ref.at[slot], sem_a).start()

        def send_beta(ref, slot, owner):
            pltpu.make_async_copy(g_s.at[2, owner], ref.at[slot, 0], sem_b).start()

        each_slot(order_ref, 0, galpha, send_alpha)
        each_slot(order_ref, 1, gbeta, send_beta)
        gm = dz_ref[...]
        for part in range(3):
            gm = gm + mm(dqkv_s[part], w_ref[part].reshape(features, features), NT)
        gm_out[...] = gm
        dvec_out[...] = jnp.zeros_like(dvec_out)
        column_sum(dvec_out, 0, dqkv_s[0])
        column_sum(dvec_out, 1, dqkv_s[2])
        wait_all(g_s.at[pl.ds(0, 2)], sem_a)
        wait_all(g_s.at[2], sem_b)


def attn_backward(order, e, do, qkv, x, dz, weights):
    tokens, features = x.shape
    pairs = features // 128
    per = features // BLOCK
    return pl.pallas_call(
        attn_backward_body,
        grid=(pairs,),
        out_shape=(
            jax.ShapeDtypeStruct((tokens, features), F32),
            jax.ShapeDtypeStruct((8, features), F32),
        )
        + (jax.ShapeDtypeStruct((per // 2, 2, BLOCK, features), BF16),) * 2
        + (jax.ShapeDtypeStruct((per // 2, 1, BLOCK, features), BF16),) * 2,
        in_specs=[
            whole(pltpu.SMEM),
            pl.BlockSpec((2, tokens, tokens), lambda step: (step, 0, 0)),
            pl.BlockSpec((2, tokens, 128), lambda step: (step, 0, 0)),
            pl.BlockSpec((3, 1, tokens, 128), lambda step: (0, step, 0, 0)),
            fixed(x.shape),
            fixed(dz.shape),
        ]
        + [whole(ANY)] * len(weights),
        out_specs=(fixed(dz.shape), fixed((8, features))) + (whole(ANY),) * 4,
        scratch_shapes=[
            VMEM((3, per, BLOCK, features), BF16),
            VMEM((3, tokens, features), BF16),
            VMEM((2, tokens, tokens), BF16),
            VMEM((3, per, BLOCK, features), BF16),
            pltpu.SemaphoreType.DMA,
            pltpu.SemaphoreType.DMA,
            pltpu.SemaphoreType.DMA,
        ],
        compiler_params=pltpu.CompilerParams(vmem_limit_bytes=VMEM_LIMIT),
        cost_estimate=pl.CostEstimate(
            flops=26 * 10**9, bytes_accessed=24 * 10**6, transcendentals=0
        ),
        name="attn_backward",
    )(order, e, do, qkv, x, dz, *weights)


def blocks_of(matrix, features):
    rows, columns = matrix.shape
    shaped = matrix.reshape(rows // BLOCK, BLOCK, columns // features, features)
    return shaped.transpose(0, 2, 1, 3)


def matrix_of(blocks):
    rows, columns, block, features = blocks.shape
    return blocks.transpose(0, 2, 1, 3).reshape(rows * block, columns * features)


CORE, X, Y, Z = 1, 2, 4, 8
Z_MASKS = (0, Z, 2 * Z, 3 * Z)


def slot_masks(first, second):
    return [
        core | high | low | z
        for core in (0, CORE)
        for high in (0, second)
        for low in (0, first)
        for z in Z_MASKS
    ]


def swap(part, mask):
    return lax.ppermute(part, AXES, [(device, device ^ mask) for device in range(32)])


def gather_streams(alpha, beta):
    cut = alpha.shape[0]
    own = jnp.concatenate([alpha, beta])
    pieces = [own] + [swap(own, mask) for mask in Z_MASKS[1:]]
    alpha4 = jnp.stack([piece[:cut] for piece in pieces])
    beta4 = jnp.stack([piece[cut:] for piece in pieces])
    alpha8 = jnp.concatenate([alpha4, swap(alpha4, Y)])
    beta8 = jnp.concatenate([beta4, swap(beta4, X)])
    alpha16 = [alpha8, swap(alpha8, X)]
    beta16 = [beta8, swap(beta8, Y)]
    return (
        alpha16 + [swap(part, CORE) for part in alpha16],
        beta16 + [swap(part, CORE) for part in beta16],
    )


def add(left, right):
    return (left.astype(F32) + right.astype(F32)).astype(BF16)


def scatter_streams(alpha, beta):
    totals = []
    cut = alpha[0].shape[1]
    stages = []
    for (mine, other), first, second in ((alpha, Y, X), (beta, X, Y)):
        stages.append((mine, swap(other, CORE), first, second))
    for mine, got, first, second in stages:
        half = mine.shape[0] // 2
        mine, sent = add(mine[:half], got[:half]), add(mine[half:], got[half:])
        got = swap(sent, second)
        half = half // 2
        mine, sent = add(mine[:half], got[:half]), add(mine[half:], got[half:])
        totals.append(add(mine, swap(sent, first)))
    joined = jnp.concatenate(totals, axis=1)
    total = joined[0].astype(F32)
    for index in range(1, 4):
        total = total + swap(joined[index], Z_MASKS[index]).astype(F32)
    return total[:cut], total[cut:]


def local(
    main_residual,
    side_residual,
    cotangent,
    lengths,
    input_weight,
    output_weight,
    expand_weight,
    reduce_weight,
    vectors,
    final_norm,
):
    tokens, features = main_residual.shape
    layers = input_weight.shape[0]
    assert lengths.shape[0] == 1 and layers == 2
    per = features // BLOCK
    groups = expand_weight.shape[2] // features
    fast = lax.axis_size(AXES) == 32 and per == 32

    if fast:
        me = lax.axis_index(AXES)
        order = jnp.stack(
            [
                me ^ jnp.array(slot_masks(Y, X), jnp.int32),
                me ^ jnp.array(slot_masks(X, Y), jnp.int32),
            ]
        )
        width = vectors.shape[1]
        spread = final_norm.shape[0]
        row = jnp.concatenate([vectors[0], vectors[1], final_norm])
        row = jnp.pad(row[None], ((0, BLOCK - 1), (0, features - row.shape[0])))
        attn_w, ffn_w = [], []
        for layer in range(layers):
            qkv = blocks_of(input_weight[layer], features)[0]
            beta = qkv[2:]
            if layer == 0:
                beta = jnp.concatenate([beta, row[None]])
            attn_w.append(gather_streams(qkv[:2], beta))
            ffn_w.append(
                gather_streams(
                    jnp.concatenate(
                        [blocks_of(expand_weight[layer], features)[0], output_weight[layer][None]]
                    ),
                    reduce_weight[layer].reshape(groups, BLOCK, features),
                )
            )
        rows = jnp.concatenate([part[:, 1, 0] for part in attn_w[0][1]])
        rows = jnp.zeros_like(rows).at[order[1]].set(rows, unique_indices=True)
        all_vectors = jnp.stack(
            [rows[:, layer * width : (layer + 1) * width].reshape(-1) for layer in range(layers)]
        ).astype(F32)
        final_full = rows[:, layers * width : layers * width + spread].reshape(-1).astype(F32)
    else:
        gather = lambda part, axis: lax.all_gather(part, AXES, axis=axis, tiled=True)
        order = jnp.tile(jnp.arange(per, dtype=jnp.int32)[None], (2, 1))
        quarters = lambda blocks: [blocks[index * 8 : index * 8 + 8] for index in range(4)]
        all_vectors = gather(vectors, 1).astype(F32)
        final_full = gather(final_norm, 0).astype(F32)
        attn_w, ffn_w = [], []
        for layer in range(layers):
            qkv = blocks_of(gather(input_weight[layer], 0), features)
            attn_w.append((quarters(qkv[:, :2]), quarters(qkv[:, 2:])))
            up = blocks_of(gather(expand_weight[layer], 0), features)
            out = blocks_of(gather(output_weight[layer], 0), features)
            down = gather(reduce_weight[layer], 0).reshape(per, -1, BLOCK, features)
            ffn_w.append((quarters(jnp.concatenate([up, out], axis=1)), quarters(down)))
    attn_w = [alpha + beta for alpha, beta in attn_w]
    ffn_w = [alpha + beta for alpha, beta in ffn_w]
    vec = jnp.concatenate(
        [
            all_vectors.reshape(layers, 12, features),
            jnp.broadcast_to(final_full.reshape(1, 2, features), (layers, 2, features)),
            jnp.zeros((layers, 2, features), F32),
        ],
        axis=1,
    )

    e0, qkv0, ctx0, rinv0 = attn_forward(order, lengths, main_residual, vec[0], attn_w[0])
    xh1, xh2, stat, m1b, hid, m2, m2b, y = ffn_call(
        True, False, False, order, vec[0], ffn_w[0], ctx0, (main_residual, side_residual), None
    )
    e1, qkv1, ctx1, rinv1 = attn_forward(order, lengths, m2b, vec[1], attn_w[1])
    layer_out, grad_side, dz, do, dvec1, *gf1 = ffn_call(
        True, True, True, order, vec[1], ffn_w[1], ctx1, (m2, y, cotangent), rinv1
    )
    gm, dvec1a, *gi1 = attn_backward(order, e1, do, qkv1, m2b, dz, attn_w[1])
    dz, do, dvec0, *gf0 = ffn_call(
        False, True, False, order, vec[0], ffn_w[0], ctx0,
        (xh1, xh2, stat, m1b, hid, gm, grad_side), rinv0,
    )
    grad_main, dvec0a, *gi0 = attn_backward(order, e0, do, qkv0, main_residual, dz, attn_w[0])

    dvec = jnp.stack(
        [
            jnp.concatenate([dvec0a[0:2], dvec0[2:12]]).reshape(-1),
            jnp.concatenate([dvec1a[0:2], dvec1[2:12]]).reshape(-1),
        ]
    )
    dfinal = dvec1[12:14].reshape(-1)
    if fast:
        up1, down1 = scatter_streams(gf1[:2], gf1[2:])
        in1 = scatter_streams(gi1[:2], gi1[2:])
        up0, down0 = scatter_streams(gf0[:2], gf0[2:])
        rows = jnp.concatenate(
            [
                dvec.reshape(layers, per, width).transpose(1, 0, 2).reshape(per, -1),
                dfinal.reshape(per, spread),
            ],
            axis=1,
        )[order[1]].astype(BF16)
        rows = jnp.pad(
            rows[:, None, None],
            ((0, 0), (0, 0), (0, BLOCK - 1), (0, features - rows.shape[1])),
        )
        half = per // 2
        alpha0, beta0 = scatter_streams(
            gi0[:2],
            [
                jnp.concatenate([gi0[2], rows[:half]], axis=1),
                jnp.concatenate([gi0[3], rows[half:]], axis=1),
            ],
        )
        grad_vec = beta0[1, 0, : layers * width].reshape(layers, width)
        grad_final = beta0[1, 0, layers * width : layers * width + spread]
        side = lambda blocks: blocks.transpose(1, 0, 2).reshape(BLOCK, -1)
        grad_in = jnp.stack(
            [side(jnp.concatenate([alpha0, beta0[:1]])), side(jnp.concatenate(in1))]
        )
        grad_out = jnp.stack([up0[groups], up1[groups]])
        grad_up = jnp.stack([side(up0[:groups]), side(up1[:groups])])
        grad_down = jnp.stack([down0.reshape(-1, features), down1.reshape(-1, features)])
    else:
        scatter = lambda part, axis: lax.psum_scatter(
            part, AXES, scatter_dimension=axis, tiled=True
        ).astype(F32)
        both = lambda make: jnp.stack([make(*gi0, *gf0), make(*gi1, *gf1)])
        join = lambda left, right: jnp.concatenate([left, right])
        grad_in = scatter(
            both(
                lambda a0, a1, b0, b1, *_: matrix_of(
                    jnp.concatenate([join(a0, a1), join(b0, b1)], axis=1)
                )
            ),
            1,
        )
        grad_out = scatter(
            both(lambda *g: matrix_of(join(g[4], g[5])[:, groups:])), 1
        )
        grad_up = scatter(both(lambda *g: matrix_of(join(g[4], g[5])[:, :groups])), 1)
        grad_down = scatter(both(lambda *g: join(g[6], g[7]).reshape(-1, features)), 1)
        grad_vec = scatter(dvec, 1)
        grad_final = scatter(dfinal, 0)
    return (
        layer_out,
        grad_main,
        grad_side,
        grad_in,
        grad_out,
        grad_up,
        grad_down,
        grad_vec,
        grad_final,
    )


def solution(mesh):
    rows = P(AXES, None)
    middle = P(None, AXES, None)
    return jax.shard_map(
        local,
        mesh=mesh,
        in_specs=(rows, rows, rows, rows, middle, middle, middle, middle, P(None, AXES), P(AXES)),
        out_specs=(rows, rows, rows, middle, middle, middle, middle, P(None, AXES), P(AXES)),
        check_vma=False,
    )
```

```python
import functools

import jax
import jax.numpy as jnp
from jax import lax
from jax.experimental import pallas as pl
from jax.experimental.pallas import tpu as pltpu
from jax.sharding import PartitionSpec as P

HEAD_DIM = 64
AXES = ("wide", "narrow")
F32 = jnp.float32
BF16 = jnp.bfloat16
NN = (((1,), (0,)), ((), ()))
NT = (((1,), (1,)), ((), ()))
TN = (((0,), (0,)), ((), ()))
MASKED = -1000000000.0
VMEM_LIMIT = 60 * 2**20
SMALL_VMEM = 24 * 2**20
BLOCK = 16
CHUNK = 512
TILE = 256
VMEM = pltpu.VMEM
ANY = pl.ANY


def mm(left, right, dims):
    return lax.dot_general(left, right, dims, preferred_element_type=F32)


def whole(memory=VMEM):
    return pl.BlockSpec(memory_space=memory)


def fixed(shape):
    zeros = (0,) * len(shape)
    return pl.BlockSpec(shape, lambda step: zeros)


def rows_of(tile, width):
    return pl.BlockSpec((tile, width), lambda step: (step, 0))


def each_slot(order_ref, refs, act):
    for index, ref in enumerate(refs):
        count = ref.shape[0]

        def one(slot, carry, ref=ref, base=index * count):
            act(ref, slot, order_ref[base + slot])
            return carry

        lax.fori_loop(0, count, one, 0)


def wait_all(ref, sem):
    pltpu.make_async_copy(ref, ref, sem).wait()


def fetch_attn(order_ref, weights, at, w_ref, sem, columns):
    def fetch(ref, slot, owner):
        pltpu.make_async_copy(
            ref.at[slot, pl.ds(at, 3), :, columns], w_ref.at[:, owner], sem
        ).start()

    each_slot(order_ref, weights, fetch)


def attn_forward_body(first, places, *refs):
    refs = list(refs)
    take = lambda: refs.pop(0)
    bounds_ref = take()
    if places is not None:
        order_ref, x_ref, vec_ref = take(), take(), take()
        weights = [take() for _ in range(8)]
        e_ref, ctx_ref, rinv_ref, qkv_ref, aux_ref, rows_ref, w_ref, sem = refs
        at = pl.program_id(0) + first
    else:
        qkv_ref, e_ref, ctx_ref, rinv_ref, aux_ref, rows_ref = refs
        at = 0
    step = pl.program_id(0)
    tokens = ctx_ref.shape[0]
    lane = lax.broadcasted_iota(jnp.int32, (tokens, 128), 1)
    low_half = lane < HEAD_DIM

    @pl.when(step == 0)
    def _():
        if places is not None:
            features = x_ref.shape[1]
            fetch_attn(order_ref, weights, places, w_ref, sem, pl.ds(0, features))
        token = lax.broadcasted_iota(jnp.int32, (tokens, 128), 0)
        column = lane % HEAD_DIM
        single = bounds_ref[0, 1] == 0
        quarter = tokens // 4
        segment = jnp.where(single, 0, token // quarter)
        inside = jnp.where(single, token, token % quarter)
        own = column == segment
        bound = jnp.where(
            segment == 0,
            bounds_ref[0, 0],
            jnp.where(
                segment == 1,
                bounds_ref[0, 1],
                jnp.where(segment == 2, bounds_ref[0, 2], bounds_ref[0, 3]),
            ),
        )
        alive = own & (inside < bound)
        aux_ref[0] = jnp.where(own, 1.0, 0.0).astype(BF16)
        aux_ref[1] = jnp.where(alive | (column >= 4), 0.0, MASKED).astype(BF16)
        rows_ref[...] = jnp.zeros_like(rows_ref)
        if places is not None:
            wait_all(w_ref, sem)
            x = x_ref[...]
            for part in range(3):
                packed = mm(x, w_ref[part].reshape(features, features), NN)
                if part == 0:
                    packed = (packed + vec_ref[0:1]).astype(BF16) * BF16(0.125)
                elif part == 2:
                    packed = (packed + vec_ref[1:2]).astype(BF16)
                else:
                    packed = packed.astype(BF16)
                for index in range(features // 128):
                    qkv_ref[part, index] = packed[:, index * 128 : (index + 1) * 128]

    query = qkv_ref[0, at]
    key = qkv_ref[1, at]
    value_t = qkv_ref[2, at].T
    ones = jnp.ones((16, tokens), BF16)
    chunk = CHUNK

    def heads(shifted):
        outs, sums = [], []
        for head in range(2):
            inside_head = low_half if head == 0 else ~low_half
            query_aug = jnp.where(inside_head, query, aux_ref[0])
            key_aug = jnp.where(inside_head, key, aux_ref[1])
            value_aug = jnp.concatenate(
                [value_t[head * HEAD_DIM : (head + 1) * HEAD_DIM], ones], axis=0
            )
            parts = []
            for start in range(0, tokens, chunk):
                scores = mm(key_aug, query_aug[start : start + chunk], NT)
                if shifted:
                    scores = scores - jnp.max(scores, axis=0, keepdims=True)
                exponent = jnp.exp(scores).astype(BF16)
                e_ref[head, :, start : start + chunk] = exponent
                mixed = mm(value_aug, exponent, NN)
                total = mixed[HEAD_DIM : HEAD_DIM + 1]
                inverse = 1.0 / total
                rows_ref[pl.ds(step * 2 + head, 1), start : start + chunk] = inverse
                parts.append(mixed[:HEAD_DIM] * inverse)
                sums.append(total)
            outs.append(jnp.concatenate(parts, axis=1))
        ctx_ref[...] = jnp.concatenate(outs, axis=0).T.astype(BF16)
        return jnp.concatenate(sums, axis=1)

    sums = heads(False)
    fits = (jnp.max(sums) <= 2.0**40) & (jnp.min(sums) >= 2.0**-40)

    @pl.when(jnp.logical_not(fits))
    def _():
        heads(True)

    @pl.when(step == pl.num_programs(0) - 1)
    def _():
        rinv_ref[...] = rows_ref[...].T


def attn_forward(bounds, first, count, qkv=None, order=None, x=None, vec=None, weights=(), places=None):
    project = places is not None
    if project:
        tokens, features = x.shape
        pairs = features // 128
    else:
        _, pairs, tokens, _ = qkv.shape
    out_shape = [
        jax.ShapeDtypeStruct((2 * count, tokens, tokens), BF16),
        jax.ShapeDtypeStruct((tokens, 128 * count), BF16),
        jax.ShapeDtypeStruct((tokens, 128), F32),
    ]
    out_specs = [
        pl.BlockSpec((2, tokens, tokens), lambda step: (step, 0, 0)),
        pl.BlockSpec((tokens, 128), lambda step: (0, step)),
        fixed((tokens, 128)),
    ]
    scratch = [VMEM((2, tokens, 128), BF16), VMEM((128, tokens), F32)]
    if project:
        operands = (bounds, order, x, vec, *weights)
        in_specs = [whole(pltpu.SMEM), whole(pltpu.SMEM), fixed(x.shape), fixed(vec.shape)]
        in_specs += [whole(ANY)] * len(weights)
        out_shape.append(jax.ShapeDtypeStruct((3, pairs, tokens, 128), BF16))
        out_specs.append(fixed((3, pairs, tokens, 128)))
        scratch += [
            VMEM((3, features // BLOCK, BLOCK, features), BF16),
            pltpu.SemaphoreType.DMA,
        ]
    else:
        operands = (bounds, qkv)
        in_specs = [
            whole(pltpu.SMEM),
            pl.BlockSpec((3, 1, tokens, 128), lambda step: (0, step + first, 0, 0)),
        ]
    return pl.pallas_call(
        functools.partial(attn_forward_body, first, places),
        grid=(count,),
        out_shape=tuple(out_shape),
        in_specs=in_specs,
        out_specs=tuple(out_specs),
        scratch_shapes=scratch,
        compiler_params=pltpu.CompilerParams(vmem_limit_bytes=VMEM_LIMIT),
        cost_estimate=pl.CostEstimate(
            flops=4 * count * 10**9, bytes_accessed=4 * count * 10**6, transcendentals=0
        ),
        name="attn_forward",
    )(*operands)


def normed(z):
    centered = z - jnp.mean(z, axis=-1, keepdims=True)
    variance = jnp.mean(centered * centered, axis=-1, keepdims=True)
    rstd = lax.rsqrt(variance + 1e-05)
    return centered * rstd, rstd


def norm_back(grad, gain, xhat, rstd):
    scaled = grad * gain
    first = jnp.mean(scaled, axis=-1, keepdims=True)
    second = jnp.mean(scaled * xhat, axis=-1, keepdims=True)
    return rstd * (scaled - first - xhat * second)


GELU_A = 0.7978845608028654
GELU_B = 0.044715


def gelu_tanh(hidden):
    square = hidden * hidden
    return jnp.tanh(hidden * (GELU_A + (GELU_A * GELU_B) * square)), square


def gelu(hidden):
    tanh, _ = gelu_tanh(hidden)
    half = 0.5 * hidden
    return half + half * tanh


def gelu_both(hidden):
    tanh, square = gelu_tanh(hidden)
    half = 0.5 * hidden
    cdf = 0.5 + 0.5 * tanh
    slope = GELU_A + (3.0 * GELU_A * GELU_B) * square
    return hidden * cdf, cdf + half * (1.0 - tanh * tanh) * slope


def column_sum(ref, row, values):
    ref[row : row + 1] += jnp.sum(values.astype(F32), axis=0, keepdims=True)


def ffn_body(forward, backward, last, pieces, places, *refs):
    refs = list(refs)
    take = lambda: refs.pop(0)
    up_at, out_at, down_at = places
    order_ref, vec_ref = take(), take()
    weights = [take() for _ in range(8)]
    ctx_refs = [take() for _ in range(pieces)]
    if forward:
        x_ref, y_ref = take(), take()
    else:
        xh1_ref, xh2_ref, stat_ref, m1b_ref, hid_ref, gm_ref, gs_ref = [take() for _ in range(7)]
    if last:
        cot_ref = take()
    if backward:
        rinv_refs = [take() for _ in range(pieces)]
    if forward and not backward:
        xh1_out, xh2_out, stat_out, m1b_out, hid_out, m2_out, m2b_out, y_out = [
            take() for _ in range(8)
        ]
    if last:
        layer_out, gs_out = take(), take()
    if backward:
        dz1_out, do_out, dvec_out = [take() for _ in range(3)]
        grads = [take() for _ in range(2)]
    wo_ref, up_ref, down_ref, sem_o, sem_u, sem_d = [take() for _ in range(6)]
    if backward:
        act_s, dhid_s, m1b_s, df_s, da_s, ctx_s, gup_s, gdown_s, go_s = [
            take() for _ in range(9)
        ]
    assert not refs
    step = pl.program_id(0)
    tile = ctx_refs[0].shape[0]
    features = vec_ref.shape[1]
    groups = up_ref.shape[0]
    wo = lambda: wo_ref[...].reshape(features, features)
    up = lambda j: up_ref[j].reshape(features, features)
    per = features // BLOCK
    down = lambda j: down_ref[j * per : (j + 1) * per].reshape(features, features)

    @pl.when(step == 0)
    def _():
        def fetch_out(ref, slot, owner):
            pltpu.make_async_copy(ref.at[slot, out_at], wo_ref.at[owner], sem_o).start()

        def fetch_up(ref, slot, owner):
            pltpu.make_async_copy(
                ref.at[slot, pl.ds(up_at, groups)], up_ref.at[:, owner], sem_u
            ).start()

        def fetch_down(ref, slot, owner):
            pltpu.make_async_copy(
                ref.at[slot, pl.ds(down_at, groups)],
                down_ref.at[pl.ds(owner * groups, groups)],
                sem_d,
            ).start()

        for fetch in (fetch_out, fetch_up, fetch_down):
            each_slot(order_ref, weights, fetch)
        if backward:
            dvec_out[...] = jnp.zeros_like(dvec_out)
        wait_all(wo_ref, sem_o)
        wait_all(up_ref, sem_u)
        wait_all(down_ref, sem_d)

    vec = lambda row: vec_ref[row : row + 1]
    ctx = jnp.concatenate([ref[...] for ref in ctx_refs], axis=1)
    if forward:
        branch = mm(ctx, wo(), NN) + vec(2)
        xh1, rstd1 = normed(x_ref[...].astype(F32) + branch)
        m1 = xh1 * vec(3) + vec(4)
        y = y_ref[...].astype(F32) + branch
        m1b = m1.astype(BF16)
        hidden = [mm(m1b, up(j), NN) + vec(8 + j) for j in range(groups)]
        if backward:
            both = [gelu_both(h) for h in hidden]
            act = [pair[0].astype(BF16) for pair in both]
        else:
            act = [gelu(h).astype(BF16) for h in hidden]
        branch = vec(5)
        for j in range(groups):
            branch = branch + mm(act[j], down(j), NN)
        xh2, rstd2 = normed(m1 + branch)
        m2 = xh2 * vec(6) + vec(7)
        y = y + branch
        if not backward:
            xh1_out[...] = xh1.astype(BF16)
            xh2_out[...] = xh2.astype(BF16)
            stat_out[...] = jnp.where(
                lax.broadcasted_iota(jnp.int32, (tile, 128), 1) < 64, rstd1, rstd2
            )
            m1b_out[...] = m1b
            for j in range(groups):
                hid_out[:, j * features : (j + 1) * features] = hidden[j].astype(BF16)
            m2_out[...] = m2
            m2b_out[...] = m2.astype(BF16)
            y_out[...] = y
    else:
        xh1 = xh1_ref[...].astype(F32)
        xh2 = xh2_ref[...].astype(F32)
        stat = stat_ref[...]
        rstd1, rstd2 = stat[:, 0:1], stat[:, 64:65]
        m1b = m1b_ref[...]
        both = [
            gelu_both(hid_ref[:, j * features : (j + 1) * features].astype(F32))
            for j in range(groups)
        ]
        act = [pair[0].astype(BF16) for pair in both]
    if last:
        yh, rstdy = normed(y)
        layer_out[...] = (m2 + yh * vec(12) + vec(13)).astype(BF16)
        gm = cot_ref[...].astype(F32)
        gs = norm_back(gm, vec(12), yh, rstdy)
        gs_out[...] = gs
        column_sum(dvec_out, 12, gm * yh)
        column_sum(dvec_out, 13, gm)
    elif backward:
        gm = gm_ref[...]
        gs = gs_ref[...]
    if not backward:
        return
    rows = pl.ds(pl.multiple_of(step * tile, tile), tile)
    column_sum(dvec_out, 6, gm * xh2)
    column_sum(dvec_out, 7, gm)
    dz2 = norm_back(gm, vec(6), xh2, rstd2)
    df = (dz2 + gs).astype(BF16)
    column_sum(dvec_out, 5, df)
    df_s[rows] = df
    m1b_s[rows] = m1b
    ctx_s[rows] = ctx
    gm = dz2
    for j in range(groups):
        columns = slice(j * features, (j + 1) * features)
        dhid = (both[j][1] * mm(df, down(j), NT)).astype(BF16)
        column_sum(dvec_out, 8 + j, dhid)
        dhid_s[rows, columns] = dhid
        act_s[rows, columns] = act[j]
        gm = gm + mm(dhid, up(j), NT)
    column_sum(dvec_out, 3, gm * xh1)
    column_sum(dvec_out, 4, gm)
    dz1 = norm_back(gm, vec(3), xh1, rstd1)
    dz1_out[...] = dz1
    da = (dz1 + gs).astype(BF16)
    column_sum(dvec_out, 2, da)
    da_s[rows] = da
    dctx = mm(da, wo(), NT)
    lane = lax.broadcasted_iota(jnp.int32, (tile, 128), 1)
    low_half = lane < HEAD_DIM
    column = lane % HEAD_DIM
    for pair in range(features // 128):
        columns = slice(pair * 128, (pair + 1) * 128)
        dpair = dctx[:, columns]
        product = dpair * ctx[:, columns].astype(F32)
        for head in range(2):
            inside = low_half if head == 0 else ~low_half
            piece, column_at = divmod((2 * pair + head) * pieces, features // HEAD_DIM)
            column_at = column_at // pieces
            inverse = rinv_refs[piece][:, column_at : column_at + 1]
            dot = -inverse * jnp.sum(jnp.where(inside, product, 0.0), axis=-1, keepdims=True)
            high = dot.astype(BF16).astype(F32)
            extra = jnp.where(column == 0, high, jnp.where(column == 1, dot - high, 0.0))
            do_out[2 * pair + head] = jnp.where(inside, dpair * inverse, extra).astype(BF16)

    @pl.when(step == pl.num_programs(0) - 1)
    def _():
        shape = (per, BLOCK, features)
        for j in range(groups):
            columns = slice(j * features, (j + 1) * features)
            gdown_s[j * per : (j + 1) * per] = (
                mm(act_s[:, columns], df_s[...], TN).astype(BF16).reshape(shape)
            )
            gup_s[j] = mm(m1b_s[...], dhid_s[:, columns], TN).astype(BF16).reshape(shape)
        go_s[...] = mm(ctx_s[...], da_s[...], TN).astype(BF16).reshape(shape)

        def send(ref, slot, owner):
            pltpu.make_async_copy(
                gup_s.at[:, owner], ref.at[slot, pl.ds(0, groups)], sem_u
            ).start()
            pltpu.make_async_copy(go_s.at[owner], ref.at[slot, groups], sem_o).start()
            pltpu.make_async_copy(
                gdown_s.at[pl.ds(owner * groups, groups)],
                ref.at[slot, pl.ds(groups + 1, groups)],
                sem_d,
            ).start()

        each_slot(order_ref, grads, send)
        wait_all(gup_s, sem_u)
        wait_all(go_s, sem_o)
        wait_all(gdown_s, sem_d)


def ffn_call(forward, backward, last, order, vec, weights, places, ctx, tiled, rinv=()):
    tokens, features = tiled[0].shape
    tile = TILE
    groups = 4
    width = groups * features
    per = features // BLOCK
    shapes = []
    if forward and not backward:
        shapes += [
            ((tokens, features), BF16),
            ((tokens, features), BF16),
            ((tokens, 128), F32),
            ((tokens, features), BF16),
            ((tokens, width), BF16),
            ((tokens, features), F32),
            ((tokens, features), BF16),
            ((tokens, features), F32),
        ]
    if last:
        shapes += [((tokens, features), BF16), ((tokens, features), F32)]
    out_specs = [rows_of(tile, shape[1]) for shape, _ in shapes]
    if backward:
        heads = features // HEAD_DIM
        shapes += [((tokens, features), F32), ((heads, tokens, 128), BF16), ((16, features), F32)]
        shapes += [((per // 2, 2 * groups + 1, BLOCK, features), BF16)] * 2
        out_specs += [
            rows_of(tile, features),
            pl.BlockSpec((heads, tile, 128), lambda step: (0, step, 0)),
            fixed((16, features)),
        ] + [whole(ANY)] * 2
    scratch = [
        VMEM((per, BLOCK, features), BF16),
        VMEM((groups, per, BLOCK, features), BF16),
        VMEM((groups * per, BLOCK, features), BF16),
        pltpu.SemaphoreType.DMA,
        pltpu.SemaphoreType.DMA,
        pltpu.SemaphoreType.DMA,
    ]
    if backward:
        scratch += [
            VMEM((tokens, width), BF16),
            VMEM((tokens, width), BF16),
            VMEM((tokens, features), BF16),
            VMEM((tokens, features), BF16),
            VMEM((tokens, features), BF16),
            VMEM((tokens, features), BF16),
            VMEM((groups, per, BLOCK, features), BF16),
            VMEM((groups * per, BLOCK, features), BF16),
            VMEM((per, BLOCK, features), BF16),
        ]
    operands = list(ctx) + list(tiled) + list(rinv)
    return pl.pallas_call(
        functools.partial(ffn_body, forward, backward, last, len(ctx), places),
        grid=(tokens // tile,),
        out_shape=tuple(jax.ShapeDtypeStruct(shape, dtype) for shape, dtype in shapes),
        in_specs=[whole(pltpu.SMEM), fixed(vec.shape)]
        + [whole(ANY)] * len(weights)
        + [rows_of(tile, operand.shape[1]) for operand in operands],
        out_specs=tuple(out_specs),
        scratch_shapes=scratch,
        compiler_params=pltpu.CompilerParams(vmem_limit_bytes=VMEM_LIMIT),
        cost_estimate=pl.CostEstimate(
            flops=(6 * forward + 12 * backward) * 10**9, bytes_accessed=16 * 10**6, transcendentals=0
        ),
        name="ffn_" + ("f" if forward else "") + ("b" if backward else ""),
    )(order, vec, *weights, *operands)


def attn_backward_body(
    first,
    count,
    places,
    order_ref,
    e_ref,
    do_ref,
    qkv_ref,
    x_ref,
    gm_ref,
    *refs,
):
    weights = refs[:8]
    gm_out, dvec_out = refs[8:10]
    grads = refs[10:12]
    w_ref, dqkv_s, ds_s, g_s, sem, sem_g = refs[12:]
    step = pl.program_id(0)
    tokens, features = x_ref.shape
    lane = lax.broadcasted_iota(jnp.int32, (tokens, 128), 1)
    low_half = lane < HEAD_DIM
    column = lane % HEAD_DIM
    width = 128 * count

    @pl.when(step == 0)
    def _():
        fetch_attn(order_ref, weights, places, w_ref, sem, pl.ds(first * 128, width))

    query = qkv_ref[0, 0]
    key_t = qkv_ref[1, 0].T
    value = qkv_ref[2, 0]
    ones = jnp.where(column < 2, 1.0, 0.0).astype(BF16)
    chunk = CHUNK
    dquery, dkey, dvalue = [], [], []
    for head in range(2):
        inside = low_half if head == 0 else ~low_half
        value_aug = jnp.where(inside, value, ones)
        key_head = key_t[head * HEAD_DIM : (head + 1) * HEAD_DIM]
        parts = []
        for start in range(0, tokens, chunk):
            columns = slice(start, start + chunk)
            dchances = mm(value_aug, do_ref[head, columns], NT)
            dscores = (e_ref[head, :, columns].astype(F32) * dchances).astype(BF16)
            ds_s[head, :, columns] = dscores
            parts.append(mm(key_head, dscores, NN))
        dquery.append(jnp.concatenate(parts, axis=1))
        dkey.append(mm(ds_s[head], query, NN))
        dvalue.append(mm(e_ref[head], do_ref[head], NN))
    here = pl.ds(pl.multiple_of(step * 128, 128), 128)
    dqkv_s[0, :, here] = (jnp.concatenate(dquery, axis=0).T * 0.125).astype(BF16)
    dqkv_s[1, :, here] = jnp.where(low_half, dkey[0], dkey[1]).astype(BF16)
    dqkv_s[2, :, here] = jnp.where(low_half, dvalue[0], dvalue[1]).astype(BF16)

    @pl.when(step == count - 1)
    def _():
        wait_all(w_ref, sem)
        x = x_ref[...]
        per = features // BLOCK
        for part in range(3):
            g_s[part] = mm(x, dqkv_s[part], TN).astype(BF16).reshape((per, BLOCK, width))

        def send(ref, slot, owner):
            pltpu.make_async_copy(g_s.at[:, owner], ref.at[slot], sem_g).start()

        each_slot(order_ref, grads, send)
        gm = gm_ref[...]
        for part in range(3):
            gm = gm + mm(dqkv_s[part], w_ref[part].reshape(features, width), NT)
        gm_out[...] = gm
        dvec_out[...] = jnp.zeros_like(dvec_out)
        column_sum(dvec_out, 0, dqkv_s[0])
        column_sum(dvec_out, 1, dqkv_s[2])
        wait_all(g_s, sem_g)


def attn_backward(order, first, count, e, e_first, do, qkv, x, gm, weights, places):
    tokens, features = x.shape
    per = features // BLOCK
    width = 128 * count
    half = lambda blocks: jax.ShapeDtypeStruct((per // 2, blocks, BLOCK, width), BF16)
    return pl.pallas_call(
        functools.partial(attn_backward_body, first, count, places),
        grid=(count,),
        out_shape=(
            jax.ShapeDtypeStruct((tokens, features), F32),
            jax.ShapeDtypeStruct((8, width), F32),
            half(3),
            half(3),
        ),
        in_specs=[
            whole(pltpu.SMEM),
            pl.BlockSpec((2, tokens, tokens), lambda step: (step + e_first, 0, 0)),
            pl.BlockSpec((2, tokens, 128), lambda step: (step + first, 0, 0)),
            pl.BlockSpec((3, 1, tokens, 128), lambda step: (0, step + first, 0, 0)),
            fixed(x.shape),
            fixed(gm.shape),
        ]
        + [whole(ANY)] * len(weights),
        out_specs=(fixed(gm.shape), fixed((8, width))) + (whole(ANY),) * 2,
        scratch_shapes=[
            VMEM((3, per, BLOCK, width), BF16),
            VMEM((3, tokens, width), BF16),
            VMEM((2, tokens, tokens), BF16),
            VMEM((3, per, BLOCK, width), BF16),
            pltpu.SemaphoreType.DMA,
            pltpu.SemaphoreType.DMA,
        ],
        compiler_params=pltpu.CompilerParams(vmem_limit_bytes=VMEM_LIMIT),
        cost_estimate=pl.CostEstimate(
            flops=6 * count * 10**9, bytes_accessed=6 * count * 10**6, transcendentals=0
        ),
        name="attn_backward",
    )(order, e, do, qkv, x, gm, *weights)


def blocks_of(matrix, features):
    rows, columns = matrix.shape
    shaped = matrix.reshape(rows // BLOCK, BLOCK, columns // features, features)
    return shaped.transpose(0, 2, 1, 3)


def matrix_of(blocks):
    rows, columns, block, features = blocks.shape
    return blocks.transpose(0, 2, 1, 3).reshape(rows * block, columns * features)


CORE, X, Y, Z = 1, 2, 4, 8
Z_MASKS = (0, Z, 2 * Z, 3 * Z)
PLANE_MASKS = (0, X, Y, X | Y)
SLOT_MASKS = [
    core | plane | z for core in (0, CORE) for plane in PLANE_MASKS for z in Z_MASKS
]


def swap(part, mask):
    return lax.ppermute(part, AXES, [(device, device ^ mask) for device in range(32)])


def after(value, *earlier):
    return lax.optimization_barrier((value, earlier))[0]


def gather_z(*blocks):
    own = jnp.concatenate(blocks)
    return [own] + [swap(own, mask) for mask in Z_MASKS[1:]]


def small_call(body, outs, name, *operands, far=False):
    return pl.pallas_call(
        body,
        out_shape=tuple(jax.ShapeDtypeStruct(shape, BF16) for shape in outs),
        in_specs=[whole()] * len(operands),
        out_specs=tuple(whole() for _ in outs),
        compiler_params=pltpu.CompilerParams(
            vmem_limit_bytes=VMEM_LIMIT if far else SMALL_VMEM
        ),
        name=name,
    )(*operands)


def pack_z(pieces):
    def body(*refs):
        for index in range(4):
            refs[4][index] = refs[index][...]

    return small_call(body, [(4, *pieces[0].shape)], "pack_z", *pieces)[0]


def gather_plane(four):
    return [swap(four, mask) for mask in PLANE_MASKS[1:]]


def gather_core(parts):
    return [swap(part, CORE) for part in parts]


def sum_core(mine, other):
    return mine, swap(other, CORE)


def sum_plane(pairs, far=True):
    cuts = [mine.shape[1] for mine, _ in pairs]
    rest = pairs[0][0].shape[2:]
    operands = [part.reshape(4, 4, *part.shape[1:]) for pair in pairs for part in pair]

    def body(*refs):
        ins, outs = refs[: len(operands)], refs[len(operands) :]
        start = 0
        for index, size in enumerate(cuts):
            left, right = ins[2 * index : 2 * index + 2]
            for plane, out in enumerate(outs):
                out[0, start : start + size] = (
                    left[plane, 0].astype(F32) + right[plane, 0].astype(F32)
                ).astype(BF16)
            start += size

    return pl.pallas_call(
        body,
        grid=(4,),
        out_shape=(jax.ShapeDtypeStruct((4, sum(cuts), *rest), BF16),) * 4,
        in_specs=[
            pl.BlockSpec((4, 1, *part.shape[2:]), lambda step: (0, step, 0, 0, 0))
            for part in operands
        ],
        out_specs=(pl.BlockSpec((1, sum(cuts), *rest), lambda step: (step, 0, 0, 0)),) * 4,
        compiler_params=pltpu.CompilerParams(
            vmem_limit_bytes=VMEM_LIMIT if far else SMALL_VMEM
        ),
        name="sum_plane",
    )(*operands)


def send_plane(parts):
    return [parts[0]] + [swap(part, mask) for part, mask in zip(parts[1:], PLANE_MASKS[1:])]


def sum_z(parts, far=True):
    def body(*refs):
        for slot in range(4):
            total = refs[0][slot].astype(F32)
            for ref in refs[1:4]:
                total = total + ref[slot].astype(F32)
            refs[4 + slot][...] = total.astype(BF16)

    return small_call(body, [parts[0].shape[1:]] * 4, "sum_z", *parts, far=far)


def send_z(pieces):
    return [pieces[0]] + [swap(piece, mask) for piece, mask in zip(pieces[1:], Z_MASKS[1:])]


def finish(offsets, ffn1, mixed, attn0, width, spread):
    _, block, features = ffn1[0].shape
    groups = (ffn1[0].shape[0] - 1) // 2

    def body(offsets_ref, *refs):
        parts = [refs[:4], refs[4:8], refs[8:12]]
        in_out, out_out, up_out, down_out, vec_out, last_out = refs[12:]

        def total(part, index):
            value = parts[part][0][index].astype(F32)
            for ref in parts[part][1:]:
                value = value + ref[index].astype(F32)
            return value

        for layer, part in ((1, 0), (0, 1)):
            for j in range(groups):
                up_out[layer, :, features * j : features * (j + 1)] = total(part, j)
                down_out[layer, block * j : block * (j + 1)] = total(part, groups + 1 + j)
            out_out[layer] = total(part, groups)
        for layer, part, start in ((1, 1, 2 * groups + 1), (0, 2, 0)):
            for j in range(3):
                in_out[layer, :, features * j : features * (j + 1)] = total(part, start + j)
        rows = total(2, 3)
        for layer in range(2):
            field = rows[0:8, 256 * layer : 256 * layer + 256]
            turned = pltpu.roll(field, 192, 1)
            chosen = jnp.where(offsets_ref[0] == 0, field, turned)
            vec_out[layer : layer + 1] = chosen[0:1, :width]
        field = rows[0:8, :128]
        chosen = field
        for turn in range(1, 128 // spread):
            turned = pltpu.roll(field, 128 - turn * spread, 1)
            chosen = jnp.where(offsets_ref[1] == turn * spread, turned, chosen)
        last_out[...] = chosen[1:2, :spread]

    shapes = [
        (2, block, 3 * features),
        (2, block, features),
        (2, block, groups * features),
        (2, block * groups, features),
        (2, width),
        (1, spread),
    ]
    return pl.pallas_call(
        body,
        out_shape=tuple(jax.ShapeDtypeStruct(shape, F32) for shape in shapes),
        in_specs=[whole(pltpu.SMEM)] + [whole()] * 12,
        out_specs=tuple(whole() for _ in shapes),
        compiler_params=pltpu.CompilerParams(vmem_limit_bytes=SMALL_VMEM),
        name="finish",
    )(offsets, *ffn1, *mixed, *attn0)


def field_of(device, width):
    start = device * width
    return start // 128 * 128, start % 128


def spread_fields(vectors, final_norm, device):
    layers, width = vectors.shape
    zeros = jnp.zeros((layers, 256), vectors.dtype)
    fields = lax.dynamic_update_slice(zeros, vectors, (0, field_of(device, width)[1]))
    spread = final_norm.shape[0]
    last = lax.dynamic_update_slice(
        jnp.zeros((512,), vectors.dtype), final_norm, (field_of(device, spread)[1],)
    )
    block = jnp.concatenate([fields.reshape(1, 512), last[None]])
    return jnp.pad(block, ((0, BLOCK - 2), (0, 0)))


def unpack_vectors(order, parts, width, spread):
    def body(order_ref, *refs):
        refs, out, flat, last = refs[:8], *refs[8:]
        flat[...] = jnp.zeros_like(flat)
        last[...] = jnp.zeros_like(last)
        out[...] = jnp.zeros_like(out)
        for index, ref in enumerate(refs):
            for slot in range(4):
                owner = order_ref[4 * index + slot]
                rows = ref[slot, 0].astype(F32)
                at = pl.ds(pl.multiple_of(owner * width // 128 * 128, 128), 256)
                for layer in range(2):
                    flat[layer : layer + 1, at] += rows[0:1, 256 * layer : 256 * layer + 256]
                at = pl.ds(pl.multiple_of(owner * spread // 128 * 128, 128), 128)
                last[0:1, at] += rows[1:2, :128]
        for layer in range(2):
            for row in range(12):
                out[layer, row : row + 1] = flat[layer : layer + 1, row * 512 : row * 512 + 512]
            for row in range(2):
                out[layer, 12 + row : 13 + row] = last[0:1, row * 512 : row * 512 + 512]

    features = parts[0].shape[-1]
    at = parts[0].shape[1] - 1
    return pl.pallas_call(
        body,
        grid=(1,),
        out_shape=jax.ShapeDtypeStruct((2, 16, features), F32),
        in_specs=[whole(pltpu.SMEM)]
        + [pl.BlockSpec((4, 1, *part.shape[2:]), lambda step: (0, at, 0, 0)) for part in parts],
        out_specs=fixed((2, 16, features)),
        scratch_shapes=[VMEM((8, 12 * features), F32), VMEM((8, 2 * features), F32)],
        compiler_params=pltpu.CompilerParams(vmem_limit_bytes=SMALL_VMEM),
        name="unpack_vectors",
    )(order, *parts)


def pack_vectors(order, attn_rows, ffn_rows, width, spread):
    features = ffn_rows[0].shape[1]

    def body(order_ref, a0, a1, f0, f1, out0, out1, flat, last):
        for layer, (attn, ffn) in enumerate(((a0, f0), (a1, f1))):
            for row in range(12):
                source = attn if row < 2 else ffn
                flat[layer : layer + 1, row * 512 : row * 512 + 512] = source[row : row + 1]
        for row in range(2):
            last[0:1, row * 512 : row * 512 + 512] = f1[12 + row : 13 + row]
        for half, out in enumerate((out0, out1)):
            out[...] = jnp.zeros_like(out)
            for slot in range(16):
                owner = order_ref[16 * half + slot]
                at = pl.ds(pl.multiple_of(owner * width // 128 * 128, 128), 256)
                fields = [flat[layer : layer + 1, at] for layer in range(2)]
                at = pl.ds(pl.multiple_of(owner * spread // 128 * 128, 128), 128)
                final = jnp.concatenate([last[0:1, at], jnp.zeros((1, 384), F32)], axis=1)
                rows = [jnp.concatenate(fields, axis=1), final, jnp.zeros((BLOCK - 2, 512), F32)]
                out[slot, 0] = jnp.concatenate(rows, axis=0).astype(BF16)

    return pl.pallas_call(
        body,
        out_shape=(jax.ShapeDtypeStruct((16, 1, BLOCK, features), BF16),) * 2,
        in_specs=[whole(pltpu.SMEM)] + [whole()] * 4,
        out_specs=(whole(), whole()),
        scratch_shapes=[VMEM((8, 12 * features), F32), VMEM((8, 2 * features), F32)],
        compiler_params=pltpu.CompilerParams(vmem_limit_bytes=SMALL_VMEM),
        name="pack_vectors",
    )(order, *attn_rows, *ffn_rows)


def total_of(pieces):
    total = pieces[0].astype(F32)
    for piece in pieces[1:]:
        total = total + piece.astype(F32)
    return total


def local(
    main_residual,
    side_residual,
    cotangent,
    lengths,
    input_weight,
    output_weight,
    expand_weight,
    reduce_weight,
    vectors,
    final_norm,
):
    tokens, features = main_residual.shape
    layers = input_weight.shape[0]
    assert lengths.shape[0] == 1 and layers == 2
    per = features // BLOCK
    pairs = features // 128
    half_pairs = pairs // 2
    groups = expand_weight.shape[2] // features
    fast = lax.axis_size(AXES) == 32 and per == 32
    attn_at = (0, 0)
    ffn_at = ((3, 3 + groups, 4 + groups), (0, groups, groups + 1))
    width = vectors.shape[1]
    spread = final_norm.shape[0]

    def vec_rows(all_vectors, final_full):
        return jnp.concatenate(
            [
                all_vectors.reshape(layers, 12, features),
                jnp.broadcast_to(final_full.reshape(1, 2, features), (layers, 2, features)),
                jnp.zeros((layers, 2, features), F32),
            ],
            axis=1,
        )

    if fast:
        me = lax.axis_index(AXES)
        order = me ^ jnp.array(SLOT_MASKS, jnp.int32)
        row = spread_fields(vectors, final_norm, me)
        qkv0, qkv1 = [blocks_of(input_weight[layer], features)[0] for layer in range(2)]
        up0, up1 = [blocks_of(expand_weight[layer], features)[0] for layer in range(2)]
        down0, down1 = [
            reduce_weight[layer].reshape(groups, BLOCK, features) for layer in range(2)
        ]
        z0 = gather_z(qkv0, row[None])
        z1 = gather_z(after(qkv1, z0[1:]), up0, output_weight[0][None], down0)
        z2 = gather_z(after(up1, z1[1:]), output_weight[1][None], down1)
        four = pack_z(z0)
        plane = gather_plane(four)
        attn0 = [four, *plane, *gather_core([four, *plane])]
        vec = unpack_vectors(order, attn0, width, spread)
        four = pack_z(z1)
        plane = gather_plane(four)
        x0 = after(main_residual, four)
    else:
        gather = lambda part, axis: lax.all_gather(part, AXES, axis=axis, tiled=True)
        order = jnp.arange(per, dtype=jnp.int32)
        eighths = lambda *blocks: [
            jnp.concatenate(blocks, axis=1)[index * 4 : index * 4 + 4] for index in range(8)
        ]
        vec = vec_rows(gather(vectors, 1).astype(F32), gather(final_norm, 0).astype(F32))
        parts = []
        for layer in range(layers):
            qkv = blocks_of(gather(input_weight[layer], 0), features)
            up = blocks_of(gather(expand_weight[layer], 0), features)
            out = blocks_of(gather(output_weight[layer], 0), features)
            down = gather(reduce_weight[layer], 0).reshape(per, -1, BLOCK, features)
            parts.append((qkv, up, out, down))
        attn0 = eighths(parts[0][0])
        mixed = eighths(parts[1][0], *parts[0][1:])
        ffn1 = eighths(*parts[1][1:])
        x0 = main_residual

    e0, ctx0, rinv0, qkv0 = attn_forward(
        lengths, 0, pairs, None, order, x0, vec[0], attn0, attn_at[0]
    )
    x0 = main_residual
    if fast:
        plane, z2 = after((plane, z2), e0)
        mixed = [four, *plane, *gather_core([four, *plane])]
        four2 = pack_z(z2)
        plane2 = gather_plane(four2)
        x0 = after(x0, four2)
    xh1, xh2, stat, m1b, hid, m2, m2b, y = ffn_call(
        True, False, False, order, vec[0], mixed, ffn_at[0], (ctx0,), (x0, side_residual)
    )
    e1, ctx1, rinv1, qkv1 = attn_forward(
        lengths, 0, pairs, None, order, m2b, vec[1], mixed, attn_at[1]
    )
    if fast:
        plane2 = after(plane2, e1)
        ffn1 = [four2, *plane2, *gather_core([four2, *plane2])]
    layer_out, grad_side, gm, do, dvec1, *gf1 = ffn_call(
        True, True, True, order, vec[1], ffn1, ffn_at[1], (ctx1,), (m2, y, cotangent), (rinv1,)
    )
    if fast:
        f1 = sum_plane([sum_core(*gf1)])
        gm = after(gm, f1)
        f1 = send_plane(f1)
    gm, dvec1a, *gi1 = attn_backward(
        order, 0, pairs, e1, 0, do, qkv1, m2b, gm, mixed, attn_at[1]
    )
    if fast:
        i1 = sum_core(*gi1)
        f1 = sum_z(after(f1, gm))
        gm = after(gm, f1)
        f1 = send_z(f1)
    gm, do, dvec0, *gf0 = ffn_call(
        False, True, False, order, vec[0], mixed, ffn_at[0], (ctx0,),
        (xh1, xh2, stat, m1b, hid, gm, grad_side), (rinv0,),
    )
    if fast:
        f1, i1 = after((f1, i1), gm)
        f0 = sum_plane([sum_core(*after(gf0, f1)), i1])
        gm = after(gm, f0)
        f0 = send_plane(f0)
    grad_main, dvec0a, *gi0 = attn_backward(
        order, 0, pairs, e0, 0, do, qkv0, main_residual, gm, attn0, attn_at[0]
    )

    if fast:
        rows = pack_vectors(order, (dvec0a, dvec1a), (dvec0, dvec1), width, spread)
        i0 = sum_plane([sum_core(*gi0), sum_core(*rows)], far=False)
        f0 = sum_z(after(f0, grad_main))
        i0 = send_plane(after(i0, f0))
        f0 = send_z(f0)
        i0 = send_z(sum_z(i0, far=False))
        offsets = jnp.stack([field_of(me, width)[1], field_of(me, spread)[1]])
        grad_in, grad_out, grad_up, grad_down, grad_vec, grad_final = finish(
            offsets, f1, f0, i0, width, spread
        )
        grad_final = grad_final[0]
    else:
        scatter = lambda part, axis: lax.psum_scatter(
            part, AXES, scatter_dimension=axis, tiled=True
        ).astype(F32)
        both = lambda make: jnp.stack(
            [make(jnp.concatenate(i), jnp.concatenate(f)) for i, f in ((gi0, gf0), (gi1, gf1))]
        )
        grad_in = scatter(both(lambda i, f: matrix_of(i)), 1)
        grad_up = scatter(both(lambda i, f: matrix_of(f[:, :groups])), 1)
        grad_out = scatter(both(lambda i, f: matrix_of(f[:, groups : groups + 1])), 1)
        grad_down = scatter(both(lambda i, f: f[:, groups + 1 :].reshape(-1, features)), 1)
        dvec = [
            jnp.concatenate([first[0:2], rest[2:12]]).reshape(-1)
            for first, rest in ((dvec0a, dvec0), (dvec1a, dvec1))
        ]
        grad_vec = scatter(jnp.stack(dvec), 1)
        grad_final = scatter(dvec1[12:14].reshape(-1), 0)
    return (
        layer_out,
        grad_main,
        grad_side,
        grad_in,
        grad_out,
        grad_up,
        grad_down,
        grad_vec,
        grad_final,
    )


def solution(mesh):
    rows = P(AXES, None)
    middle = P(None, AXES, None)
    return jax.shard_map(
        local,
        mesh=mesh,
        in_specs=(rows, rows, rows, rows, middle, middle, middle, middle, P(None, AXES), P(AXES)),
        out_specs=(rows, rows, rows, middle, middle, middle, middle, P(None, AXES), P(AXES)),
        check_vma=False,
    )
```

```python
import functools

import jax
import jax.numpy as jnp
from jax import lax
from jax.experimental import pallas as pl
from jax.experimental.pallas import tpu as pltpu
from jax.sharding import PartitionSpec as P

HEAD_DIM = 64
AXES = ("wide", "narrow")
F32 = jnp.float32
BF16 = jnp.bfloat16
NN = (((1,), (0,)), ((), ()))
NT = (((1,), (1,)), ((), ()))
TN = (((0,), (0,)), ((), ()))
MASKED = -1000000000.0
VMEM_LIMIT = 60 * 2**20
SMALL_VMEM = 24 * 2**20


def cost(microseconds):
    return pl.CostEstimate(
        flops=microseconds * 10**9, bytes_accessed=microseconds * 10**6, transcendentals=0
    )


BLOCK = 16
CHUNK = 512
TILE = 256
ROWS = 64
VMEM = pltpu.VMEM
ANY = pl.ANY


def mm(left, right, dims):
    return lax.dot_general(left, right, dims, preferred_element_type=F32)


def whole(memory=VMEM):
    return pl.BlockSpec(memory_space=memory)


def fixed(shape):
    zeros = (0,) * len(shape)
    return pl.BlockSpec(shape, lambda step: zeros)


def rows_of(tile, width):
    return pl.BlockSpec((tile, width), lambda step: (step, 0))


AT_Z, AT_PLANE, AT_CORE, AT_FIELDS = 16, 17, 18, 19


def each_part(place_ref, weights, stream):
    return [
        (weights[index].at[near], place_ref[2 * index + near])
        for index in range(4 * stream, 4 * stream + 4)
        for near in range(2)
    ]


def wait_all(ref, sem):
    pltpu.make_async_copy(ref, ref, sem).wait()


def fetch_attn(order_ref, weights, at, w_ref, sem, columns):
    for ref, low in each_part(order_ref, weights, 0):
        pltpu.make_async_copy(
            ref.at[pl.ds(at, 2), :, :, columns], w_ref.at[pl.ds(0, 2), :, low], sem
        ).start()
    for ref, low in each_part(order_ref, weights, 1):
        pltpu.make_async_copy(ref.at[at, :, :, columns], w_ref.at[2, :, low], sem).start()


def attn_forward_body(first, count, places, *refs):
    refs = list(refs)
    take = lambda: refs.pop(0)
    bounds_ref = take()
    if places is not None:
        order_ref, x_ref, vec_ref = take(), take(), take()
        weights = [take() for _ in range(8)]
        e_ref, ctx_ref, rinv_ref, qkv_ref, aux_ref, rows_ref, w_ref, sem = refs
        at = pl.program_id(0) + first
    else:
        qkv_ref, e_ref, ctx_ref, rinv_ref, aux_ref, rows_ref = refs
        at = 0
    step = pl.program_id(0)
    tokens = ctx_ref.shape[0]
    lane = lax.broadcasted_iota(jnp.int32, (tokens, 128), 1)
    low_half = lane < HEAD_DIM

    @pl.when(step == 0)
    def _():
        if places is not None:
            features = x_ref.shape[1]
            fetch_attn(order_ref, weights, places, w_ref, sem, pl.ds(0, features))
        token = lax.broadcasted_iota(jnp.int32, (tokens, 128), 0)
        column = lane % HEAD_DIM
        single = bounds_ref[0, 1] == 0
        quarter = tokens // 4
        segment = jnp.where(single, 0, token // quarter)
        inside = jnp.where(single, token, token % quarter)
        own = column == segment
        bound = jnp.where(
            segment == 0,
            bounds_ref[0, 0],
            jnp.where(
                segment == 1,
                bounds_ref[0, 1],
                jnp.where(segment == 2, bounds_ref[0, 2], bounds_ref[0, 3]),
            ),
        )
        alive = own & (inside < bound)
        aux_ref[0] = jnp.where(own, 1.0, 0.0).astype(BF16)
        aux_ref[1] = jnp.where(alive | (column >= 4), 0.0, MASKED).astype(BF16)
        rows_ref[...] = jnp.zeros_like(rows_ref)
        if places is not None:
            wait_all(w_ref, sem)
            x = x_ref[...]
            for part in range(3):
                packed = mm(x, w_ref[part].reshape(features, features), NN)
                if part == 0:
                    packed = (packed + vec_ref[0:1]).astype(BF16) * BF16(0.125)
                elif part == 2:
                    packed = (packed + vec_ref[1:2]).astype(BF16)
                else:
                    packed = packed.astype(BF16)
                for index in range(features // 128):
                    qkv_ref[part, index] = packed[:, index * 128 : (index + 1) * 128]

    query = qkv_ref[0, at]
    key = qkv_ref[1, at]
    value_t = qkv_ref[2, at].T
    ones = jnp.ones((16, tokens), BF16)
    chunk = CHUNK

    def heads(shifted):
        outs, sums = [], []
        for head in range(2):
            inside_head = low_half if head == 0 else ~low_half
            query_aug = jnp.where(inside_head, query, aux_ref[0])
            key_aug = jnp.where(inside_head, key, aux_ref[1])
            value_aug = jnp.concatenate(
                [value_t[head * HEAD_DIM : (head + 1) * HEAD_DIM], ones], axis=0
            )
            parts = []
            for start in range(0, tokens, chunk):
                scores = mm(key_aug, query_aug[start : start + chunk], NT)
                if shifted:
                    scores = scores - jnp.max(scores, axis=0, keepdims=True)
                exponent = jnp.exp(scores).astype(BF16)
                e_ref[head, :, start : start + chunk] = exponent
                mixed = mm(value_aug, exponent, NN)
                total = mixed[HEAD_DIM : HEAD_DIM + 1]
                inverse = 1.0 / total
                rows_ref[pl.ds(step * 2 + head, 1), start : start + chunk] = inverse
                parts.append(mixed[:HEAD_DIM] * inverse)
                sums.append(total)
            outs.append(jnp.concatenate(parts, axis=1))
        ctx_ref[...] = jnp.concatenate(outs, axis=0).T.astype(BF16)
        return jnp.concatenate(sums, axis=1)

    sums = heads(False)
    fits = (jnp.max(sums) <= 2.0**40) & (jnp.min(sums) >= 2.0**-40)

    @pl.when(jnp.logical_not(fits))
    def _():
        heads(True)

    @pl.when(step == pl.num_programs(0) - 1)
    def _():
        inverses = rows_ref[...].T
        high = inverses.astype(BF16).astype(F32)
        low = pltpu.roll(inverses - high, 2 * count, 1)
        rinv_ref[...] = (high + low).astype(BF16)


def attn_forward(bounds, first, count, qkv=None, order=None, x=None, vec=None, weights=(), places=None):
    project = places is not None
    if project:
        tokens, features = x.shape
        pairs = features // 128
    else:
        _, pairs, tokens, _ = qkv.shape
    out_shape = [
        jax.ShapeDtypeStruct((2 * count, tokens, tokens), BF16),
        jax.ShapeDtypeStruct((tokens, 128 * count), BF16),
        jax.ShapeDtypeStruct((tokens, 128), BF16),
    ]
    out_specs = [
        pl.BlockSpec((2, tokens, tokens), lambda step: (step, 0, 0)),
        pl.BlockSpec((tokens, 128), lambda step: (0, step)),
        fixed((tokens, 128)),
    ]
    scratch = [VMEM((2, tokens, 128), BF16), VMEM((128, tokens), F32)]
    if project:
        operands = (bounds, order, x, vec, *weights)
        in_specs = [whole(pltpu.SMEM), whole(pltpu.SMEM), fixed(x.shape), fixed(vec.shape)]
        in_specs += [whole(ANY)] * len(weights)
        out_shape.append(jax.ShapeDtypeStruct((3, pairs, tokens, 128), BF16))
        out_specs.append(fixed((3, pairs, tokens, 128)))
        scratch += [
            VMEM((3, 4, features // BLOCK // 4, BLOCK, features), BF16),
            pltpu.SemaphoreType.DMA,
        ]
    else:
        operands = (bounds, qkv)
        in_specs = [
            whole(pltpu.SMEM),
            pl.BlockSpec((3, 1, tokens, 128), lambda step: (0, step + first, 0, 0)),
        ]
    return pl.pallas_call(
        functools.partial(attn_forward_body, first, count, places),
        grid=(count,),
        out_shape=tuple(out_shape),
        in_specs=in_specs,
        out_specs=tuple(out_specs),
        scratch_shapes=scratch,
        compiler_params=pltpu.CompilerParams(vmem_limit_bytes=VMEM_LIMIT),
        cost_estimate=cost(14),
        name="attn_forward",
    )(*operands)


def normed(z):
    centered = z - jnp.mean(z, axis=-1, keepdims=True)
    variance = jnp.mean(centered * centered, axis=-1, keepdims=True)
    rstd = lax.rsqrt(variance + 1e-05)
    return centered * rstd, rstd


def norm_back(grad, gain, xhat, rstd):
    scaled = grad * gain
    first = jnp.mean(scaled, axis=-1, keepdims=True)
    second = jnp.mean(scaled * xhat, axis=-1, keepdims=True)
    return rstd * (scaled - first - xhat * second)


GELU_A = 0.7978845608028654
GELU_B = 0.044715


def gelu(hidden, sloped):
    square = hidden * hidden
    tanh = jnp.tanh(hidden * (BF16(GELU_A) + BF16(GELU_A * GELU_B) * square))
    chance = BF16(0.5) + BF16(0.5) * tanh
    active = hidden * chance
    if not sloped:
        return active
    inner = BF16(GELU_A) + BF16(3.0 * GELU_A * GELU_B) * square
    return active, chance + active * (BF16(1.0) - tanh) * inner


def column_sum(ref, row, values):
    ref[row : row + 1] += jnp.sum(values.astype(F32), axis=0, keepdims=True)


def weave(vector_work, matrix_work):
    done = 0
    for index, work in enumerate(vector_work):
        work()
        target = (index + 1) * len(matrix_work) // len(vector_work)
        for matrix in matrix_work[done:target]:
            matrix()
        done = target
    for matrix in matrix_work[done:]:
        matrix()


def ffn_body(mode, places, in_names, out_names, scratch_names, *refs):
    forward, backward, last = mode
    refs = list(refs)
    take = lambda count: [refs.pop(0) for _ in range(count)]
    up_at, (out_stream, out_at), down_at = places
    order_ref, vec_ref = take(2)
    weights = take(8)
    ins = dict(zip(in_names, take(len(in_names))))
    outs = dict(zip(out_names, take(len(out_names))))
    if backward:
        dvec_out, *grads = take(3)
    here = dict(zip(scratch_names, take(len(scratch_names))))
    wo_ref, up_ref, down_ref, sem_w, sem_in, sem_out = take(6)
    assert not refs
    tokens = here["ctx"].shape[0]
    features = vec_ref.shape[1]
    groups = up_ref.shape[0]
    per = features // BLOCK
    wo = lambda: wo_ref[...].reshape(features, features)
    up = lambda j, zs: up_ref[j, zs].reshape(-1, features)
    down = lambda j, part: down_ref[j, part].reshape(-1, features)
    every = slice(None)
    up_halves = [slice(0, 2), slice(2, 4)]
    down_halves = [slice(0, 4), slice(4, 8)]
    wide = features // 2
    half_columns = [slice(0, wide), slice(wide, features)]
    of = lambda j: slice(j * features, (j + 1) * features)
    vec = lambda row: vec_ref[row : row + 1]
    copy_in = {
        name: pltpu.make_async_copy(ref, here[name], sem_in.at[index])
        for index, (name, ref) in enumerate(ins.items())
    }
    sem_of = {name: sem_out.at[index] for index, name in enumerate(outs)}

    def leave(*names, rows=slice(None), columns=None):
        for name in names:
            at = (rows,) if columns is None else (rows, columns)
            if name == "do":
                at = (slice(None), rows)
            pltpu.make_async_copy(
                here[name].at[at], outs[name].at[at], sem_of[name]
            ).start()

    def leave_all():
        for name, ref in outs.items():
            wait_all(here[name], sem_of[name])

    blocks = [slice(start, start + TILE) for start in range(0, tokens, TILE)]
    chunks = [slice(start, start + ROWS) for start in range(0, tokens, ROWS)]

    def fetch_out(ref, low):
        pltpu.make_async_copy(ref.at[out_at], wo_ref.at[:, low], sem_w.at[0]).start()

    def fetch_up(ref, low):
        pltpu.make_async_copy(
            ref.at[pl.ds(up_at, groups)], up_ref.at[:, :, low], sem_w.at[1]
        ).start()

    def fetch_down(ref, low):
        for block in range(groups):
            pltpu.make_async_copy(
                ref.at[down_at + block], down_ref.at[:, low, block], sem_w.at[2]
            ).start()

    early = ("ctx", "x", "y") if forward else ("gm", "gs", "xh2", "stat")
    for name in early:
        copy_in[name].start()
    for fetch in (fetch_out, fetch_up, fetch_down) if forward else (fetch_down, fetch_up, fetch_out):
        stream = {fetch_out: out_stream, fetch_up: 0, fetch_down: 1}[fetch]
        for ref, low in each_part(order_ref, weights, stream):
            fetch(ref, low)
    for name in in_names:
        if name not in early:
            copy_in[name].start()
    waited = set()

    def need(*names):
        for name in names:
            if name not in waited:
                waited.add(name)
                copy_in[name].wait()

    if backward:
        dvec_out[...] = jnp.zeros_like(dvec_out)
    if forward:
        need("ctx", "x", "y")
        wait_all(wo_ref, sem_w.at[0])
        for rows in blocks:
            branch = mm(here["ctx"][rows], wo(), NN) + vec(2)
            xh1, rstd1 = normed(here["x"][rows].astype(F32) + branch)
            m1 = xh1 * vec(3) + vec(4)
            here["m1"][rows] = m1
            here["m1b"][rows] = m1.astype(BF16)
            here["y_new"][rows] = here["y"][rows].astype(F32) + branch
            here["xh1"][rows] = xh1.astype(BF16)
            here["stat"][rows, :64] = jnp.broadcast_to(rstd1, (TILE, 64))
            if not backward:
                leave("xh1", "m1b", rows=rows)
        wait_all(up_ref, sem_w.at[1])

        def hidden_dots(j):
            def piece(rows):
                here["work"][j % 2, rows] = mm(here["m1b"][rows], up(j, every), NN)

            return [functools.partial(piece, rows) for rows in blocks]

        def activate(j):
            def piece(rows):
                hidden = (here["work"][j % 2, rows] + vec(8 + j)).astype(BF16)
                if backward:
                    active, slope = gelu(hidden, True)
                    here["hid"][rows, of(j)] = slope
                else:
                    active = gelu(hidden, False)
                    here["hid"][rows, of(j)] = hidden
                here["act"][rows, of(j)] = active

            return [functools.partial(piece, rows) for rows in chunks]

        def branch_dots(j):
            def piece(rows):
                part = mm(here["act"][rows, of(j)], down(j, every), NN)
                here["sum"][rows] = part + (vec(5) if j == 0 else here["sum"][rows])

            return [functools.partial(piece, rows) for rows in blocks]

        weave([], hidden_dots(0))
        wait_all(down_ref, sem_w.at[2])
        for j in range(groups):
            matrix = hidden_dots(j + 1) if j + 1 < groups else []
            if j > 0:
                matrix = matrix + branch_dots(j - 1)
            weave(activate(j), matrix)
            if not backward:
                leave("hid", columns=of(j))
        weave([], branch_dots(groups - 1))
        if last:
            need("cot")
        for rows in blocks:
            xh2, rstd2 = normed(here["m1"][rows] + here["sum"][rows])
            m2 = xh2 * vec(6) + vec(7)
            y = here["y_new"][rows] + here["sum"][rows]
            if not backward:
                here["xh2"][rows] = xh2.astype(BF16)
                here["stat"][rows, 64:] = jnp.broadcast_to(rstd2, (TILE, 64))
                here["m2"][rows] = m2
                here["m2b"][rows] = m2.astype(BF16)
                here["y_new"][rows] = y
                leave("xh2", "stat", "m2", "m2b", "y_new", rows=rows)
                continue
            yh, rstdy = normed(y)
            here["layer_out"][rows] = (m2 + yh * vec(12) + vec(13)).astype(BF16)
            gm = here["cot"][rows].astype(F32)
            gs = norm_back(gm, vec(12), yh, rstdy)
            here["gs"][rows] = gs
            column_sum(dvec_out, 12, gm * yh)
            column_sum(dvec_out, 13, gm)
            column_sum(dvec_out, 6, gm * xh2)
            column_sum(dvec_out, 7, gm)
            dz2 = norm_back(gm, vec(6), xh2, rstd2)
            df = (dz2 + gs).astype(BF16)
            column_sum(dvec_out, 5, df)
            here["df"][rows] = df
            here["sum"][rows] = dz2
            leave("layer_out", "gs", rows=rows)
        if not backward:
            leave_all()
            return
    else:
        need("gm", "gs", "xh2", "stat")
        for rows in blocks:
            gm = here["gm"][rows]
            xh2 = here["xh2"][rows].astype(F32)
            column_sum(dvec_out, 6, gm * xh2)
            column_sum(dvec_out, 7, gm)
            dz2 = norm_back(gm, vec(6), xh2, here["stat"][rows, 64:65])
            df = (dz2 + here["gs"][rows]).astype(BF16)
            column_sum(dvec_out, 5, df)
            here["df"][rows] = df
            here["sum"][rows] = dz2
        wait_all(down_ref, sem_w.at[2])

    def back_dots(j):
        def piece(rows, columns):
            here["work"][j % 2, :, columns] = mm(here["df"][...], down(j, rows), NT)

        return [functools.partial(piece, *part) for part in zip(down_halves, half_columns)]

    def activate_back(j):
        def piece(rows):
            dactive = here["work"][j % 2, rows].astype(BF16)
            slope = here["hid"][rows, of(j)]
            if not forward:
                active, slope = gelu(slope, True)
                here["act"][rows, of(j)] = active
            dhidden = slope * dactive
            here["hid"][rows, of(j)] = dhidden
            column_sum(dvec_out, 8 + j, dhidden)

        return [functools.partial(piece, rows) for rows in chunks]

    def main_dots(j):
        def piece(rows, columns):
            here["sum"][:, columns] += mm(here["hid"][:, of(j)], up(j, rows), NT)

        return [functools.partial(piece, *part) for part in zip(up_halves, half_columns)]

    gup, gdown, gout = here["gup"], here["gdown"], here["gout"]

    def down_grads(j):
        def piece(index, columns):
            rows = slice(j * features + columns.start, j * features + columns.stop)
            gdown[4 * j + 2 * index : 4 * j + 2 * index + 2] = (
                mm(here["act"][:, rows], here["df"][...], TN)
                .astype(BF16)
                .reshape(2, 2, groups, BLOCK, features)
            )

        return [functools.partial(piece, *part) for part in enumerate(half_columns)]

    def up_grads(j):
        def piece(columns):
            source = slice(j * features + columns.start, j * features + columns.stop)
            gup[16 * j : 16 * j + 16, :, :, columns] = (
                mm(here["m1b"][...], here["hid"][:, source], TN)
                .astype(BF16)
                .reshape(16, 2, BLOCK, wide)
            )

        return [functools.partial(piece, columns) for columns in half_columns]

    weave([], back_dots(0))
    if not forward:
        need("hid")
    for j in range(groups):
        if not forward and j == 1:
            wait_all(up_ref, sem_w.at[1])
        matrix = back_dots(j + 1) if j + 1 < groups else []
        if j > 0:
            matrix = matrix + main_dots(j - 1) + down_grads(j - 1)
        weave(activate_back(j), matrix)
    weave([], main_dots(groups - 1))
    need(*in_names)
    if not forward:
        wait_all(wo_ref, sem_w.at[0])

    lane = lax.broadcasted_iota(jnp.int32, (TILE, 128), 1)
    low_half = lane < HEAD_DIM
    column = lane % HEAD_DIM

    def norm_one(rows):
        gm = here["sum"][rows]
        xh1 = here["xh1"][rows].astype(F32)
        column_sum(dvec_out, 3, gm * xh1)
        column_sum(dvec_out, 4, gm)
        dz1 = norm_back(gm, vec(3), xh1, here["stat"][rows, 0:1])
        here["dz1"][rows] = dz1
        da = (dz1 + here["gs"][rows]).astype(BF16)
        column_sum(dvec_out, 2, da)
        here["da"][rows] = da
        leave("dz1", rows=rows)

    heads = features // HEAD_DIM
    iota = lambda shape, axis: lax.broadcasted_iota(jnp.int32, shape, axis)
    if backward:
        mark = lambda picked: jnp.where(picked, 1.0, 0.0).astype(BF16)
        shape = (features, 128)
        place = mark(iota(shape, 1) % HEAD_DIM // 2 == iota(shape, 0) // HEAD_DIM)
        part = iota((128, 128), 0)
        part = jnp.where(part < 2 * heads, part % heads, heads)
        turn = mark(iota((128, 128), 1) % HEAD_DIM // 2 == part)
        shape = (128, features)
        part = iota(shape, 0)
        part = jnp.where(part < 2 * heads, part % heads, heads)
        share = mark(iota(shape, 1) // HEAD_DIM == part)

    def context_one(rows):
        dctx = mm(here["da"][rows], wo(), NT)
        product = dctx * here["ctx"][rows].astype(F32)
        high = product.astype(BF16)
        low = (product - high.astype(F32)).astype(BF16)
        inverse = here["rinv"][rows]
        dots = -(mm(high, place, NN) + mm(low, place, NN)) * mm(inverse, turn, NN)
        high = dots.astype(BF16).astype(F32)
        extra = jnp.where(column % 2 == 0, high, dots - high).astype(BF16)
        scaled = (dctx * mm(inverse, share, NN)).astype(BF16)
        for at in range(heads):
            pair = slice(at // 2 * 128, at // 2 * 128 + 128)
            inside = low_half if at % 2 == 0 else ~low_half
            here["do"][at, rows] = jnp.where(inside, scaled[:, pair], extra)
        leave("do", rows=rows)

    vector = [functools.partial(norm_one, rows) for rows in blocks]
    vector += [functools.partial(context_one, rows) for rows in blocks]
    matrix = down_grads(groups - 1)
    for j in range(groups):
        matrix = matrix + up_grads(j)
    weave(vector, matrix)
    gout[...] = (
        mm(here["ctx"][...], here["da"][...], TN)
        .astype(BF16)
        .reshape(16, 2, BLOCK, features)
    )
    for index, ref in enumerate(grads):
        core = order_ref[AT_CORE] if index == 0 else 1 - order_ref[AT_CORE]
        at = lambda block, count=1: ref.at[pl.ds(16 * block, 16 * count)]
        pltpu.make_async_copy(gup.at[:, core], at(0, groups), sem_w.at[1]).start()
        pltpu.make_async_copy(gout.at[:, core], at(groups), sem_w.at[0]).start()
        for block in range(groups):
            pltpu.make_async_copy(
                gdown.at[:, core, block], at(groups + 1 + block), sem_w.at[2]
            ).start()
    wait_all(gup, sem_w.at[1])
    wait_all(gout, sem_w.at[0])
    wait_all(gdown, sem_w.at[2])
    leave_all()


def ffn_call(forward, backward, last, order, vec, weights, places, ctx, tiled, rinv=None):
    tokens, features = ctx.shape
    groups = 4
    width = groups * features
    per = features // BLOCK
    heads = features // HEAD_DIM
    if forward:
        ins = dict(zip(("ctx", "x", "y", "cot"), (ctx, *tiled)))
    else:
        names = ("ctx", "xh1", "xh2", "stat", "m1b", "hid", "gm", "gs")
        ins = dict(zip(names, (ctx, *tiled)))
    if backward:
        ins["rinv"] = rinv
    square, full = (tokens, features), (tokens, width)
    small = (tokens, 128)
    scratch = {name: (value.shape, value.dtype) for name, value in ins.items()}
    scratch["work"] = ((2, *square), F32)
    scratch["sum"] = (square, F32)
    scratch["act"] = (full, BF16)
    if forward:
        scratch.update(
            m1=(square, F32), m1b=(square, BF16), y_new=(square, F32), xh1=(square, BF16),
            stat=(small, F32), hid=(full, BF16),
        )
    if last:
        scratch.update(layer_out=(square, BF16), gs=(square, F32))
    if forward and not backward:
        scratch.update(xh2=(square, BF16), m2=(square, F32), m2b=(square, BF16))
        out_names = ["xh1", "xh2", "stat", "m1b", "hid", "m2", "m2b", "y_new"]
    else:
        scratch.update(
            df=(square, BF16), dz1=(square, F32), da=(square, BF16), do=((heads, *small), BF16),
            gup=((16 * groups, 2, BLOCK, features), BF16),
            gdown=((16, 2, groups, BLOCK, features), BF16),
            gout=((16, 2, BLOCK, features), BF16),
        )
        out_names = (["layer_out", "gs"] if last else []) + ["dz1", "do"]
    out_shape = [jax.ShapeDtypeStruct(*scratch[name]) for name in out_names]
    out_specs = [whole(ANY)] * len(out_names)
    if backward:
        half = jax.ShapeDtypeStruct((16 * (2 * groups + 1), BLOCK, features), BF16)
        out_shape += [jax.ShapeDtypeStruct((16, features), F32), half, half]
        out_specs += [whole(), whole(ANY), whole(ANY)]
    return pl.pallas_call(
        functools.partial(
            ffn_body, (forward, backward, last), places, tuple(ins), tuple(out_names),
            tuple(scratch),
        ),
        out_shape=tuple(out_shape),
        in_specs=[whole(pltpu.SMEM), whole()] + [whole(ANY)] * (8 + len(ins)),
        out_specs=tuple(out_specs),
        scratch_shapes=[VMEM(*kind) for kind in scratch.values()]
        + [
            VMEM((4, 8, BLOCK, features), BF16),
            VMEM((groups, 4, 8, BLOCK, features), BF16),
            VMEM((4, 8, groups, BLOCK, features), BF16),
            pltpu.SemaphoreType.DMA((3,)),
            pltpu.SemaphoreType.DMA((len(ins),)),
            pltpu.SemaphoreType.DMA((len(out_names),)),
        ],
        compiler_params=pltpu.CompilerParams(vmem_limit_bytes=VMEM_LIMIT),
        cost_estimate=cost(6 * forward + 12 * backward),
        name="ffn_" + ("f" if forward else "") + ("b" if backward else ""),
    )(order, vec, *weights, *ins.values())


def attn_backward_body(
    first,
    count,
    places,
    order_ref,
    e_ref,
    do_ref,
    qkv_ref,
    x_ref,
    gm_ref,
    *refs,
):
    weights = refs[:8]
    gm_out, dvec_out = refs[8:10]
    grads = refs[10:12]
    w_ref, dqkv_s, ds_s, g_s, sem, sem_g = refs[12:]
    step = pl.program_id(0)
    tokens, features = x_ref.shape
    lane = lax.broadcasted_iota(jnp.int32, (tokens, 128), 1)
    low_half = lane < HEAD_DIM
    column = lane % HEAD_DIM
    width = 128 * count

    @pl.when(step == 0)
    def _():
        fetch_attn(order_ref, weights, places, w_ref, sem, pl.ds(first * 128, width))

    query = qkv_ref[0, 0]
    key_t = qkv_ref[1, 0].T
    value = qkv_ref[2, 0]
    chunk = CHUNK
    dquery, dkey, dvalue = [], [], []
    for head in range(2):
        inside = low_half if head == 0 else ~low_half
        ones = jnp.where(column // 2 == 2 * (step + first) + head, 1.0, 0.0).astype(BF16)
        value_aug = jnp.where(inside, value, ones)
        key_head = key_t[head * HEAD_DIM : (head + 1) * HEAD_DIM]
        parts = []
        for start in range(0, tokens, chunk):
            columns = slice(start, start + chunk)
            dchances = mm(value_aug, do_ref[head, columns], NT)
            dscores = (e_ref[head, :, columns].astype(F32) * dchances).astype(BF16)
            ds_s[head, :, columns] = dscores
            parts.append(mm(key_head, dscores, NN))
        dquery.append(jnp.concatenate(parts, axis=1))
        dkey.append(mm(ds_s[head], query, NN))
        dvalue.append(mm(e_ref[head], do_ref[head], NN))
    here = pl.ds(pl.multiple_of(step * 128, 128), 128)
    dqkv_s[0, :, here] = (jnp.concatenate(dquery, axis=0).T * 0.125).astype(BF16)
    dqkv_s[1, :, here] = jnp.where(low_half, dkey[0], dkey[1]).astype(BF16)
    dqkv_s[2, :, here] = jnp.where(low_half, dvalue[0], dvalue[1]).astype(BF16)

    @pl.when(step == count - 1)
    def _():
        wait_all(w_ref, sem)
        x = x_ref[...]
        for part in range(3):
            g_s[16 * part : 16 * part + 16] = (
                mm(x, dqkv_s[part], TN).astype(BF16).reshape((16, 2, BLOCK, width))
            )
        for index, ref in enumerate(grads):
            core = order_ref[AT_CORE] if index == 0 else 1 - order_ref[AT_CORE]
            pltpu.make_async_copy(g_s.at[:, core], ref, sem_g).start()
        gm = gm_ref[...]
        for part in range(3):
            gm = gm + mm(dqkv_s[part], w_ref[part].reshape(features, width), NT)
        gm_out[...] = gm
        dvec_out[...] = jnp.zeros_like(dvec_out)
        column_sum(dvec_out, 0, dqkv_s[0])
        column_sum(dvec_out, 1, dqkv_s[2])
        wait_all(g_s, sem_g)


def attn_backward(order, first, count, e, e_first, do, qkv, x, gm, weights, places):
    tokens, features = x.shape
    per = features // BLOCK
    width = 128 * count
    half = jax.ShapeDtypeStruct((16 * 3, BLOCK, width), BF16)
    return pl.pallas_call(
        functools.partial(attn_backward_body, first, count, places),
        grid=(count,),
        out_shape=(
            jax.ShapeDtypeStruct((tokens, features), F32),
            jax.ShapeDtypeStruct((8, width), F32),
            half,
            half,
        ),
        in_specs=[
            whole(pltpu.SMEM),
            pl.BlockSpec((2, tokens, tokens), lambda step: (step + e_first, 0, 0)),
            pl.BlockSpec((2, tokens, 128), lambda step: (step + first, 0, 0)),
            pl.BlockSpec((3, 1, tokens, 128), lambda step: (0, step + first, 0, 0)),
            fixed(x.shape),
            fixed(gm.shape),
        ]
        + [whole(ANY)] * len(weights),
        out_specs=(fixed(gm.shape), fixed((8, width))) + (whole(ANY),) * 2,
        scratch_shapes=[
            VMEM((3, 4, 8, BLOCK, width), BF16),
            VMEM((3, tokens, width), BF16),
            VMEM((2, tokens, tokens), BF16),
            VMEM((16 * 3, 2, BLOCK, width), BF16),
            pltpu.SemaphoreType.DMA,
            pltpu.SemaphoreType.DMA,
        ],
        compiler_params=pltpu.CompilerParams(vmem_limit_bytes=VMEM_LIMIT),
        cost_estimate=cost(26),
        name="attn_backward",
    )(order, e, do, qkv, x, gm, *weights)


def blocks_of(matrix, features):
    rows, columns = matrix.shape
    shaped = matrix.reshape(rows // BLOCK, BLOCK, columns // features, features)
    return shaped.transpose(0, 2, 1, 3)


def matrix_of(blocks):
    rows, columns, block, features = blocks.shape
    return blocks.transpose(0, 2, 1, 3).reshape(rows * block, columns * features)


CORE, X, Y, Z = 1, 2, 4, 8
Z_MASKS = (0, Z, 2 * Z, 3 * Z)
PLANE_MASKS = (0, X, Y, X | Y)
LOW_MASKS = [
    core | second | first
    for high, low in ((X, Y), (Y, X))
    for core in (0, CORE)
    for second in (0, high)
    for first in (0, low)
]


def swap(part, mask):
    return lax.ppermute(part, AXES, [(device, device ^ mask) for device in range(32)])


def after(value, *earlier):
    return lax.optimization_barrier((value, earlier))[0]


def prepare(place, in_w, out_w, up_w, down_w, vectors, final_norm):
    _, block, features = out_w.shape
    groups = up_w.shape[2] // features
    width, spread = vectors.shape[1], final_norm.shape[0]

    def body(place_ref, in_ref, out_ref, up_ref, down_ref, vec_ref, last_ref, *refs):
        own, rows = refs[:3], refs[3]
        rows[...] = jnp.zeros_like(rows)
        rows[0:2, :width] = vec_ref[...].astype(F32)
        rows[8:9, :spread] = last_ref[...].astype(F32)
        field = rows[0:8, :256]
        field = jnp.where(place_ref[AT_FIELDS] == 0, field, pltpu.roll(field, 64, 1))
        last = rows[8:16, :128]
        chosen = last
        for turn in range(1, 128 // spread):
            turned = pltpu.roll(last, turn * spread, 1)
            chosen = jnp.where(place_ref[AT_FIELDS + 1] == turn * spread, turned, chosen)
        rows[...] = jnp.zeros_like(rows)
        rows[0:1, :256] = field[0:1]
        rows[0:1, 256:512] = field[1:2]
        rows[1:2, :128] = chosen[0:1]
        parts = lambda ref, layer, count: [
            ref[layer, :, features * j : features * (j + 1)] for j in range(count)
        ]
        qkv = [parts(in_ref, layer, 3) for layer in range(2)]
        up = [parts(up_ref, layer, groups) for layer in range(2)]
        down = [
            [down_ref[layer, block * j : block * (j + 1)] for j in range(groups)]
            for layer in range(2)
        ]
        out = [out_ref[layer] for layer in range(2)]
        laid = [
            qkv[0] + [rows[...].astype(BF16)],
            qkv[1][:2] + up[0] + qkv[1][2:] + [out[0]] + down[0],
            up[1] + [out[1]] + down[1],
        ]
        for ref, pieces in zip(own, laid):
            for index, piece in enumerate(pieces):
                ref[index] = piece

    outs = [(count, block, features) for count in (4, 2 * groups + 4, 2 * groups + 1)]
    operands = (in_w, out_w, up_w, down_w, vectors, final_norm[None])
    return pl.pallas_call(
        body,
        grid=(1,),
        out_shape=tuple(jax.ShapeDtypeStruct(shape, BF16) for shape in outs),
        in_specs=[whole(pltpu.SMEM)] + [fixed(part.shape) for part in operands],
        out_specs=tuple(fixed(shape) for shape in outs),
        scratch_shapes=[VMEM((block, features), F32)],
        compiler_params=pltpu.CompilerParams(vmem_limit_bytes=VMEM_LIMIT),
        name="prepare",
    )(place, *operands)


def gather_z(own):
    return [own] + [swap(own, mask) for mask in Z_MASKS[1:]]


def pack_z(place, pieces):
    blocks, *rest = pieces[0].shape

    def body(place_ref, *refs):
        for index in range(4):
            refs[4][:, place_ref[AT_Z] ^ index] = refs[index][...]

    return pl.pallas_call(
        body,
        out_shape=jax.ShapeDtypeStruct((blocks, 4, *rest), BF16),
        in_specs=[whole(pltpu.SMEM)] + [whole()] * 4,
        out_specs=whole(),
        compiler_params=pltpu.CompilerParams(vmem_limit_bytes=SMALL_VMEM),
        name="pack_z",
    )(place, *pieces)


def gather_first(four, cut):
    streams = (four[:cut], Y, X), (four[cut:], X, Y)
    return [(part, swap(part, first), second) for part, first, second in streams]


def gather_second(streams, near):
    return [swap(part, second) for part, (_, _, second) in zip(near, streams)]


def join_two(streams):
    def body(a_ref, b_ref, c_ref, d_ref, out0, out1):
        out0[0], out0[1] = a_ref[...], b_ref[...]
        out1[0], out1[1] = c_ref[...], d_ref[...]

    parts = [part for near, far, _ in streams for part in (near, far)]
    shapes = [(2, *parts[0].shape), (2, *parts[2].shape)]
    return pl.pallas_call(
        body,
        out_shape=tuple(jax.ShapeDtypeStruct(shape, BF16) for shape in shapes),
        in_specs=[whole()] * 4,
        out_specs=(whole(), whole()),
        compiler_params=pltpu.CompilerParams(vmem_limit_bytes=SMALL_VMEM),
        name="join_two",
    )(*parts)


def gather_core(near, far):
    near = after(near, far)
    return [
        part
        for pair in zip(near, far)
        for part in (*pair, *[swap(half, CORE) for half in pair])
    ]


def sum_core(mine, other):
    return mine, swap(other, CORE)


def sum_plane(place, pairs):
    pairs = [[part.reshape(-1, 4, 4, *part.shape[1:]) for part in pair] for pair in pairs]
    rest = pairs[0][0].shape[3:]
    sizes = [pair[0].shape[0] for pair in pairs]
    count = 3 if all(size % 3 == 0 for size in sizes) else 1
    starts = [sum(sizes[:index]) // count for index in range(len(sizes))]
    ends = [(start * count + size) // count for start, size in zip(starts, sizes)]
    operands = [part for pair in pairs for part in pair]

    def block_of(start, end):
        at = lambda step: (jnp.clip(step, start, end - 1) - start, 0, 0, 0, 0)
        return pl.BlockSpec((count, 4, 4, *rest), at)

    def body(place_ref, *refs):
        outs = refs[len(operands) :]
        step = pl.program_id(0)
        for index, (start, end) in enumerate(zip(starts, ends)):
            left, right = refs[2 * index : 2 * index + 2]

            @pl.when((step >= start) & (step < end))
            def _(left=left, right=right):
                for mask, out in enumerate(outs):
                    plane = place_ref[AT_PLANE] ^ mask
                    out[...] = (
                        left[:, :, plane].astype(F32) + right[:, :, plane].astype(F32)
                    ).astype(BF16)

    blocks = sum(sizes)
    return pl.pallas_call(
        body,
        grid=(ends[-1],),
        out_shape=(jax.ShapeDtypeStruct((blocks, 4, *rest), BF16),) * 4,
        in_specs=[whole(pltpu.SMEM)]
        + [block_of(*span) for span in zip(starts, ends) for _ in range(2)],
        out_specs=(pl.BlockSpec((count, 4, *rest), lambda step: (step, 0, 0, 0)),) * 4,
        compiler_params=pltpu.CompilerParams(vmem_limit_bytes=SMALL_VMEM),
        name="sum_plane",
    )(place, *operands)


def send_plane(parts):
    return [parts[0]] + [swap(part, mask) for part, mask in zip(parts[1:], PLANE_MASKS[1:])]


def sum_z(place, parts):
    blocks, _, *rest = parts[0].shape
    count = 3 if blocks % 3 == 0 else 1

    def body(place_ref, *refs):
        for mask in range(4):
            z = place_ref[AT_Z] ^ mask
            total = refs[0][:, z].astype(F32)
            for ref in refs[1:4]:
                total = total + ref[:, z].astype(F32)
            refs[4 + mask][...] = total.astype(BF16)

    return pl.pallas_call(
        body,
        grid=(blocks // count,),
        out_shape=(jax.ShapeDtypeStruct((blocks, *rest), BF16),) * 4,
        in_specs=[whole(pltpu.SMEM)]
        + [pl.BlockSpec((count, 4, *rest), lambda step: (step, 0, 0, 0))] * 4,
        out_specs=(pl.BlockSpec((count, *rest), lambda step: (step, 0, 0)),) * 4,
        compiler_params=pltpu.CompilerParams(vmem_limit_bytes=SMALL_VMEM),
        name="sum_z",
    )(place, *parts)


def send_z(pieces):
    return [pieces[0]] + [swap(piece, mask) for piece, mask in zip(pieces[1:], Z_MASKS[1:])]


def finish(place, ffn1, ffn0, attn0, width, spread):
    _, block, features = ffn1[0].shape
    groups = (ffn1[0].shape[0] - 1) // 2

    def body(place_ref, *refs):
        parts = [refs[:4], refs[4:8], refs[8:12]]
        in_out, out_out, up_out, down_out, vec_out, last_out = refs[12:]

        def total(part, index):
            value = parts[part][0][index].astype(F32)
            for ref in parts[part][1:]:
                value = value + ref[index].astype(F32)
            return value

        for layer, part in ((1, 0), (0, 1)):
            for j in range(groups):
                up_out[layer, :, features * j : features * (j + 1)] = total(part, j)
                down_out[layer, block * j : block * (j + 1)] = total(part, groups + 1 + j)
            out_out[layer] = total(part, groups)
        for layer, part, start in ((1, 1, 2 * groups + 1), (0, 2, 0)):
            for j in range(3):
                in_out[layer, :, features * j : features * (j + 1)] = total(part, start + j)
        rows = total(2, 3)
        for layer in range(2):
            field = rows[0:8, 256 * layer : 256 * layer + 256]
            turned = pltpu.roll(field, 192, 1)
            chosen = jnp.where(place_ref[AT_FIELDS] == 0, field, turned)
            vec_out[layer : layer + 1] = chosen[0:1, :width]
        field = rows[0:8, :128]
        chosen = field
        for turn in range(1, 128 // spread):
            turned = pltpu.roll(field, 128 - turn * spread, 1)
            chosen = jnp.where(place_ref[AT_FIELDS + 1] == turn * spread, turned, chosen)
        last_out[...] = chosen[1:2, :spread]

    shapes = [
        (2, block, 3 * features),
        (2, block, features),
        (2, block, groups * features),
        (2, block * groups, features),
        (2, width),
        (1, spread),
    ]
    return pl.pallas_call(
        body,
        out_shape=tuple(jax.ShapeDtypeStruct(shape, F32) for shape in shapes),
        in_specs=[whole(pltpu.SMEM)] + [whole()] * 12,
        out_specs=tuple(whole() for _ in shapes),
        compiler_params=pltpu.CompilerParams(vmem_limit_bytes=SMALL_VMEM),
        name="finish",
    )(place, *ffn1, *ffn0, *attn0)


def field_of(device, width):
    start = device * width
    return start // 128 * 128, start % 128


def unpack_vectors(order, parts, width, spread):
    def body(order_ref, *refs):
        refs, out, flat, last = refs[:4], *refs[4:]
        flat[...] = jnp.zeros_like(flat)
        last[...] = jnp.zeros_like(last)
        out[...] = jnp.zeros_like(out)
        for index, ref in enumerate(refs):
            for near, z in [(near, z) for near in range(2) for z in range(4)]:
                owner = 8 * z + order_ref[8 + 2 * index + near]
                rows = ref[near, 0, z].astype(F32)
                at = pl.ds(pl.multiple_of(owner * width // 128 * 128, 128), 256)
                for layer in range(2):
                    flat[layer : layer + 1, at] += rows[0:1, 256 * layer : 256 * layer + 256]
                at = pl.ds(pl.multiple_of(owner * spread // 128 * 128, 128), 128)
                last[0:1, at] += rows[1:2, :128]
        for layer in range(2):
            for row in range(12):
                out[layer, row : row + 1] = flat[layer : layer + 1, row * 512 : row * 512 + 512]
            for row in range(2):
                out[layer, 12 + row : 13 + row] = last[0:1, row * 512 : row * 512 + 512]

    features = parts[0].shape[-1]
    at = parts[0].shape[1] - 1
    return pl.pallas_call(
        body,
        grid=(1,),
        out_shape=jax.ShapeDtypeStruct((2, 16, features), F32),
        in_specs=[whole(pltpu.SMEM)]
        + [
            pl.BlockSpec((2, 1, *part.shape[2:]), lambda step: (0, at, 0, 0, 0)) for part in parts
        ],
        out_specs=fixed((2, 16, features)),
        scratch_shapes=[VMEM((8, 12 * features), F32), VMEM((8, 2 * features), F32)],
        compiler_params=pltpu.CompilerParams(vmem_limit_bytes=SMALL_VMEM),
        name="unpack_vectors",
    )(order, *parts)


def pack_vectors(order, attn_rows, ffn_rows, width, spread):
    features = ffn_rows[0].shape[1]

    def body(order_ref, a0, a1, f0, f1, out0, out1, flat, last):
        for layer, (attn, ffn) in enumerate(((a0, f0), (a1, f1))):
            for row in range(12):
                source = attn if row < 2 else ffn
                flat[layer : layer + 1, row * 512 : row * 512 + 512] = source[row : row + 1]
        for row in range(2):
            last[0:1, row * 512 : row * 512 + 512] = f1[12 + row : 13 + row]
        for half, out in enumerate((out0, out1)):
            out[...] = jnp.zeros_like(out)
            core = order_ref[AT_CORE] if half == 0 else 1 - order_ref[AT_CORE]
            for pair in range(16):
                owner = 2 * pair + core
                at = pl.ds(pl.multiple_of(owner * width // 128 * 128, 128), 256)
                fields = [flat[layer : layer + 1, at] for layer in range(2)]
                at = pl.ds(pl.multiple_of(owner * spread // 128 * 128, 128), 128)
                final = jnp.concatenate([last[0:1, at], jnp.zeros((1, 384), F32)], axis=1)
                rows = [jnp.concatenate(fields, axis=1), final, jnp.zeros((BLOCK - 2, 512), F32)]
                out[pair] = jnp.concatenate(rows, axis=0).astype(BF16)

    return pl.pallas_call(
        body,
        out_shape=(jax.ShapeDtypeStruct((16, BLOCK, features), BF16),) * 2,
        in_specs=[whole(pltpu.SMEM)] + [whole()] * 4,
        out_specs=(whole(), whole()),
        scratch_shapes=[VMEM((8, 12 * features), F32), VMEM((8, 2 * features), F32)],
        compiler_params=pltpu.CompilerParams(vmem_limit_bytes=SMALL_VMEM),
        name="pack_vectors",
    )(order, *attn_rows, *ffn_rows)


def total_of(pieces):
    total = pieces[0].astype(F32)
    for piece in pieces[1:]:
        total = total + piece.astype(F32)
    return total


def local(
    main_residual,
    side_residual,
    cotangent,
    lengths,
    input_weight,
    output_weight,
    expand_weight,
    reduce_weight,
    vectors,
    final_norm,
):
    tokens, features = main_residual.shape
    layers = input_weight.shape[0]
    assert lengths.shape[0] == 1 and layers == 2
    per = features // BLOCK
    pairs = features // 128
    half_pairs = pairs // 2
    groups = expand_weight.shape[2] // features
    fast = lax.axis_size(AXES) == 32 and per == 32
    ffn_at = ((2, (1, 1), 2), (0, (0, groups), 0))
    width = vectors.shape[1]
    spread = final_norm.shape[0]

    def vec_rows(all_vectors, final_full):
        return jnp.concatenate(
            [
                all_vectors.reshape(layers, 12, features),
                jnp.broadcast_to(final_full.reshape(1, 2, features), (layers, 2, features)),
                jnp.zeros((layers, 2, features), F32),
            ],
            axis=1,
        )

    if fast:
        me = lax.axis_index(AXES)
        order = jnp.concatenate(
            [
                (me ^ jnp.array(LOW_MASKS, jnp.int32)) & 7,
                jnp.stack(
                    [
                        me // Z,
                        me // X & 3,
                        me & CORE,
                        field_of(me, width)[1],
                        field_of(me, spread)[1],
                    ]
                ),
            ]
        )
        own = prepare(
            order, input_weight, output_weight, expand_weight, reduce_weight, vectors, final_norm
        )
        z0 = gather_z(own[0])
        z1 = gather_z(after(own[1], z0[1:]))
        two = gather_first(pack_z(order, z0), 2)
        near = join_two(two)
        attn0 = gather_core(near, gather_second(two, near))
        vec = unpack_vectors(order, attn0[4:], width, spread)
        two = gather_first(pack_z(order, after(z1, near)), groups + 2)
        z2 = gather_z(after(own[2], attn0))
        near = join_two(two)
        far = gather_second(two, near)
        x0 = after(main_residual, near)
    else:
        gather = lambda part, axis: lax.all_gather(part, AXES, axis=axis, tiled=True)
        order = jnp.array(LOW_MASKS + [0] * 5, jnp.int32)

        def streams(*two):
            parts = []
            for stream, blocks in enumerate(two):
                joined = jnp.concatenate(blocks, axis=1)
                joined = joined.reshape(4, 8, *joined.shape[1:]).transpose(1, 2, 0, 3, 4)
                lows = LOW_MASKS[8 * stream : 8 * stream + 8]
                parts += [joined[jnp.array(lows[at : at + 2])] for at in range(0, 8, 2)]
            return parts

        vec = vec_rows(gather(vectors, 1).astype(F32), gather(final_norm, 0).astype(F32))
        parts = []
        for layer in range(layers):
            qkv = blocks_of(gather(input_weight[layer], 0), features)
            up = blocks_of(gather(expand_weight[layer], 0), features)
            out = blocks_of(gather(output_weight[layer], 0), features)
            down = gather(reduce_weight[layer], 0).reshape(per, -1, BLOCK, features)
            parts.append((qkv, up, out, down))
        (qkv0, up0, out0, down0), (qkv1, up1, out1, down1) = parts
        attn0 = streams([qkv0[:, :2]], [qkv0[:, 2:]])
        mixed = streams([qkv1[:, :2], up0], [qkv1[:, 2:], out0, down0])
        ffn1 = streams([up1, out1], [down1])
        x0 = main_residual

    e0, ctx0, rinv0, qkv0 = attn_forward(
        lengths, 0, pairs, None, order, x0, vec[0], attn0, 0
    )
    x0 = main_residual
    if fast:
        far, z2 = after((far, z2), e0)
        mixed = gather_core(near, far)
        two = gather_first(pack_z(order, z2), groups + 1)
        x0 = after(x0, *[part for part, _, _ in two])
    xh1, xh2, stat, m1b, hid, m2, m2b, y = ffn_call(
        True, False, False, order, vec[0], mixed, ffn_at[0], ctx0, (x0, side_residual)
    )
    x1 = m2b
    if fast:
        two = [(part, after(got, m2b), mask) for part, got, mask in two]
        near = join_two(two)
        x1 = after(m2b, near)
        far = gather_second(two, near)
    e1, ctx1, rinv1, qkv1 = attn_forward(
        lengths, 0, pairs, None, order, x1, vec[1], mixed, 0
    )
    if fast:
        ffn1 = gather_core(near, after(far, e1))
    layer_out, grad_side, gm, do, dvec1, *gf1 = ffn_call(
        True, True, True, order, vec[1], ffn1, ffn_at[1], ctx1, (m2, y, cotangent), rinv1
    )
    if fast:
        f1 = sum_plane(order, [sum_core(*gf1)])
        gm = after(gm, f1)
        f1 = send_plane(f1)
    gm, dvec1a, *gi1 = attn_backward(
        order, 0, pairs, e1, 0, do, qkv1, m2b, gm, mixed, 0
    )
    if fast:
        i1 = sum_core(*gi1)
        f1 = sum_z(order, after(f1, gm))
        gm = after(gm, f1)
        f1 = send_z(f1)
    gm, do, dvec0, *gf0 = ffn_call(
        False, True, False, order, vec[0], mixed, ffn_at[0], ctx0,
        (xh1, xh2, stat, m1b, hid, gm, grad_side), rinv0,
    )
    if fast:
        f1, i1 = after((f1, i1), gm)
        f0 = sum_plane(order, [sum_core(*after(gf0, f1)), i1])
        gm = after(gm, f0)
        f0 = send_plane(f0)
    grad_main, dvec0a, *gi0 = attn_backward(
        order, 0, pairs, e0, 0, do, qkv0, main_residual, gm, attn0, 0
    )

    if fast:
        rows = pack_vectors(order, (dvec0a, dvec1a), (dvec0, dvec1), width, spread)
        i0 = sum_plane(order, [sum_core(*gi0), sum_core(*rows)])
        f0 = send_z(sum_z(order, after(f0, grad_main)))
        i0 = send_plane(after(i0, f0[0]))
        i0 = send_z(sum_z(order, i0))
        grad_in, grad_out, grad_up, grad_down, grad_vec, grad_final = finish(
            order, f1, f0, i0, width, spread
        )
        grad_final = grad_final[0]
    else:
        scatter = lambda part, axis: lax.psum_scatter(
            part, AXES, scatter_dimension=axis, tiled=True
        ).astype(F32)

        def natural(even, odd):
            joined = jnp.stack([even, odd], axis=1)
            return joined.reshape(-1, per, *even.shape[1:]).swapaxes(0, 1)

        both = lambda make: jnp.stack(
            [make(natural(*i), natural(*f)) for i, f in ((gi0, gf0), (gi1, gf1))]
        )
        grad_in = scatter(both(lambda i, f: matrix_of(i)), 1)
        grad_up = scatter(both(lambda i, f: matrix_of(f[:, :groups])), 1)
        grad_out = scatter(both(lambda i, f: matrix_of(f[:, groups : groups + 1])), 1)
        grad_down = scatter(both(lambda i, f: f[:, groups + 1 :].reshape(-1, features)), 1)
        dvec = [
            jnp.concatenate([first[0:2], rest[2:12]]).reshape(-1)
            for first, rest in ((dvec0a, dvec0), (dvec1a, dvec1))
        ]
        grad_vec = scatter(jnp.stack(dvec), 1)
        grad_final = scatter(dvec1[12:14].reshape(-1), 0)
    return (
        layer_out,
        grad_main,
        grad_side,
        grad_in,
        grad_out,
        grad_up,
        grad_down,
        grad_vec,
        grad_final,
    )


def solution(mesh):
    rows = P(AXES, None)
    middle = P(None, AXES, None)
    return jax.shard_map(
        local,
        mesh=mesh,
        in_specs=(rows, rows, rows, rows, middle, middle, middle, middle, P(None, AXES), P(AXES)),
        out_specs=(rows, rows, rows, middle, middle, middle, middle, P(None, AXES), P(AXES)),
        check_vma=False,
    )
```

```python
import functools

import jax
import jax.numpy as jnp
from jax import lax
from jax.experimental import pallas as pl
from jax.experimental.pallas import tpu as pltpu
from jax.sharding import PartitionSpec as P

HEAD_DIM = 64
AXES = ("wide", "narrow")
F32 = jnp.float32
BF16 = jnp.bfloat16
NN = (((1,), (0,)), ((), ()))
NT = (((1,), (1,)), ((), ()))
TN = (((0,), (0,)), ((), ()))
MASKED = -1000000000.0
VMEM_LIMIT = 60 * 2**20
SMALL_VMEM = 24 * 2**20


def cost(microseconds):
    return pl.CostEstimate(
        flops=microseconds * 10**9, bytes_accessed=microseconds * 10**6, transcendentals=0
    )


BLOCK = 16
CHUNK = 512
TILE = 256
ROWS = 64
VMEM = pltpu.VMEM
ANY = pl.ANY


def mm(left, right, dims):
    return lax.dot_general(left, right, dims, preferred_element_type=F32)


def whole(memory=VMEM):
    return pl.BlockSpec(memory_space=memory)


def fixed(shape):
    zeros = (0,) * len(shape)
    return pl.BlockSpec(shape, lambda step: zeros)


def rows_of(tile, width):
    return pl.BlockSpec((tile, width), lambda step: (step, 0))


AT_Z, AT_PLANE, AT_CORE, AT_FIELDS = 16, 17, 18, 19


def each_part(place_ref, weights, stream):
    return [
        (weights[index].at[near], place_ref[2 * index + near])
        for index in range(4 * stream, 4 * stream + 4)
        for near in range(2)
    ]


def wait_all(ref, sem):
    pltpu.make_async_copy(ref, ref, sem).wait()


def fetch_attn(order_ref, weights, at, w_ref, sem, columns):
    for ref, low in each_part(order_ref, weights, 0):
        pltpu.make_async_copy(
            ref.at[pl.ds(at, 2), :, :, columns], w_ref.at[pl.ds(0, 2), :, low], sem
        ).start()
    for ref, low in each_part(order_ref, weights, 1):
        pltpu.make_async_copy(ref.at[at, :, :, columns], w_ref.at[2, :, low], sem).start()


def attn_forward_body(first, count, places, layer, *refs):
    refs = list(refs)
    take = lambda: refs.pop(0)
    bounds_ref = take()
    if places is not None:
        order_ref, x_ref, vec_ref = take(), take(), take()
        weights = [take() for _ in range(8)]
        e_ref, ctx_ref, rinv_ref, qkv_ref, aux_ref, rows_ref, w_ref, sem = refs
        at = pl.program_id(0) + first
    else:
        qkv_ref, e_ref, ctx_ref, rinv_ref, aux_ref, rows_ref = refs
        at = 0
    step = pl.program_id(0)
    tokens = ctx_ref.shape[0]
    lane = lax.broadcasted_iota(jnp.int32, (tokens, 128), 1)
    low_half = lane < HEAD_DIM

    @pl.when(step == 0)
    def _():
        if places is not None:
            features = x_ref.shape[1]
            fetch_attn(order_ref, weights, places, w_ref, sem, pl.ds(0, features))
        token = lax.broadcasted_iota(jnp.int32, (tokens, 128), 0)
        column = lane % HEAD_DIM
        single = bounds_ref[0, 1] == 0
        quarter = tokens // 4
        segment = jnp.where(single, 0, token // quarter)
        inside = jnp.where(single, token, token % quarter)
        own = column == segment
        bound = jnp.where(
            segment == 0,
            bounds_ref[0, 0],
            jnp.where(
                segment == 1,
                bounds_ref[0, 1],
                jnp.where(segment == 2, bounds_ref[0, 2], bounds_ref[0, 3]),
            ),
        )
        alive = own & (inside < bound)
        aux_ref[0] = jnp.where(own, 1.0, 0.0).astype(BF16)
        aux_ref[1] = jnp.where(alive | (column >= 4), 0.0, MASKED).astype(BF16)
        rows_ref[...] = jnp.zeros_like(rows_ref)
        if places is not None:
            wait_all(w_ref, sem)
            x = x_ref[...]
            for part in range(3):
                packed = mm(x, w_ref[part].reshape(features, features), NN)
                if part == 0:
                    packed = (packed + vec_ref[layer, 0:1]).astype(BF16) * BF16(0.125)
                elif part == 2:
                    packed = (packed + vec_ref[layer, 1:2]).astype(BF16)
                else:
                    packed = packed.astype(BF16)
                for index in range(features // 128):
                    qkv_ref[part, index] = packed[:, index * 128 : (index + 1) * 128]

    query = qkv_ref[0, at]
    key = qkv_ref[1, at]
    value_t = qkv_ref[2, at].T
    ones = jnp.ones((16, tokens), BF16)
    chunk = CHUNK

    def heads(shifted):
        outs, sums = [], []
        for head in range(2):
            inside_head = low_half if head == 0 else ~low_half
            query_aug = jnp.where(inside_head, query, aux_ref[0])
            key_aug = jnp.where(inside_head, key, aux_ref[1])
            value_aug = jnp.concatenate(
                [value_t[head * HEAD_DIM : (head + 1) * HEAD_DIM], ones], axis=0
            )
            parts = []
            for start in range(0, tokens, chunk):
                scores = mm(key_aug, query_aug[start : start + chunk], NT)
                if shifted:
                    scores = scores - jnp.max(scores, axis=0, keepdims=True)
                exponent = jnp.exp(scores).astype(BF16)
                e_ref[head, :, start : start + chunk] = exponent
                mixed = mm(value_aug, exponent, NN)
                total = mixed[HEAD_DIM : HEAD_DIM + 1]
                inverse = 1.0 / total
                rows_ref[pl.ds(step * 2 + head, 1), start : start + chunk] = inverse
                parts.append(mixed[:HEAD_DIM] * inverse)
                sums.append(total)
            outs.append(jnp.concatenate(parts, axis=1))
        ctx_ref[...] = jnp.concatenate(outs, axis=0).T.astype(BF16)
        return jnp.concatenate(sums, axis=1)

    sums = heads(False)
    fits = (jnp.max(sums) <= 2.0**40) & (jnp.min(sums) >= 2.0**-40)

    @pl.when(jnp.logical_not(fits))
    def _():
        heads(True)

    @pl.when(step == pl.num_programs(0) - 1)
    def _():
        inverses = rows_ref[...].T
        high = inverses.astype(BF16).astype(F32)
        low = pltpu.roll(inverses - high, 2 * count, 1)
        rinv_ref[...] = (high + low).astype(BF16)


def attn_forward(bounds, first, count, qkv=None, order=None, x=None, vec=None, weights=(), places=None, layer=0):
    project = places is not None
    if project:
        tokens, features = x.shape
        pairs = features // 128
    else:
        _, pairs, tokens, _ = qkv.shape
    out_shape = [
        jax.ShapeDtypeStruct((2 * count, tokens, tokens), BF16),
        jax.ShapeDtypeStruct((tokens, 128 * count), BF16),
        jax.ShapeDtypeStruct((tokens, 128), BF16),
    ]
    out_specs = [
        pl.BlockSpec((2, tokens, tokens), lambda step: (step, 0, 0)),
        pl.BlockSpec((tokens, 128), lambda step: (0, step)),
        fixed((tokens, 128)),
    ]
    scratch = [VMEM((2, tokens, 128), BF16), VMEM((128, tokens), F32)]
    if project:
        operands = (bounds, order, x, vec, *weights)
        in_specs = [whole(pltpu.SMEM), whole(pltpu.SMEM), fixed(x.shape), fixed(vec.shape)]
        in_specs += [whole(pltpu.HBM)] * len(weights)
        out_shape.append(jax.ShapeDtypeStruct((3, pairs, tokens, 128), BF16))
        out_specs.append(fixed((3, pairs, tokens, 128)))
        scratch += [
            VMEM((3, 4, features // BLOCK // 4, BLOCK, features), BF16),
            pltpu.SemaphoreType.DMA,
        ]
    else:
        operands = (bounds, qkv)
        in_specs = [
            whole(pltpu.SMEM),
            pl.BlockSpec((3, 1, tokens, 128), lambda step: (0, step + first, 0, 0)),
        ]
    return pl.pallas_call(
        functools.partial(attn_forward_body, first, count, places, layer),
        grid=(count,),
        out_shape=tuple(out_shape),
        in_specs=in_specs,
        out_specs=tuple(out_specs),
        scratch_shapes=scratch,
        compiler_params=pltpu.CompilerParams(vmem_limit_bytes=VMEM_LIMIT),
        cost_estimate=cost(14),
        name="attn_forward",
    )(*operands)


def normed(z):
    centered = z - jnp.mean(z, axis=-1, keepdims=True)
    variance = jnp.mean(centered * centered, axis=-1, keepdims=True)
    rstd = lax.rsqrt(variance + 1e-05)
    return centered * rstd, rstd


def norm_back(grad, gain, xhat, rstd):
    scaled = grad * gain
    first = jnp.mean(scaled, axis=-1, keepdims=True)
    second = jnp.mean(scaled * xhat, axis=-1, keepdims=True)
    return rstd * (scaled - first - xhat * second)


GELU_A = 0.7978845608028654
GELU_B = 0.044715


def gelu(hidden, sloped):
    square = hidden * hidden
    tanh = jnp.tanh(hidden * (BF16(GELU_A) + BF16(GELU_A * GELU_B) * square))
    chance = BF16(0.5) + BF16(0.5) * tanh
    active = hidden * chance
    if not sloped:
        return active
    inner = BF16(GELU_A) + BF16(3.0 * GELU_A * GELU_B) * square
    return active, chance + active * (BF16(1.0) - tanh) * inner


def column_sum(ref, row, values):
    ref[row : row + 1] += jnp.sum(values.astype(F32), axis=0, keepdims=True)


def weave(vector_work, matrix_work):
    done = 0
    for index, work in enumerate(vector_work):
        work()
        target = (index + 1) * len(matrix_work) // len(vector_work)
        for matrix in matrix_work[done:target]:
            matrix()
        done = target
    for matrix in matrix_work[done:]:
        matrix()


def ffn_body(mode, layer, places, in_names, out_names, scratch_names, *refs):
    forward, backward, last = mode
    refs = list(refs)
    take = lambda count: [refs.pop(0) for _ in range(count)]
    up_at, (out_stream, out_at), down_at = places
    order_ref, vec_ref = take(2)
    weights = take(8)
    ins = dict(zip(in_names, take(len(in_names))))
    outs = dict(zip(out_names, take(len(out_names))))
    if backward:
        dvec_out, *grads = take(3)
    here = dict(zip(scratch_names, take(len(scratch_names))))
    wo_ref, up_ref, down_ref, sem_w, sem_in, sem_out = take(6)
    assert not refs
    tokens = here["ctx"].shape[0]
    features = vec_ref.shape[2]
    groups = up_ref.shape[0]
    per = features // BLOCK
    wo = lambda: wo_ref[...].reshape(features, features)
    up = lambda j, zs: up_ref[j, zs].reshape(-1, features)
    down = lambda j, part: down_ref[j, part].reshape(-1, features)
    every = slice(None)
    up_halves = [slice(0, 2), slice(2, 4)]
    down_halves = [slice(0, 4), slice(4, 8)]
    wide = features // 2
    half_columns = [slice(0, wide), slice(wide, features)]
    of = lambda j: slice(j * features, (j + 1) * features)
    vec = lambda row: vec_ref[layer, row : row + 1]
    copy_in = {
        name: pltpu.make_async_copy(ref, here[name], sem_in.at[index])
        for index, (name, ref) in enumerate(ins.items())
    }
    sem_of = {name: sem_out.at[index] for index, name in enumerate(outs)}

    def leave(*names, rows=slice(None), columns=None):
        for name in names:
            at = (rows,) if columns is None else (rows, columns)
            if name == "do":
                at = (slice(None), rows)
            pltpu.make_async_copy(
                here[name].at[at], outs[name].at[at], sem_of[name]
            ).start()

    def leave_all():
        for name, ref in outs.items():
            wait_all(here[name], sem_of[name])

    blocks = [slice(start, start + TILE) for start in range(0, tokens, TILE)]
    chunks = [slice(start, start + ROWS) for start in range(0, tokens, ROWS)]

    def fetch_out(ref, low):
        pltpu.make_async_copy(ref.at[out_at], wo_ref.at[:, low], sem_w.at[0]).start()

    def fetch_up(ref, low):
        pltpu.make_async_copy(
            ref.at[pl.ds(up_at, groups)], up_ref.at[:, :, low], sem_w.at[1]
        ).start()

    def fetch_down(ref, low):
        for block in range(groups):
            pltpu.make_async_copy(
                ref.at[down_at + block], down_ref.at[:, low, block], sem_w.at[2]
            ).start()

    early = ("ctx", "x", "y") if forward else ("gm", "gs", "xh2", "stat")
    for name in early:
        copy_in[name].start()
    for fetch in (fetch_out, fetch_up, fetch_down) if forward else (fetch_down, fetch_up, fetch_out):
        stream = {fetch_out: out_stream, fetch_up: 0, fetch_down: 1}[fetch]
        for ref, low in each_part(order_ref, weights, stream):
            fetch(ref, low)
    for name in in_names:
        if name not in early:
            copy_in[name].start()
    waited = set()

    def need(*names):
        for name in names:
            if name not in waited:
                waited.add(name)
                copy_in[name].wait()

    if backward:
        dvec_out[...] = jnp.zeros_like(dvec_out)
    if forward:
        need("ctx", "x", "y")
        wait_all(wo_ref, sem_w.at[0])
        for rows in blocks:
            branch = mm(here["ctx"][rows], wo(), NN) + vec(2)
            xh1, rstd1 = normed(here["x"][rows].astype(F32) + branch)
            m1 = xh1 * vec(3) + vec(4)
            here["m1"][rows] = m1
            here["m1b"][rows] = m1.astype(BF16)
            here["y_new"][rows] = here["y"][rows].astype(F32) + branch
            here["xh1"][rows] = xh1.astype(BF16)
            here["stat"][rows, :64] = jnp.broadcast_to(rstd1, (TILE, 64))
            if not backward:
                leave("xh1", "m1b", rows=rows)
        wait_all(up_ref, sem_w.at[1])

        def hidden_dots(j):
            def piece(rows):
                here["work"][j % 2, rows] = mm(here["m1b"][rows], up(j, every), NN)

            return [functools.partial(piece, rows) for rows in blocks]

        def activate(j):
            def piece(rows):
                hidden = (here["work"][j % 2, rows] + vec(8 + j)).astype(BF16)
                if backward:
                    active, slope = gelu(hidden, True)
                    here["hid"][rows, of(j)] = slope
                else:
                    active = gelu(hidden, False)
                    here["hid"][rows, of(j)] = hidden
                here["act"][rows, of(j)] = active

            return [functools.partial(piece, rows) for rows in chunks]

        def branch_dots(j):
            def piece(rows):
                part = mm(here["act"][rows, of(j)], down(j, every), NN)
                here["sum"][rows] = part + (vec(5) if j == 0 else here["sum"][rows])

            return [functools.partial(piece, rows) for rows in blocks]

        weave([], hidden_dots(0))
        wait_all(down_ref, sem_w.at[2])
        for j in range(groups):
            matrix = hidden_dots(j + 1) if j + 1 < groups else []
            if j > 0:
                matrix = matrix + branch_dots(j - 1)
            weave(activate(j), matrix)
            if not backward:
                leave("hid", columns=of(j))
        weave([], branch_dots(groups - 1))
        if last:
            need("cot")
        for rows in blocks:
            xh2, rstd2 = normed(here["m1"][rows] + here["sum"][rows])
            m2 = xh2 * vec(6) + vec(7)
            y = here["y_new"][rows] + here["sum"][rows]
            if not backward:
                here["xh2"][rows] = xh2.astype(BF16)
                here["stat"][rows, 64:] = jnp.broadcast_to(rstd2, (TILE, 64))
                here["m2"][rows] = m2
                here["m2b"][rows] = m2.astype(BF16)
                here["y_new"][rows] = y
                leave("xh2", "stat", "m2", "m2b", "y_new", rows=rows)
                continue
            yh, rstdy = normed(y)
            here["layer_out"][rows] = (m2 + yh * vec(12) + vec(13)).astype(BF16)
            gm = here["cot"][rows].astype(F32)
            gs = norm_back(gm, vec(12), yh, rstdy)
            here["gs"][rows] = gs
            column_sum(dvec_out, 12, gm * yh)
            column_sum(dvec_out, 13, gm)
            column_sum(dvec_out, 6, gm * xh2)
            column_sum(dvec_out, 7, gm)
            dz2 = norm_back(gm, vec(6), xh2, rstd2)
            df = (dz2 + gs).astype(BF16)
            column_sum(dvec_out, 5, df)
            here["df"][rows] = df
            here["sum"][rows] = dz2
            leave("layer_out", "gs", rows=rows)
        if not backward:
            leave_all()
            return
    else:
        need("gm", "gs", "xh2", "stat")
        for rows in blocks:
            gm = here["gm"][rows]
            xh2 = here["xh2"][rows].astype(F32)
            column_sum(dvec_out, 6, gm * xh2)
            column_sum(dvec_out, 7, gm)
            dz2 = norm_back(gm, vec(6), xh2, here["stat"][rows, 64:65])
            df = (dz2 + here["gs"][rows]).astype(BF16)
            column_sum(dvec_out, 5, df)
            here["df"][rows] = df
            here["sum"][rows] = dz2
        wait_all(down_ref, sem_w.at[2])

    def back_dots(j):
        def piece(rows, columns):
            here["work"][j % 2, :, columns] = mm(here["df"][...], down(j, rows), NT)

        return [functools.partial(piece, *part) for part in zip(down_halves, half_columns)]

    def activate_back(j):
        def piece(rows):
            dactive = here["work"][j % 2, rows].astype(BF16)
            slope = here["hid"][rows, of(j)]
            if not forward:
                active, slope = gelu(slope, True)
                here["act"][rows, of(j)] = active
            dhidden = slope * dactive
            here["hid"][rows, of(j)] = dhidden
            column_sum(dvec_out, 8 + j, dhidden)

        return [functools.partial(piece, rows) for rows in chunks]

    def main_dots(j):
        def piece(rows, columns):
            here["sum"][:, columns] += mm(here["hid"][:, of(j)], up(j, rows), NT)

        return [functools.partial(piece, *part) for part in zip(up_halves, half_columns)]

    gup, gdown, gout = here["gup"], here["gdown"], here["gout"]

    def down_grads(j):
        def piece(index, columns):
            rows = slice(j * features + columns.start, j * features + columns.stop)
            gdown[4 * j + 2 * index : 4 * j + 2 * index + 2] = (
                mm(here["act"][:, rows], here["df"][...], TN)
                .astype(BF16)
                .reshape(2, 2, groups, BLOCK, features)
            )

        return [functools.partial(piece, *part) for part in enumerate(half_columns)]

    def up_grads(j):
        def piece(columns):
            source = slice(j * features + columns.start, j * features + columns.stop)
            gup[16 * j : 16 * j + 16, :, :, columns] = (
                mm(here["m1b"][...], here["hid"][:, source], TN)
                .astype(BF16)
                .reshape(16, 2, BLOCK, wide)
            )

        return [functools.partial(piece, columns) for columns in half_columns]

    weave([], back_dots(0))
    if not forward:
        need("hid")
    for j in range(groups):
        if not forward and j == 1:
            wait_all(up_ref, sem_w.at[1])
        matrix = back_dots(j + 1) if j + 1 < groups else []
        if j > 0:
            matrix = matrix + main_dots(j - 1) + down_grads(j - 1)
        weave(activate_back(j), matrix)
    weave([], main_dots(groups - 1))
    need(*in_names)
    if not forward:
        wait_all(wo_ref, sem_w.at[0])

    lane = lax.broadcasted_iota(jnp.int32, (TILE, 128), 1)
    low_half = lane < HEAD_DIM
    column = lane % HEAD_DIM

    def norm_one(rows):
        gm = here["sum"][rows]
        xh1 = here["xh1"][rows].astype(F32)
        column_sum(dvec_out, 3, gm * xh1)
        column_sum(dvec_out, 4, gm)
        dz1 = norm_back(gm, vec(3), xh1, here["stat"][rows, 0:1])
        here["dz1"][rows] = dz1
        da = (dz1 + here["gs"][rows]).astype(BF16)
        column_sum(dvec_out, 2, da)
        here["da"][rows] = da
        leave("dz1", rows=rows)

    heads = features // HEAD_DIM
    iota = lambda shape, axis: lax.broadcasted_iota(jnp.int32, shape, axis)
    if backward:
        mark = lambda picked: jnp.where(picked, 1.0, 0.0).astype(BF16)
        shape = (features, 128)
        place = mark(iota(shape, 1) % HEAD_DIM // 2 == iota(shape, 0) // HEAD_DIM)
        part = iota((128, 128), 0)
        part = jnp.where(part < 2 * heads, part % heads, heads)
        turn = mark(iota((128, 128), 1) % HEAD_DIM // 2 == part)
        shape = (128, features)
        part = iota(shape, 0)
        part = jnp.where(part < 2 * heads, part % heads, heads)
        share = mark(iota(shape, 1) // HEAD_DIM == part)

    def context_one(rows):
        dctx = mm(here["da"][rows], wo(), NT)
        product = dctx * here["ctx"][rows].astype(F32)
        high = product.astype(BF16)
        low = (product - high.astype(F32)).astype(BF16)
        inverse = here["rinv"][rows]
        dots = -(mm(high, place, NN) + mm(low, place, NN)) * mm(inverse, turn, NN)
        high = dots.astype(BF16).astype(F32)
        extra = jnp.where(column % 2 == 0, high, dots - high).astype(BF16)
        scaled = (dctx * mm(inverse, share, NN)).astype(BF16)
        for at in range(heads):
            pair = slice(at // 2 * 128, at // 2 * 128 + 128)
            inside = low_half if at % 2 == 0 else ~low_half
            here["do"][at, rows] = jnp.where(inside, scaled[:, pair], extra)
        leave("do", rows=rows)

    def send(source, sem):
        for index, ref in enumerate(grads):
            core = order_ref[AT_CORE] if index == 0 else 1 - order_ref[AT_CORE]
            for block, count, part in source(core):
                pltpu.make_async_copy(
                    part, ref.at[pl.ds(16 * block, 16 * count)], sem_w.at[sem]
                ).start()

    matrix = down_grads(groups - 1) + up_grads(0)
    weave([functools.partial(norm_one, rows) for rows in blocks], matrix)
    send(
        lambda core: [
            (groups + 1 + block, 1, gdown.at[:, core, block]) for block in range(groups)
        ],
        2,
    )
    matrix = [piece for j in range(1, groups) for piece in up_grads(j)]
    weave([functools.partial(context_one, rows) for rows in blocks], matrix)
    send(lambda core: [(0, groups, gup.at[:, core])], 1)
    gout[...] = (
        mm(here["ctx"][...], here["da"][...], TN)
        .astype(BF16)
        .reshape(16, 2, BLOCK, features)
    )
    send(lambda core: [(groups, 1, gout.at[:, core])], 0)
    wait_all(gup, sem_w.at[1])
    wait_all(gout, sem_w.at[0])
    wait_all(gdown, sem_w.at[2])
    leave_all()


def ffn_call(forward, backward, last, layer, order, vec, weights, places, ctx, tiled, rinv=None):
    tokens, features = ctx.shape
    groups = 4
    width = groups * features
    per = features // BLOCK
    heads = features // HEAD_DIM
    if forward:
        ins = dict(zip(("ctx", "x", "y", "cot"), (ctx, *tiled)))
    else:
        names = ("ctx", "xh1", "xh2", "stat", "m1b", "hid", "gm", "gs")
        ins = dict(zip(names, (ctx, *tiled)))
    if backward:
        ins["rinv"] = rinv
    square, full = (tokens, features), (tokens, width)
    small = (tokens, 128)
    scratch = {name: (value.shape, value.dtype) for name, value in ins.items()}
    scratch["work"] = ((2, *square), F32)
    scratch["sum"] = (square, F32)
    scratch["act"] = (full, BF16)
    if forward:
        scratch.update(
            m1=(square, F32), m1b=(square, BF16), y_new=(square, F32), xh1=(square, BF16),
            stat=(small, F32), hid=(full, BF16),
        )
    if last:
        scratch.update(layer_out=(square, BF16), gs=(square, F32))
    if forward and not backward:
        scratch.update(xh2=(square, BF16), m2=(square, F32), m2b=(square, BF16))
        out_names = ["xh1", "xh2", "stat", "m1b", "hid", "m2", "m2b", "y_new"]
    else:
        scratch.update(
            df=(square, BF16), dz1=(square, F32), da=(square, BF16), do=((heads, *small), BF16),
            gup=((16 * groups, 2, BLOCK, features), BF16),
            gdown=((16, 2, groups, BLOCK, features), BF16),
            gout=((16, 2, BLOCK, features), BF16),
        )
        out_names = (["layer_out", "gs"] if last else []) + ["dz1", "do"]
    out_shape = [jax.ShapeDtypeStruct(*scratch[name]) for name in out_names]
    out_specs = [whole(ANY)] * len(out_names)
    if backward:
        half = jax.ShapeDtypeStruct((16 * (2 * groups + 1), BLOCK, features), BF16)
        out_shape += [jax.ShapeDtypeStruct((16, features), F32), half, half]
        out_specs += [whole(), whole(ANY), whole(ANY)]
    return pl.pallas_call(
        functools.partial(
            ffn_body, (forward, backward, last), layer, places, tuple(ins), tuple(out_names),
            tuple(scratch),
        ),
        out_shape=tuple(out_shape),
        in_specs=[whole(pltpu.SMEM), whole()] + [whole(pltpu.HBM)] * (8 + len(ins)),
        out_specs=tuple(out_specs),
        scratch_shapes=[VMEM(*kind) for kind in scratch.values()]
        + [
            VMEM((4, 8, BLOCK, features), BF16),
            VMEM((groups, 4, 8, BLOCK, features), BF16),
            VMEM((4, 8, groups, BLOCK, features), BF16),
            pltpu.SemaphoreType.DMA((3,)),
            pltpu.SemaphoreType.DMA((len(ins),)),
            pltpu.SemaphoreType.DMA((len(out_names),)),
        ],
        compiler_params=pltpu.CompilerParams(vmem_limit_bytes=VMEM_LIMIT),
        cost_estimate=cost(6 * forward + 12 * backward),
        name="ffn_" + ("f" if forward else "") + ("b" if backward else ""),
    )(order, vec, *weights, *ins.values())


def attn_backward_body(
    first,
    count,
    places,
    whole_step,
    order_ref,
    e_ref,
    do_ref,
    qkv_ref,
    x_ref,
    gm_ref,
    *refs,
):
    if whole_step:
        weights, refs = refs[:8], refs[8:]
        gm_out, dvec_out, *grads, w_ref, dqkv_s, ds_s, g_s, sem, sem_g = refs
    else:
        dqkv_s, dvec_out, *grads, ds_s, g_s, sem_g = refs
    step = pl.program_id(0)
    tokens, features = x_ref.shape
    lane = lax.broadcasted_iota(jnp.int32, (tokens, 128), 1)
    low_half = lane < HEAD_DIM
    column = lane % HEAD_DIM
    width = 128 * count

    if whole_step:

        @pl.when(step == 0)
        def _():
            fetch_attn(order_ref, weights, places, w_ref, sem, pl.ds(first * 128, width))

    query = qkv_ref[0, 0]
    key_t = qkv_ref[1, 0].T
    value = qkv_ref[2, 0]
    chunk = CHUNK
    dquery, dkey, dvalue = [], [], []
    for head in range(2):
        inside = low_half if head == 0 else ~low_half
        ones = jnp.where(column // 2 == 2 * (step + first) + head, 1.0, 0.0).astype(BF16)
        value_aug = jnp.where(inside, value, ones)
        key_head = key_t[head * HEAD_DIM : (head + 1) * HEAD_DIM]
        parts = []
        for start in range(0, tokens, chunk):
            columns = slice(start, start + chunk)
            dchances = mm(value_aug, do_ref[head, columns], NT)
            dscores = (e_ref[head, :, columns].astype(F32) * dchances).astype(BF16)
            ds_s[head, :, columns] = dscores
            parts.append(mm(key_head, dscores, NN))
        dquery.append(jnp.concatenate(parts, axis=1))
        dkey.append(mm(ds_s[head], query, NN))
        dvalue.append(mm(e_ref[head], do_ref[head], NN))
    here = pl.ds(pl.multiple_of(step * 128, 128), 128)
    dqkv_s[0, :, here] = (jnp.concatenate(dquery, axis=0).T * 0.125).astype(BF16)
    dqkv_s[1, :, here] = jnp.where(low_half, dkey[0], dkey[1]).astype(BF16)
    dqkv_s[2, :, here] = jnp.where(low_half, dvalue[0], dvalue[1]).astype(BF16)

    @pl.when(step == count - 1)
    def _():
        x = x_ref[...]
        for part in range(3):
            g_s[16 * part : 16 * part + 16] = (
                mm(x, dqkv_s[part], TN).astype(BF16).reshape((16, 2, BLOCK, width))
            )
        for index, ref in enumerate(grads):
            core = order_ref[AT_CORE] if index == 0 else 1 - order_ref[AT_CORE]
            pltpu.make_async_copy(g_s.at[:, core], ref, sem_g).start()
        if whole_step:
            wait_all(w_ref, sem)
            gm = gm_ref[...]
            for part in range(3):
                gm = gm + mm(dqkv_s[part], w_ref[part].reshape(features, width), NT)
            gm_out[...] = gm
        dvec_out[...] = jnp.zeros_like(dvec_out)
        column_sum(dvec_out, 0, dqkv_s[0])
        column_sum(dvec_out, 1, dqkv_s[2])
        wait_all(g_s, sem_g)


def attn_backward(order, first, count, e, e_first, do, qkv, x, gm, weights, places):
    tokens, features = x.shape
    width = 128 * count
    half = jax.ShapeDtypeStruct((16 * 3, BLOCK, width), BF16)
    whole_step = weights is not None
    operands = [order, e, do, qkv, x] + ([gm, *weights] if whole_step else [x])
    in_specs = [
        whole(pltpu.SMEM),
        pl.BlockSpec((2, tokens, tokens), lambda step: (step + e_first, 0, 0)),
        pl.BlockSpec((2, tokens, 128), lambda step: (step + first, 0, 0)),
        pl.BlockSpec((3, 1, tokens, 128), lambda step: (0, step + first, 0, 0)),
        fixed(x.shape),
    ]
    scratch = [
        VMEM((2, tokens, tokens), BF16),
        VMEM((16 * 3, 2, BLOCK, width), BF16),
    ]
    if whole_step:
        in_specs += [fixed(gm.shape)] + [whole(pltpu.HBM)] * len(weights)
        result = jax.ShapeDtypeStruct((tokens, features), F32)
        scratch = [VMEM((3, 4, 8, BLOCK, width), BF16), VMEM((3, tokens, width), BF16)] + scratch
        scratch.append(pltpu.SemaphoreType.DMA)
    else:
        in_specs.append(whole(ANY))
        result = jax.ShapeDtypeStruct((3, tokens, width), BF16)
    return pl.pallas_call(
        functools.partial(attn_backward_body, first, count, places, whole_step),
        grid=(count,),
        out_shape=(result, jax.ShapeDtypeStruct((8, width), F32), half, half),
        in_specs=in_specs,
        out_specs=(fixed(result.shape), fixed((8, width))) + (whole(ANY),) * 2,
        scratch_shapes=scratch + [pltpu.SemaphoreType.DMA],
        compiler_params=pltpu.CompilerParams(vmem_limit_bytes=VMEM_LIMIT),
        cost_estimate=cost(26),
        name="attn_backward",
    )(*operands)


def input_gradient(order, dqkv, dz, weights, places):
    tokens, features = dz.shape
    tile = tokens // 4

    def body(order_ref, dqkv_ref, dz_ref, *refs):
        parts, (out, w_ref, sem) = refs[:8], refs[8:]

        @pl.when(pl.program_id(0) == 0)
        def _():
            fetch_attn(order_ref, parts, places, w_ref, sem, pl.ds(0, features))
            wait_all(w_ref, sem)

        total = dz_ref[...]
        for part in range(3):
            total = total + mm(dqkv_ref[part], w_ref[part].reshape(features, features), NT)
        out[...] = total

    return pl.pallas_call(
        body,
        grid=(4,),
        out_shape=jax.ShapeDtypeStruct((tokens, features), F32),
        in_specs=[
            whole(pltpu.SMEM),
            pl.BlockSpec((3, tile, features), lambda step: (0, step, 0)),
            rows_of(tile, features),
        ]
        + [whole(pltpu.HBM)] * len(weights),
        out_specs=rows_of(tile, features),
        scratch_shapes=[
            VMEM((3, 4, 8, BLOCK, features), BF16),
            pltpu.SemaphoreType.DMA,
        ],
        compiler_params=pltpu.CompilerParams(vmem_limit_bytes=VMEM_LIMIT),
        cost_estimate=cost(4),
        name="input_gradient",
    )(order, dqkv, dz, *weights)


def blocks_of(matrix, features):
    rows, columns = matrix.shape
    shaped = matrix.reshape(rows // BLOCK, BLOCK, columns // features, features)
    return shaped.transpose(0, 2, 1, 3)


def matrix_of(blocks):
    rows, columns, block, features = blocks.shape
    return blocks.transpose(0, 2, 1, 3).reshape(rows * block, columns * features)


CORE, X, Y, Z = 1, 2, 4, 8
Z_MASKS = (0, Z, 2 * Z, 3 * Z)
PLANE_MASKS = (0, X, Y, X | Y)
LOW_MASKS = [
    core | second | first
    for high, low in ((X, Y), (Y, X))
    for core in (0, CORE)
    for second in (0, high)
    for first in (0, low)
]


def swap(part, mask):
    return lax.ppermute(part, AXES, [(device, device ^ mask) for device in range(32)])


def after(value, *earlier):
    return lax.optimization_barrier((value, earlier))[0]


def prepare(place, in_w, out_w, up_w, down_w, vectors, final_norm):
    _, block, features = out_w.shape
    groups = up_w.shape[2] // features
    width, spread = vectors.shape[1], final_norm.shape[0]

    def body(place_ref, in_ref, out_ref, up_ref, down_ref, vec_ref, last_ref, *refs):
        own, rows = refs[:3], refs[3]
        rows[...] = jnp.zeros_like(rows)
        rows[0:2, :width] = vec_ref[...].astype(F32)
        rows[8:9, :spread] = last_ref[...].astype(F32)
        field = rows[0:8, :256]
        field = jnp.where(place_ref[AT_FIELDS] == 0, field, pltpu.roll(field, 64, 1))
        last = rows[8:16, :128]
        chosen = last
        for turn in range(1, 128 // spread):
            turned = pltpu.roll(last, turn * spread, 1)
            chosen = jnp.where(place_ref[AT_FIELDS + 1] == turn * spread, turned, chosen)
        rows[...] = jnp.zeros_like(rows)
        rows[0:1, :256] = field[0:1]
        rows[0:1, 256:512] = field[1:2]
        rows[1:2, :128] = chosen[0:1]
        parts = lambda ref, layer, count: [
            ref[layer, :, features * j : features * (j + 1)] for j in range(count)
        ]
        qkv = [parts(in_ref, layer, 3) for layer in range(2)]
        up = [parts(up_ref, layer, groups) for layer in range(2)]
        down = [
            [down_ref[layer, block * j : block * (j + 1)] for j in range(groups)]
            for layer in range(2)
        ]
        out = [out_ref[layer] for layer in range(2)]
        laid = [
            qkv[0] + [rows[...].astype(BF16)],
            qkv[1][:2] + up[0] + qkv[1][2:] + [out[0]] + down[0],
            up[1] + [out[1]] + down[1],
        ]
        for ref, pieces in zip(own, laid):
            for index, piece in enumerate(pieces):
                ref[index] = piece

    outs = [(count, block, features) for count in (4, 2 * groups + 4, 2 * groups + 1)]
    operands = (in_w, out_w, up_w, down_w, vectors, final_norm[None])
    return pl.pallas_call(
        body,
        grid=(1,),
        out_shape=tuple(jax.ShapeDtypeStruct(shape, BF16) for shape in outs),
        in_specs=[whole(pltpu.SMEM)] + [fixed(part.shape) for part in operands],
        out_specs=tuple(fixed(shape) for shape in outs),
        scratch_shapes=[VMEM((block, features), F32)],
        compiler_params=pltpu.CompilerParams(vmem_limit_bytes=VMEM_LIMIT),
        name="prepare",
    )(place, *operands)


def gather_z(own):
    return [own] + [swap(own, mask) for mask in Z_MASKS[1:]]


def pack_z(place, pieces):
    blocks, *rest = pieces[0].shape

    def body(place_ref, *refs):
        for index in range(4):
            refs[4][:, place_ref[AT_Z] ^ index] = refs[index][...]

    return pl.pallas_call(
        body,
        out_shape=jax.ShapeDtypeStruct((blocks, 4, *rest), BF16),
        in_specs=[whole(pltpu.SMEM)] + [whole()] * 4,
        out_specs=whole(),
        compiler_params=pltpu.CompilerParams(vmem_limit_bytes=SMALL_VMEM),
        name="pack_z",
    )(place, *pieces)


def gather_first(four, cut):
    streams = (four[:cut], Y, X), (four[cut:], X, Y)
    return [(part, swap(part, first), second) for part, first, second in streams]


def gather_second(streams, near):
    return [swap(part, second) for part, (_, _, second) in zip(near, streams)]


def join_two(streams):
    def body(a_ref, b_ref, c_ref, d_ref, out0, out1):
        out0[0], out0[1] = a_ref[...], b_ref[...]
        out1[0], out1[1] = c_ref[...], d_ref[...]

    parts = [part for near, far, _ in streams for part in (near, far)]
    shapes = [(2, *parts[0].shape), (2, *parts[2].shape)]
    return pl.pallas_call(
        body,
        out_shape=tuple(jax.ShapeDtypeStruct(shape, BF16) for shape in shapes),
        in_specs=[whole()] * 4,
        out_specs=(whole(), whole()),
        compiler_params=pltpu.CompilerParams(vmem_limit_bytes=SMALL_VMEM),
        name="join_two",
    )(*parts)


def gather_core(near, far, late):
    near = after(near, far) if late else near
    return [
        part
        for pair in zip(near, far)
        for part in (*pair, *[swap(half, CORE) for half in pair])
    ]


def sum_core(mine, other):
    return hold(mine), swap(other, CORE)


def hold(part):
    def body(in_ref, out_ref, sem):
        copy = pltpu.make_async_copy(in_ref, out_ref, sem)
        copy.start()
        copy.wait()

    return pl.pallas_call(
        body,
        out_shape=jax.ShapeDtypeStruct(part.shape, part.dtype),
        in_specs=[whole(pltpu.HBM)],
        out_specs=whole(),
        scratch_shapes=[pltpu.SemaphoreType.DMA],
        compiler_params=pltpu.CompilerParams(vmem_limit_bytes=SMALL_VMEM),
        cost_estimate=cost(1),
        name="hold",
    )(part)


def sum_plane(place, pairs):
    pairs = [[part.reshape(-1, 4, 4, *part.shape[1:]) for part in pair] for pair in pairs]
    kept, got = zip(*pairs)
    rest = kept[0].shape[3:]
    sizes = [part.shape[0] for part in kept]

    def body(place_ref, *refs):
        outs = refs[2 * len(sizes) :]
        start = 0
        for index, size in enumerate(sizes):
            left, right = refs[index], refs[len(sizes) + index]
            for mask, out in enumerate(outs):
                plane = place_ref[AT_PLANE] ^ mask
                out[start : start + size] = (
                    left[:, :, plane].astype(F32) + right[:, :, plane].astype(F32)
                ).astype(BF16)
            start += size

    return pl.pallas_call(
        body,
        out_shape=(jax.ShapeDtypeStruct((sum(sizes), 4, *rest), BF16),) * 4,
        in_specs=[whole(pltpu.SMEM)] + [whole()] * (2 * len(sizes)),
        out_specs=(whole(),) * 4,
        compiler_params=pltpu.CompilerParams(vmem_limit_bytes=SMALL_VMEM),
        name="sum_plane",
    )(place, *kept, *got)


def send_plane(parts):
    return [parts[0]] + [swap(part, mask) for part, mask in zip(parts[1:], PLANE_MASKS[1:])]


def sum_z(place, parts):
    blocks, _, *rest = parts[0].shape
    count = 3 if blocks % 3 == 0 else 1

    def body(place_ref, *refs):
        for mask in range(4):
            z = place_ref[AT_Z] ^ mask
            total = refs[0][:, z].astype(F32)
            for ref in refs[1:4]:
                total = total + ref[:, z].astype(F32)
            refs[4 + mask][...] = total.astype(BF16)

    return pl.pallas_call(
        body,
        grid=(blocks // count,),
        out_shape=(jax.ShapeDtypeStruct((blocks, *rest), BF16),) * 4,
        in_specs=[whole(pltpu.SMEM)]
        + [pl.BlockSpec((count, 4, *rest), lambda step: (step, 0, 0, 0))] * 4,
        out_specs=(pl.BlockSpec((count, *rest), lambda step: (step, 0, 0)),) * 4,
        compiler_params=pltpu.CompilerParams(vmem_limit_bytes=SMALL_VMEM),
        name="sum_z",
    )(place, *parts)


def send_z(pieces):
    return [pieces[0]] + [swap(piece, mask) for piece, mask in zip(pieces[1:], Z_MASKS[1:])]


def finish(place, ffn1, ffn0, attn0, width, spread):
    _, block, features = ffn1[0].shape
    groups = (ffn1[0].shape[0] - 1) // 2

    def body(place_ref, *refs):
        parts = [refs[:4], refs[4:8], refs[8:12]]
        in_out, out_out, up_out, down_out, vec_out, last_out = refs[12:]

        def total(part, index):
            value = parts[part][0][index].astype(F32)
            for ref in parts[part][1:]:
                value = value + ref[index].astype(F32)
            return value

        for layer, part in ((1, 0), (0, 1)):
            for j in range(groups):
                up_out[layer, :, features * j : features * (j + 1)] = total(part, j)
                down_out[layer, block * j : block * (j + 1)] = total(part, groups + 1 + j)
            out_out[layer] = total(part, groups)
        for layer, part, start in ((1, 1, 2 * groups + 1), (0, 2, 0)):
            for j in range(3):
                in_out[layer, :, features * j : features * (j + 1)] = total(part, start + j)
        rows = total(2, 3)
        for layer in range(2):
            field = rows[0:8, 256 * layer : 256 * layer + 256]
            turned = pltpu.roll(field, 192, 1)
            chosen = jnp.where(place_ref[AT_FIELDS] == 0, field, turned)
            vec_out[layer : layer + 1] = chosen[0:1, :width]
        field = rows[0:8, :128]
        chosen = field
        for turn in range(1, 128 // spread):
            turned = pltpu.roll(field, 128 - turn * spread, 1)
            chosen = jnp.where(place_ref[AT_FIELDS + 1] == turn * spread, turned, chosen)
        last_out[...] = chosen[1:2, :spread]

    shapes = [
        (2, block, 3 * features),
        (2, block, features),
        (2, block, groups * features),
        (2, block * groups, features),
        (2, width),
        (1, spread),
    ]
    return pl.pallas_call(
        body,
        out_shape=tuple(jax.ShapeDtypeStruct(shape, F32) for shape in shapes),
        in_specs=[whole(pltpu.SMEM)] + [whole()] * 12,
        out_specs=tuple(whole() for _ in shapes),
        compiler_params=pltpu.CompilerParams(vmem_limit_bytes=SMALL_VMEM),
        name="finish",
    )(place, *ffn1, *ffn0, *attn0)


def field_of(device, width):
    start = device * width
    return start // 128 * 128, start % 128


def unpack_vectors(order, parts, width, spread):
    def body(order_ref, *refs):
        refs, out, flat, last = refs[:4], *refs[4:]
        flat[...] = jnp.zeros_like(flat)
        last[...] = jnp.zeros_like(last)
        out[...] = jnp.zeros_like(out)
        for index, ref in enumerate(refs):
            for near, z in [(near, z) for near in range(2) for z in range(4)]:
                owner = 8 * z + order_ref[8 + 2 * index + near]
                rows = ref[near, 0, z].astype(F32)
                at = pl.ds(pl.multiple_of(owner * width // 128 * 128, 128), 256)
                for layer in range(2):
                    flat[layer : layer + 1, at] += rows[0:1, 256 * layer : 256 * layer + 256]
                at = pl.ds(pl.multiple_of(owner * spread // 128 * 128, 128), 128)
                last[0:1, at] += rows[1:2, :128]
        for layer in range(2):
            for row in range(12):
                out[layer, row : row + 1] = flat[layer : layer + 1, row * 512 : row * 512 + 512]
            for row in range(2):
                out[layer, 12 + row : 13 + row] = last[0:1, row * 512 : row * 512 + 512]

    features = parts[0].shape[-1]
    at = parts[0].shape[1] - 1
    return pl.pallas_call(
        body,
        grid=(1,),
        out_shape=jax.ShapeDtypeStruct((2, 16, features), F32),
        in_specs=[whole(pltpu.SMEM)]
        + [
            pl.BlockSpec((2, 1, *part.shape[2:]), lambda step: (0, at, 0, 0, 0)) for part in parts
        ],
        out_specs=fixed((2, 16, features)),
        scratch_shapes=[VMEM((8, 12 * features), F32), VMEM((8, 2 * features), F32)],
        compiler_params=pltpu.CompilerParams(vmem_limit_bytes=SMALL_VMEM),
        name="unpack_vectors",
    )(order, *parts)


def pack_vectors(order, attn_rows, ffn_rows, width, spread):
    features = ffn_rows[0].shape[1]

    def body(order_ref, a0, a1, f0, f1, out0, out1, flat, last):
        for layer, (attn, ffn) in enumerate(((a0, f0), (a1, f1))):
            for row in range(12):
                source = attn if row < 2 else ffn
                flat[layer : layer + 1, row * 512 : row * 512 + 512] = source[row : row + 1]
        for row in range(2):
            last[0:1, row * 512 : row * 512 + 512] = f1[12 + row : 13 + row]
        for half, out in enumerate((out0, out1)):
            out[...] = jnp.zeros_like(out)
            core = order_ref[AT_CORE] if half == 0 else 1 - order_ref[AT_CORE]
            for pair in range(16):
                owner = 2 * pair + core
                at = pl.ds(pl.multiple_of(owner * width // 128 * 128, 128), 256)
                fields = [flat[layer : layer + 1, at] for layer in range(2)]
                at = pl.ds(pl.multiple_of(owner * spread // 128 * 128, 128), 128)
                final = jnp.concatenate([last[0:1, at], jnp.zeros((1, 384), F32)], axis=1)
                rows = [jnp.concatenate(fields, axis=1), final, jnp.zeros((BLOCK - 2, 512), F32)]
                out[pair] = jnp.concatenate(rows, axis=0).astype(BF16)

    return pl.pallas_call(
        body,
        out_shape=(jax.ShapeDtypeStruct((16, BLOCK, features), BF16),) * 2,
        in_specs=[whole(pltpu.SMEM)] + [whole()] * 4,
        out_specs=(whole(), whole()),
        scratch_shapes=[VMEM((8, 12 * features), F32), VMEM((8, 2 * features), F32)],
        compiler_params=pltpu.CompilerParams(vmem_limit_bytes=SMALL_VMEM),
        name="pack_vectors",
    )(order, *attn_rows, *ffn_rows)


def total_of(pieces):
    total = pieces[0].astype(F32)
    for piece in pieces[1:]:
        total = total + piece.astype(F32)
    return total


def local(
    main_residual,
    side_residual,
    cotangent,
    lengths,
    input_weight,
    output_weight,
    expand_weight,
    reduce_weight,
    vectors,
    final_norm,
):
    tokens, features = main_residual.shape
    layers = input_weight.shape[0]
    assert lengths.shape[0] == 1 and layers == 2
    per = features // BLOCK
    pairs = features // 128
    half_pairs = pairs // 2
    groups = expand_weight.shape[2] // features
    fast = lax.axis_size(AXES) == 32 and per == 32
    ffn_at = ((2, (1, 1), 2), (0, (0, groups), 0))
    width = vectors.shape[1]
    spread = final_norm.shape[0]

    def vec_rows(all_vectors, final_full):
        return jnp.concatenate(
            [
                all_vectors.reshape(layers, 12, features),
                jnp.broadcast_to(final_full.reshape(1, 2, features), (layers, 2, features)),
                jnp.zeros((layers, 2, features), F32),
            ],
            axis=1,
        )

    if fast:
        me = lax.axis_index(AXES)
        table = [
            [(device ^ mask) & 7 for mask in LOW_MASKS]
            + [device // Z, device // X & 3, device & CORE]
            + [field_of(device, width)[1], field_of(device, spread)[1]]
            for device in range(32)
        ]
        order = jnp.array(table, jnp.int32)[me]
        own = prepare(
            order, input_weight, output_weight, expand_weight, reduce_weight, vectors, final_norm
        )
        z0 = gather_z(own[0])
        z1 = gather_z(after(own[1], z0[1:]))
        two = gather_first(pack_z(order, z0), 2)
        near = join_two(two)
        attn0 = gather_core(near, gather_second(two, near), True)
        vec = unpack_vectors(order, attn0[4:], width, spread)
        two = gather_first(pack_z(order, after(z1, near)), groups + 2)
        z2 = gather_z(after(own[2], attn0))
        near = join_two(two)
        far = gather_second(two, near)
        x0 = after(main_residual, near)
    else:
        gather = lambda part, axis: lax.all_gather(part, AXES, axis=axis, tiled=True)
        order = jnp.array(LOW_MASKS + [0] * 5, jnp.int32)

        def streams(*two):
            parts = []
            for stream, blocks in enumerate(two):
                joined = jnp.concatenate(blocks, axis=1)
                joined = joined.reshape(4, 8, *joined.shape[1:]).transpose(1, 2, 0, 3, 4)
                lows = LOW_MASKS[8 * stream : 8 * stream + 8]
                parts += [joined[jnp.array(lows[at : at + 2])] for at in range(0, 8, 2)]
            return parts

        vec = vec_rows(gather(vectors, 1).astype(F32), gather(final_norm, 0).astype(F32))
        parts = []
        for layer in range(layers):
            qkv = blocks_of(gather(input_weight[layer], 0), features)
            up = blocks_of(gather(expand_weight[layer], 0), features)
            out = blocks_of(gather(output_weight[layer], 0), features)
            down = gather(reduce_weight[layer], 0).reshape(per, -1, BLOCK, features)
            parts.append((qkv, up, out, down))
        (qkv0, up0, out0, down0), (qkv1, up1, out1, down1) = parts
        attn0 = streams([qkv0[:, :2]], [qkv0[:, 2:]])
        mixed = streams([qkv1[:, :2], up0], [qkv1[:, 2:], out0, down0])
        ffn1 = streams([up1, out1], [down1])
        x0 = main_residual

    e0, ctx0, rinv0, qkv0 = attn_forward(
        lengths, 0, pairs, None, order, x0, vec, attn0, 0, 0
    )
    x0 = main_residual
    if fast:
        far, z2 = after((far, z2), e0)
        mixed = gather_core(near, far, True)
        two = gather_first(pack_z(order, z2), groups + 1)
        x0 = after(x0, *[part for part, _, _ in two])
    xh1, xh2, stat, m1b, hid, m2, m2b, y = ffn_call(
        True, False, False, 0, order, vec, mixed, ffn_at[0], ctx0, (x0, side_residual)
    )
    x1 = m2b
    if fast:
        two = [(part, after(got, m2b), mask) for part, got, mask in two]
        near = join_two(two)
        x1 = after(m2b, near)
        far = gather_second(two, near)
    e1, ctx1, rinv1, qkv1 = attn_forward(
        lengths, 0, pairs, None, order, x1, vec, mixed, 0, 1
    )
    if fast:
        ffn1 = gather_core(near, after(far, e1), False)
    layer_out, grad_side, gm, do, dvec1, *gf1 = ffn_call(
        True, True, True, 1, order, vec, ffn1, ffn_at[1], ctx1, (m2, y, cotangent), rinv1
    )
    if fast:
        f1 = sum_plane(order, [sum_core(*gf1)])
        gm = after(gm, f1)
        f1 = send_plane(f1)
    gm, dvec1a, *gi1 = attn_backward(
        order, 0, pairs, e1, 0, do, qkv1, m2b, gm, mixed, 0
    )
    if fast:
        i1 = sum_core(*gi1)
        f1 = sum_z(order, after(f1, gm))
        gm = after(gm, f1)
        f1 = send_z(f1)
    gm, do, dvec0, *gf0 = ffn_call(
        False, True, False, 0, order, vec, mixed, ffn_at[0], ctx0,
        (xh1, xh2, stat, m1b, hid, gm, grad_side), rinv0,
    )
    if fast:
        f1, i1 = after((f1, i1), gm)
        f0 = sum_plane(order, [sum_core(*after(gf0, f1)), i1])
        do = after(do, f0)
        f0 = send_plane(f0)
    dqkv, dvec0a, *gi0 = attn_backward(
        order, 0, pairs, e0, 0, do, qkv0, main_residual, None, None, 0
    )
    if fast:
        rows = pack_vectors(order, (dvec0a, dvec1a), (dvec0, dvec1), width, spread)
        i0 = sum_plane(order, [sum_core(*gi0), sum_core(*rows)])
        f0 = send_z(sum_z(order, after(f0, dqkv)))
        i0 = send_plane(after(i0, f0[0]))
        gm, dqkv = after((gm, dqkv), f0[0], i0[0])
        grad_main = input_gradient(order, dqkv, gm, attn0, 0)
        i0 = send_z(sum_z(order, after(i0, grad_main)))
        grad_in, grad_out, grad_up, grad_down, grad_vec, grad_final = finish(
            order, f1, f0, i0, width, spread
        )
        grad_final = grad_final[0]
    else:
        grad_main = input_gradient(order, dqkv, gm, attn0, 0)
        scatter = lambda part, axis: lax.psum_scatter(
            part, AXES, scatter_dimension=axis, tiled=True
        ).astype(F32)

        def natural(even, odd):
            joined = jnp.stack([even, odd], axis=1)
            return joined.reshape(-1, per, *even.shape[1:]).swapaxes(0, 1)

        both = lambda make: jnp.stack(
            [make(natural(*i), natural(*f)) for i, f in ((gi0, gf0), (gi1, gf1))]
        )
        grad_in = scatter(both(lambda i, f: matrix_of(i)), 1)
        grad_up = scatter(both(lambda i, f: matrix_of(f[:, :groups])), 1)
        grad_out = scatter(both(lambda i, f: matrix_of(f[:, groups : groups + 1])), 1)
        grad_down = scatter(both(lambda i, f: f[:, groups + 1 :].reshape(-1, features)), 1)
        dvec = [
            jnp.concatenate([first[0:2], rest[2:12]]).reshape(-1)
            for first, rest in ((dvec0a, dvec0), (dvec1a, dvec1))
        ]
        grad_vec = scatter(jnp.stack(dvec), 1)
        grad_final = scatter(dvec1[12:14].reshape(-1), 0)
    return (
        layer_out,
        grad_main,
        grad_side,
        grad_in,
        grad_out,
        grad_up,
        grad_down,
        grad_vec,
        grad_final,
    )


def solution(mesh):
    rows = P(AXES, None)
    middle = P(None, AXES, None)
    return jax.shard_map(
        local,
        mesh=mesh,
        in_specs=(rows, rows, rows, rows, middle, middle, middle, middle, P(None, AXES), P(AXES)),
        out_specs=(rows, rows, rows, middle, middle, middle, middle, P(None, AXES), P(AXES)),
        check_vma=False,
    )
```

```python
import functools

import jax
import jax.numpy as jnp
from jax import lax
from jax.experimental import pallas as pl
from jax.experimental.pallas import tpu as pltpu
from jax.sharding import PartitionSpec as P

HEAD_DIM = 64
AXES = ("wide", "narrow")
F32 = jnp.float32
BF16 = jnp.bfloat16
NN = (((1,), (0,)), ((), ()))
NT = (((1,), (1,)), ((), ()))
TN = (((0,), (0,)), ((), ()))
MASKED = -1000000000.0
VMEM_LIMIT = 60 * 2**20
SMALL_VMEM = 24 * 2**20


def cost(microseconds):
    return pl.CostEstimate(
        flops=microseconds * 10**9, bytes_accessed=microseconds * 10**6, transcendentals=0
    )


BLOCK = 16
CHUNK = 512
TILE = 256
ROWS = 64
VMEM = pltpu.VMEM
ANY = pl.ANY


def mm(left, right, dims):
    return lax.dot_general(left, right, dims, preferred_element_type=F32)


def whole(memory=VMEM):
    return pl.BlockSpec(memory_space=memory)


def fixed(shape):
    zeros = (0,) * len(shape)
    return pl.BlockSpec(shape, lambda step: zeros)


def rows_of(tile, width):
    return pl.BlockSpec((tile, width), lambda step: (step, 0))


AT_Z, AT_PLANE, AT_CORE, AT_FIELDS = 16, 17, 18, 19


def each_part(place_ref, weights, stream):
    return [
        (weights[index].at[near], place_ref[2 * index + near])
        for index in range(4 * stream, 4 * stream + 4)
        for near in range(2)
    ]


def wait_all(ref, sem):
    pltpu.make_async_copy(ref, ref, sem).wait()


def fetch_attn(order_ref, weights, at, w_ref, sem, columns):
    for ref, low in each_part(order_ref, weights, 0):
        pltpu.make_async_copy(
            ref.at[pl.ds(at, 2), :, :, columns], w_ref.at[pl.ds(0, 2), :, low], sem
        ).start()
    for ref, low in each_part(order_ref, weights, 1):
        pltpu.make_async_copy(ref.at[at, :, :, columns], w_ref.at[2, :, low], sem).start()


def project(x, w_ref, vec_ref, layer, part):
    features = x.shape[1]
    packed = mm(x, w_ref[part].reshape(features, features), NN)
    if part == 0:
        return (packed + vec_ref[layer, 0:1]).astype(BF16) * BF16(0.125)
    if part == 2:
        packed = packed + vec_ref[layer, 1:2]
    return packed.astype(BF16)


def attn_forward_body(first, count, places, layer, *refs):
    refs = list(refs)
    take = lambda: refs.pop(0)
    bounds_ref = take()
    if places is not None:
        order_ref, x_ref, vec_ref = take(), take(), take()
        weights = [take() for _ in range(8)]
        e_ref, ctx_ref, rinv_ref, qkv_ref, aux_ref, rows_ref, w_ref, sem = refs
        at = pl.program_id(0) + first
    else:
        qkv_ref, e_ref, ctx_ref, rinv_ref, aux_ref, rows_ref = refs
        at = 0
    step = pl.program_id(0)
    tokens = ctx_ref.shape[0]
    lane = lax.broadcasted_iota(jnp.int32, (tokens, 128), 1)
    low_half = lane < HEAD_DIM

    @pl.when(step == 0)
    def _():
        if places is not None:
            features = x_ref.shape[1]
            fetch_attn(order_ref, weights, places, w_ref, sem, pl.ds(0, features))
        token = lax.broadcasted_iota(jnp.int32, (tokens, 128), 0)
        column = lane % HEAD_DIM
        single = bounds_ref[0, 1] == 0
        quarter = tokens // 4
        segment = jnp.where(single, 0, token // quarter)
        inside = jnp.where(single, token, token % quarter)
        own = column == segment
        bound = jnp.where(
            segment == 0,
            bounds_ref[0, 0],
            jnp.where(
                segment == 1,
                bounds_ref[0, 1],
                jnp.where(segment == 2, bounds_ref[0, 2], bounds_ref[0, 3]),
            ),
        )
        alive = own & (inside < bound)
        aux_ref[0] = jnp.where(own, 1.0, 0.0).astype(BF16)
        aux_ref[1] = jnp.where(alive | (column >= 4), 0.0, MASKED).astype(BF16)
        rows_ref[...] = jnp.zeros_like(rows_ref)
        if places is not None:
            wait_all(w_ref, sem)
            x = x_ref[...]
            for part in range(3):
                packed = project(x, w_ref, vec_ref, layer, part)
                for index in range(features // 128):
                    qkv_ref[part, index] = packed[:, index * 128 : (index + 1) * 128]

    query = qkv_ref[0, at]
    key = qkv_ref[1, at]
    value_t = qkv_ref[2, at].T
    ones = jnp.ones((16, tokens), BF16)
    chunk = CHUNK

    def heads(shifted):
        outs, sums = [], []
        for head in range(2):
            inside_head = low_half if head == 0 else ~low_half
            query_aug = jnp.where(inside_head, query, aux_ref[0])
            key_aug = jnp.where(inside_head, key, aux_ref[1])
            value_aug = jnp.concatenate(
                [value_t[head * HEAD_DIM : (head + 1) * HEAD_DIM], ones], axis=0
            )
            parts = []
            for start in range(0, tokens, chunk):
                scores = mm(key_aug, query_aug[start : start + chunk], NT)
                if shifted:
                    scores = scores - jnp.max(scores, axis=0, keepdims=True)
                exponent = jnp.exp(scores).astype(BF16)
                e_ref[head, :, start : start + chunk] = exponent
                mixed = mm(value_aug, exponent, NN)
                total = mixed[HEAD_DIM : HEAD_DIM + 1]
                inverse = 1.0 / total
                rows_ref[pl.ds(step * 2 + head, 1), start : start + chunk] = inverse
                parts.append(mixed[:HEAD_DIM] * inverse)
                sums.append(total)
            outs.append(jnp.concatenate(parts, axis=1))
        ctx_ref[...] = jnp.concatenate(outs, axis=0).T.astype(BF16)
        return jnp.concatenate(sums, axis=1)

    sums = heads(False)
    fits = (jnp.max(sums) <= 2.0**40) & (jnp.min(sums) >= 2.0**-40)

    @pl.when(jnp.logical_not(fits))
    def _():
        heads(True)

    @pl.when(step == pl.num_programs(0) - 1)
    def _():
        inverses = rows_ref[...].T
        high = inverses.astype(BF16).astype(F32)
        low = pltpu.roll(inverses - high, 2 * count, 1)
        rinv_ref[...] = (high + low).astype(BF16)


def attn_forward(bounds, first, count, qkv=None, order=None, x=None, vec=None, weights=(), places=None, layer=0):
    project = places is not None
    if project:
        tokens, features = x.shape
        pairs = features // 128
    else:
        _, pairs, tokens, _ = qkv.shape
    out_shape = [
        jax.ShapeDtypeStruct((2 * count, tokens, tokens), BF16),
        jax.ShapeDtypeStruct((tokens, 128 * count), BF16),
        jax.ShapeDtypeStruct((tokens, 128), BF16),
    ]
    out_specs = [
        pl.BlockSpec((2, tokens, tokens), lambda step: (step, 0, 0)),
        pl.BlockSpec((tokens, 128), lambda step: (0, step)),
        fixed((tokens, 128)),
    ]
    scratch = [VMEM((2, tokens, 128), BF16), VMEM((128, tokens), F32)]
    if project:
        operands = (bounds, order, x, vec, *weights)
        in_specs = [whole(pltpu.SMEM), whole(pltpu.SMEM), fixed(x.shape), fixed(vec.shape)]
        in_specs += [whole(pltpu.HBM)] * len(weights)
        out_shape.append(jax.ShapeDtypeStruct((3, pairs, tokens, 128), BF16))
        out_specs.append(fixed((3, pairs, tokens, 128)))
        scratch += [
            VMEM((3, 4, features // BLOCK // 4, BLOCK, features), BF16),
            pltpu.SemaphoreType.DMA,
        ]
    else:
        operands = (bounds, qkv)
        in_specs = [
            whole(pltpu.SMEM),
            pl.BlockSpec((3, 1, tokens, 128), lambda step: (0, step + first, 0, 0)),
        ]
    return pl.pallas_call(
        functools.partial(attn_forward_body, first, count, places, layer),
        grid=(count,),
        out_shape=tuple(out_shape),
        in_specs=in_specs,
        out_specs=tuple(out_specs),
        scratch_shapes=scratch,
        compiler_params=pltpu.CompilerParams(vmem_limit_bytes=VMEM_LIMIT),
        cost_estimate=cost(14),
        name="attn_forward",
    )(*operands)


def normed(z):
    centered = z - jnp.mean(z, axis=-1, keepdims=True)
    variance = jnp.mean(centered * centered, axis=-1, keepdims=True)
    rstd = lax.rsqrt(variance + 1e-05)
    return centered * rstd, rstd


def norm_back(grad, gain, xhat, rstd):
    scaled = grad * gain
    first = jnp.mean(scaled, axis=-1, keepdims=True)
    second = jnp.mean(scaled * xhat, axis=-1, keepdims=True)
    return rstd * (scaled - first - xhat * second)


GELU_A = 0.7978845608028654
GELU_B = 0.044715


def gelu(hidden, sloped):
    square = hidden * hidden
    tanh = jnp.tanh(hidden * (BF16(GELU_A) + BF16(GELU_A * GELU_B) * square))
    chance = BF16(0.5) + BF16(0.5) * tanh
    active = hidden * chance
    if not sloped:
        return active
    inner = BF16(GELU_A) + BF16(3.0 * GELU_A * GELU_B) * square
    return active, chance + active * (BF16(1.0) - tanh) * inner


def column_sum(ref, row, values):
    ref[row : row + 1] += jnp.sum(values.astype(F32), axis=0, keepdims=True)


def weave(vector_work, matrix_work):
    done = 0
    for index, work in enumerate(vector_work):
        work()
        target = (index + 1) * len(matrix_work) // len(vector_work)
        for matrix in matrix_work[done:target]:
            matrix()
        done = target
    for matrix in matrix_work[done:]:
        matrix()


def ffn_body(mode, layer, places, in_names, out_names, scratch_names, *refs):
    forward, backward, last = mode
    refs = list(refs)
    take = lambda count: [refs.pop(0) for _ in range(count)]
    up_at, (out_stream, out_at), down_at = places
    order_ref, vec_ref = take(2)
    weights = take(8)
    ins = dict(zip(in_names, take(len(in_names))))
    outs = dict(zip(out_names, take(len(out_names))))
    if backward:
        dvec_out, *grads = take(3)
    here = dict(zip(scratch_names, take(len(scratch_names))))
    wo_ref, up_ref, down_ref, sem_w, sem_in, sem_out = take(6)
    if not backward:
        (next_ref,) = take(1)
    assert not refs
    tokens = here["ctx"].shape[0]
    features = vec_ref.shape[2]
    groups = up_ref.shape[0]
    per = features // BLOCK
    wo = lambda: wo_ref[...].reshape(features, features)
    up = lambda j, zs: up_ref[j, zs].reshape(-1, features)
    down = lambda j, part: down_ref[j, part].reshape(-1, features)
    every = slice(None)
    up_halves = [slice(0, 2), slice(2, 4)]
    down_halves = [slice(0, 4), slice(4, 8)]
    wide = features // 2
    half_columns = [slice(0, wide), slice(wide, features)]
    of = lambda j: slice(j * features, (j + 1) * features)
    vec = lambda row: vec_ref[layer, row : row + 1]
    copy_in = {
        name: pltpu.make_async_copy(ref, here[name], sem_in.at[index])
        for index, (name, ref) in enumerate(ins.items())
    }
    sem_of = {name: sem_out.at[index] for index, name in enumerate(outs)}

    def leave(*names, rows=slice(None), columns=None):
        for name in names:
            at = (rows,) if columns is None else (rows, columns)
            if name == "do":
                at = (slice(None), rows)
            if name == "qkv":
                at = (slice(None), slice(None), rows)
            pltpu.make_async_copy(
                here[name].at[at], outs[name].at[at], sem_of[name]
            ).start()

    def leave_all():
        for name, ref in outs.items():
            wait_all(here[name], sem_of[name])

    blocks = [slice(start, start + TILE) for start in range(0, tokens, TILE)]
    chunks = [slice(start, start + ROWS) for start in range(0, tokens, ROWS)]

    def fetch_out(ref, low):
        pltpu.make_async_copy(ref.at[out_at], wo_ref.at[:, low], sem_w.at[0]).start()

    def fetch_up(ref, low):
        pltpu.make_async_copy(
            ref.at[pl.ds(up_at, groups)], up_ref.at[:, :, low], sem_w.at[1]
        ).start()

    def fetch_down(ref, low):
        for block in range(groups):
            pltpu.make_async_copy(
                ref.at[down_at + block], down_ref.at[:, low, block], sem_w.at[2]
            ).start()

    early = ("ctx", "x", "y") if forward else ("gm", "gs", "xh2", "stat")
    for name in early:
        copy_in[name].start()
    for fetch in (fetch_out, fetch_up, fetch_down) if forward else (fetch_down, fetch_up, fetch_out):
        stream = {fetch_out: out_stream, fetch_up: 0, fetch_down: 1}[fetch]
        for ref, low in each_part(order_ref, weights, stream):
            fetch(ref, low)
    if not backward:
        fetch_attn(order_ref, weights, 0, next_ref, sem_w.at[3], pl.ds(0, features))
    for name in in_names:
        if name not in early:
            copy_in[name].start()
    waited = set()

    def need(*names):
        for name in names:
            if name not in waited:
                waited.add(name)
                copy_in[name].wait()

    if backward:
        dvec_out[...] = jnp.zeros_like(dvec_out)
    if forward:
        need("ctx", "x", "y")
        wait_all(wo_ref, sem_w.at[0])
        for rows in blocks:
            branch = mm(here["ctx"][rows], wo(), NN) + vec(2)
            xh1, rstd1 = normed(here["x"][rows].astype(F32) + branch)
            m1 = xh1 * vec(3) + vec(4)
            here["m1"][rows] = m1
            here["m1b"][rows] = m1.astype(BF16)
            here["y_new"][rows] = here["y"][rows].astype(F32) + branch
            here["xh1"][rows] = xh1.astype(BF16)
            here["stat"][rows, :64] = jnp.broadcast_to(rstd1, (TILE, 64))
            if not backward:
                leave("xh1", "m1b", rows=rows)
        wait_all(up_ref, sem_w.at[1])

        def hidden_dots(j):
            def piece(rows):
                here["work"][j % 2, rows] = mm(here["m1b"][rows], up(j, every), NN)

            return [functools.partial(piece, rows) for rows in blocks]

        def activate(j):
            def piece(rows):
                hidden = (here["work"][j % 2, rows] + vec(8 + j)).astype(BF16)
                if backward:
                    active, slope = gelu(hidden, True)
                    here["hid"][rows, of(j)] = slope
                else:
                    active = gelu(hidden, False)
                    here["hid"][rows, of(j)] = hidden
                here["act"][rows, of(j)] = active

            return [functools.partial(piece, rows) for rows in chunks]

        def branch_dots(j):
            def piece(rows):
                part = mm(here["act"][rows, of(j)], down(j, every), NN)
                here["sum"][rows] = part + (vec(5) if j == 0 else here["sum"][rows])

            return [functools.partial(piece, rows) for rows in blocks]

        weave([], hidden_dots(0))
        wait_all(down_ref, sem_w.at[2])
        for j in range(groups):
            matrix = hidden_dots(j + 1) if j + 1 < groups else []
            if j > 0:
                matrix = matrix + branch_dots(j - 1)
            weave(activate(j), matrix)
            if not backward:
                leave("hid", columns=of(j))
        weave([], branch_dots(groups - 1))
        if last:
            need("cot")
        if not backward:
            wait_all(next_ref, sem_w.at[3])
        for rows in blocks:
            xh2, rstd2 = normed(here["m1"][rows] + here["sum"][rows])
            m2 = xh2 * vec(6) + vec(7)
            y = here["y_new"][rows] + here["sum"][rows]
            if not backward:
                here["xh2"][rows] = xh2.astype(BF16)
                here["stat"][rows, 64:] = jnp.broadcast_to(rstd2, (TILE, 64))
                here["m2"][rows] = m2
                here["m2b"][rows] = m2.astype(BF16)
                here["y_new"][rows] = y
                leave("xh2", "stat", "m2", "m2b", "y_new", rows=rows)
                for part in range(3):
                    packed = project(here["m2b"][rows], next_ref, vec_ref, layer + 1, part)
                    for index in range(features // 128):
                        here["qkv"][part, index, rows] = packed[
                            :, index * 128 : (index + 1) * 128
                        ]
                leave("qkv", rows=rows)
                continue
            yh, rstdy = normed(y)
            here["layer_out"][rows] = (m2 + yh * vec(12) + vec(13)).astype(BF16)
            gm = here["cot"][rows].astype(F32)
            gs = norm_back(gm, vec(12), yh, rstdy)
            here["gs"][rows] = gs
            column_sum(dvec_out, 12, gm * yh)
            column_sum(dvec_out, 13, gm)
            column_sum(dvec_out, 6, gm * xh2)
            column_sum(dvec_out, 7, gm)
            dz2 = norm_back(gm, vec(6), xh2, rstd2)
            df = (dz2 + gs).astype(BF16)
            column_sum(dvec_out, 5, df)
            here["df"][rows] = df
            here["sum"][rows] = dz2
            leave("layer_out", "gs", rows=rows)
        if not backward:
            leave_all()
            return
    else:
        need("gm", "gs", "xh2", "stat")
        for rows in blocks:
            gm = here["gm"][rows]
            xh2 = here["xh2"][rows].astype(F32)
            column_sum(dvec_out, 6, gm * xh2)
            column_sum(dvec_out, 7, gm)
            dz2 = norm_back(gm, vec(6), xh2, here["stat"][rows, 64:65])
            df = (dz2 + here["gs"][rows]).astype(BF16)
            column_sum(dvec_out, 5, df)
            here["df"][rows] = df
            here["sum"][rows] = dz2
        wait_all(down_ref, sem_w.at[2])

    def back_dots(j):
        def piece(rows, columns):
            here["work"][j % 2, :, columns] = mm(here["df"][...], down(j, rows), NT)

        return [functools.partial(piece, *part) for part in zip(down_halves, half_columns)]

    def activate_back(j):
        def piece(rows):
            dactive = here["work"][j % 2, rows].astype(BF16)
            slope = here["hid"][rows, of(j)]
            if not forward:
                active, slope = gelu(slope, True)
                here["act"][rows, of(j)] = active
            dhidden = slope * dactive
            here["hid"][rows, of(j)] = dhidden
            column_sum(dvec_out, 8 + j, dhidden)

        return [functools.partial(piece, rows) for rows in chunks]

    def main_dots(j):
        def piece(rows, columns):
            here["sum"][:, columns] += mm(here["hid"][:, of(j)], up(j, rows), NT)

        return [functools.partial(piece, *part) for part in zip(up_halves, half_columns)]

    gup, gdown, gout = here["gup"], here["gdown"], here["gout"]

    def down_grads(j):
        def piece(index, columns):
            rows = slice(j * features + columns.start, j * features + columns.stop)
            gdown[4 * j + 2 * index : 4 * j + 2 * index + 2] = (
                mm(here["act"][:, rows], here["df"][...], TN)
                .astype(BF16)
                .reshape(2, 2, groups, BLOCK, features)
            )

        return [functools.partial(piece, *part) for part in enumerate(half_columns)]

    def up_grads(j):
        def piece(columns):
            source = slice(j * features + columns.start, j * features + columns.stop)
            gup[16 * j : 16 * j + 16, :, :, columns] = (
                mm(here["m1b"][...], here["hid"][:, source], TN)
                .astype(BF16)
                .reshape(16, 2, BLOCK, wide)
            )

        return [functools.partial(piece, columns) for columns in half_columns]

    weave([], back_dots(0))
    if not forward:
        need("hid")
    for j in range(groups):
        if not forward and j == 1:
            wait_all(up_ref, sem_w.at[1])
        matrix = back_dots(j + 1) if j + 1 < groups else []
        if j > 0:
            matrix = matrix + main_dots(j - 1) + down_grads(j - 1)
        weave(activate_back(j), matrix)
    weave([], main_dots(groups - 1))
    need(*in_names)
    if not forward:
        wait_all(wo_ref, sem_w.at[0])

    lane = lax.broadcasted_iota(jnp.int32, (TILE, 128), 1)
    low_half = lane < HEAD_DIM
    column = lane % HEAD_DIM

    def norm_one(rows):
        gm = here["sum"][rows]
        xh1 = here["xh1"][rows].astype(F32)
        column_sum(dvec_out, 3, gm * xh1)
        column_sum(dvec_out, 4, gm)
        dz1 = norm_back(gm, vec(3), xh1, here["stat"][rows, 0:1])
        here["dz1"][rows] = dz1
        da = (dz1 + here["gs"][rows]).astype(BF16)
        column_sum(dvec_out, 2, da)
        here["da"][rows] = da
        leave("dz1", rows=rows)

    heads = features // HEAD_DIM
    iota = lambda shape, axis: lax.broadcasted_iota(jnp.int32, shape, axis)
    if backward:
        mark = lambda picked: jnp.where(picked, 1.0, 0.0).astype(BF16)
        shape = (features, 128)
        place = mark(iota(shape, 1) % HEAD_DIM // 2 == iota(shape, 0) // HEAD_DIM)
        part = iota((128, 128), 0)
        part = jnp.where(part < 2 * heads, part % heads, heads)
        turn = mark(iota((128, 128), 1) % HEAD_DIM // 2 == part)
        shape = (128, features)
        part = iota(shape, 0)
        part = jnp.where(part < 2 * heads, part % heads, heads)
        share = mark(iota(shape, 1) // HEAD_DIM == part)

    def context_one(rows):
        dctx = mm(here["da"][rows], wo(), NT)
        product = dctx * here["ctx"][rows].astype(F32)
        high = product.astype(BF16)
        low = (product - high.astype(F32)).astype(BF16)
        inverse = here["rinv"][rows]
        dots = -(mm(high, place, NN) + mm(low, place, NN)) * mm(inverse, turn, NN)
        high = dots.astype(BF16).astype(F32)
        extra = jnp.where(column % 2 == 0, high, dots - high).astype(BF16)
        scaled = (dctx * mm(inverse, share, NN)).astype(BF16)
        for at in range(heads):
            pair = slice(at // 2 * 128, at // 2 * 128 + 128)
            inside = low_half if at % 2 == 0 else ~low_half
            here["do"][at, rows] = jnp.where(inside, scaled[:, pair], extra)
        leave("do", rows=rows)

    def send(source, sem):
        for index, ref in enumerate(grads):
            core = order_ref[AT_CORE] if index == 0 else 1 - order_ref[AT_CORE]
            for block, count, part in source(core):
                pltpu.make_async_copy(
                    part, ref.at[pl.ds(16 * block, 16 * count)], sem_w.at[sem]
                ).start()

    matrix = down_grads(groups - 1) + up_grads(0)
    weave([functools.partial(norm_one, rows) for rows in blocks], matrix)
    send(
        lambda core: [
            (groups + 1 + block, 1, gdown.at[:, core, block]) for block in range(groups)
        ],
        2,
    )
    matrix = [piece for j in range(1, groups) for piece in up_grads(j)]
    weave([functools.partial(context_one, rows) for rows in blocks], matrix)
    send(lambda core: [(0, groups, gup.at[:, core])], 1)
    gout[...] = (
        mm(here["ctx"][...], here["da"][...], TN)
        .astype(BF16)
        .reshape(16, 2, BLOCK, features)
    )
    send(lambda core: [(groups, 1, gout.at[:, core])], 0)
    wait_all(gup, sem_w.at[1])
    wait_all(gout, sem_w.at[0])
    wait_all(gdown, sem_w.at[2])
    leave_all()


def ffn_call(forward, backward, last, layer, order, vec, weights, places, ctx, tiled, rinv=None):
    tokens, features = ctx.shape
    groups = 4
    width = groups * features
    per = features // BLOCK
    heads = features // HEAD_DIM
    if forward:
        ins = dict(zip(("ctx", "x", "y", "cot"), (ctx, *tiled)))
    else:
        names = ("ctx", "xh1", "xh2", "stat", "m1b", "hid", "gm", "gs")
        ins = dict(zip(names, (ctx, *tiled)))
    if backward:
        ins["rinv"] = rinv
    square, full = (tokens, features), (tokens, width)
    small = (tokens, 128)
    scratch = {name: (value.shape, value.dtype) for name, value in ins.items()}
    scratch["work"] = ((2, *square), F32)
    scratch["sum"] = (square, F32)
    scratch["act"] = (full, BF16)
    if forward:
        scratch.update(
            m1=(square, F32), m1b=(square, BF16), y_new=(square, F32), xh1=(square, BF16),
            stat=(small, F32), hid=(full, BF16),
        )
    if last:
        scratch.update(layer_out=(square, BF16), gs=(square, F32))
    if forward and not backward:
        scratch.update(
            xh2=(square, BF16), m2=(square, F32), m2b=(square, BF16),
            qkv=((3, features // 128, *small), BF16),
        )
        out_names = ["xh1", "xh2", "stat", "m1b", "hid", "m2", "m2b", "y_new", "qkv"]
    else:
        scratch.update(
            df=(square, BF16), dz1=(square, F32), da=(square, BF16), do=((heads, *small), BF16),
            gup=((16 * groups, 2, BLOCK, features), BF16),
            gdown=((16, 2, groups, BLOCK, features), BF16),
            gout=((16, 2, BLOCK, features), BF16),
        )
        out_names = (["layer_out", "gs"] if last else []) + ["dz1", "do"]
    out_shape = [jax.ShapeDtypeStruct(*scratch[name]) for name in out_names]
    out_specs = [whole(ANY)] * len(out_names)
    if backward:
        half = jax.ShapeDtypeStruct((16 * (2 * groups + 1), BLOCK, features), BF16)
        out_shape += [jax.ShapeDtypeStruct((16, features), F32), half, half]
        out_specs += [whole(), whole(ANY), whole(ANY)]
    return pl.pallas_call(
        functools.partial(
            ffn_body, (forward, backward, last), layer, places, tuple(ins), tuple(out_names),
            tuple(scratch),
        ),
        out_shape=tuple(out_shape),
        in_specs=[whole(pltpu.SMEM), whole()] + [whole(pltpu.HBM)] * (8 + len(ins)),
        out_specs=tuple(out_specs),
        scratch_shapes=[VMEM(*kind) for kind in scratch.values()]
        + [
            VMEM((4, 8, BLOCK, features), BF16),
            VMEM((groups, 4, 8, BLOCK, features), BF16),
            VMEM((4, 8, groups, BLOCK, features), BF16),
            pltpu.SemaphoreType.DMA((4,)),
            pltpu.SemaphoreType.DMA((len(ins),)),
            pltpu.SemaphoreType.DMA((len(out_names),)),
        ]
        + ([] if backward else [VMEM((3, 4, 8, BLOCK, features), BF16)]),
        compiler_params=pltpu.CompilerParams(vmem_limit_bytes=VMEM_LIMIT),
        cost_estimate=cost(6 * forward + 12 * backward),
        name="ffn_" + ("f" if forward else "") + ("b" if backward else ""),
    )(order, vec, *weights, *ins.values())


def attn_backward_body(
    first,
    count,
    places,
    whole_step,
    order_ref,
    e_ref,
    do_ref,
    qkv_ref,
    x_ref,
    gm_ref,
    *refs,
):
    if whole_step:
        weights, refs = refs[:8], refs[8:]
        gm_out, dvec_out, *grads, w_ref, dqkv_s, ds_s, g_s, sem, sem_g = refs
    else:
        dqkv_s, dvec_out, *grads, ds_s, g_s, sem_g = refs
    step = pl.program_id(0)
    tokens, features = x_ref.shape
    lane = lax.broadcasted_iota(jnp.int32, (tokens, 128), 1)
    low_half = lane < HEAD_DIM
    column = lane % HEAD_DIM
    width = 128 * count

    if whole_step:

        @pl.when(step == 0)
        def _():
            fetch_attn(order_ref, weights, places, w_ref, sem, pl.ds(first * 128, width))

    query = qkv_ref[0, 0]
    key_t = qkv_ref[1, 0].T
    value = qkv_ref[2, 0]
    chunk = CHUNK
    dquery, dkey, dvalue = [], [], []
    for head in range(2):
        inside = low_half if head == 0 else ~low_half
        ones = jnp.where(column // 2 == 2 * (step + first) + head, 1.0, 0.0).astype(BF16)
        value_aug = jnp.where(inside, value, ones)
        key_head = key_t[head * HEAD_DIM : (head + 1) * HEAD_DIM]
        parts = []
        for start in range(0, tokens, chunk):
            columns = slice(start, start + chunk)
            dchances = mm(value_aug, do_ref[head, columns], NT)
            dscores = (e_ref[head, :, columns].astype(F32) * dchances).astype(BF16)
            ds_s[head, :, columns] = dscores
            parts.append(mm(key_head, dscores, NN))
        dquery.append(jnp.concatenate(parts, axis=1))
        dkey.append(mm(ds_s[head], query, NN))
        dvalue.append(mm(e_ref[head], do_ref[head], NN))
    here = pl.ds(pl.multiple_of(step * 128, 128), 128)
    dqkv_s[0, :, here] = (jnp.concatenate(dquery, axis=0).T * 0.125).astype(BF16)
    dqkv_s[1, :, here] = jnp.where(low_half, dkey[0], dkey[1]).astype(BF16)
    dqkv_s[2, :, here] = jnp.where(low_half, dvalue[0], dvalue[1]).astype(BF16)

    @pl.when(step == count - 1)
    def _():
        x = x_ref[...]
        for part in range(3):
            g_s[16 * part : 16 * part + 16] = (
                mm(x, dqkv_s[part], TN).astype(BF16).reshape((16, 2, BLOCK, width))
            )
        for index, ref in enumerate(grads):
            core = order_ref[AT_CORE] if index == 0 else 1 - order_ref[AT_CORE]
            pltpu.make_async_copy(g_s.at[:, core], ref, sem_g).start()
        if whole_step:
            wait_all(w_ref, sem)
            gm = gm_ref[...]
            for part in range(3):
                gm = gm + mm(dqkv_s[part], w_ref[part].reshape(features, width), NT)
            gm_out[...] = gm
        dvec_out[...] = jnp.zeros_like(dvec_out)
        column_sum(dvec_out, 0, dqkv_s[0])
        column_sum(dvec_out, 1, dqkv_s[2])
        wait_all(g_s, sem_g)


def attn_backward(order, first, count, e, e_first, do, qkv, x, gm, weights, places):
    tokens, features = x.shape
    width = 128 * count
    half = jax.ShapeDtypeStruct((16 * 3, BLOCK, width), BF16)
    whole_step = weights is not None
    operands = [order, e, do, qkv, x] + ([gm, *weights] if whole_step else [x])
    in_specs = [
        whole(pltpu.SMEM),
        pl.BlockSpec((2, tokens, tokens), lambda step: (step + e_first, 0, 0)),
        pl.BlockSpec((2, tokens, 128), lambda step: (step + first, 0, 0)),
        pl.BlockSpec((3, 1, tokens, 128), lambda step: (0, step + first, 0, 0)),
        fixed(x.shape),
    ]
    scratch = [
        VMEM((2, tokens, tokens), BF16),
        VMEM((16 * 3, 2, BLOCK, width), BF16),
    ]
    if whole_step:
        in_specs += [fixed(gm.shape)] + [whole(pltpu.HBM)] * len(weights)
        result = jax.ShapeDtypeStruct((tokens, features), F32)
        scratch = [VMEM((3, 4, 8, BLOCK, width), BF16), VMEM((3, tokens, width), BF16)] + scratch
        scratch.append(pltpu.SemaphoreType.DMA)
    else:
        in_specs.append(whole(ANY))
        result = jax.ShapeDtypeStruct((3, tokens, width), BF16)
    return pl.pallas_call(
        functools.partial(attn_backward_body, first, count, places, whole_step),
        grid=(count,),
        out_shape=(result, jax.ShapeDtypeStruct((8, width), F32), half, half),
        in_specs=in_specs,
        out_specs=(fixed(result.shape), fixed((8, width))) + (whole(ANY),) * 2,
        scratch_shapes=scratch + [pltpu.SemaphoreType.DMA],
        compiler_params=pltpu.CompilerParams(vmem_limit_bytes=VMEM_LIMIT),
        cost_estimate=cost(26),
        name="attn_backward",
    )(*operands)


def input_gradient(order, dqkv, dz, weights, places):
    tokens, features = dz.shape
    tile = tokens // 4

    def body(order_ref, dqkv_ref, dz_ref, *refs):
        parts, (out, w_ref, sem) = refs[:8], refs[8:]

        @pl.when(pl.program_id(0) == 0)
        def _():
            fetch_attn(order_ref, parts, places, w_ref, sem, pl.ds(0, features))
            wait_all(w_ref, sem)

        total = dz_ref[...]
        for part in range(3):
            total = total + mm(dqkv_ref[part], w_ref[part].reshape(features, features), NT)
        out[...] = total

    return pl.pallas_call(
        body,
        grid=(4,),
        out_shape=jax.ShapeDtypeStruct((tokens, features), F32),
        in_specs=[
            whole(pltpu.SMEM),
            pl.BlockSpec((3, tile, features), lambda step: (0, step, 0)),
            rows_of(tile, features),
        ]
        + [whole(pltpu.HBM)] * len(weights),
        out_specs=rows_of(tile, features),
        scratch_shapes=[
            VMEM((3, 4, 8, BLOCK, features), BF16),
            pltpu.SemaphoreType.DMA,
        ],
        compiler_params=pltpu.CompilerParams(vmem_limit_bytes=VMEM_LIMIT),
        cost_estimate=cost(4),
        name="input_gradient",
    )(order, dqkv, dz, *weights)


def blocks_of(matrix, features):
    rows, columns = matrix.shape
    shaped = matrix.reshape(rows // BLOCK, BLOCK, columns // features, features)
    return shaped.transpose(0, 2, 1, 3)


def matrix_of(blocks):
    rows, columns, block, features = blocks.shape
    return blocks.transpose(0, 2, 1, 3).reshape(rows * block, columns * features)


CORE, X, Y, Z = 1, 2, 4, 8
Z_MASKS = (0, Z, 2 * Z, 3 * Z)
PLANE_MASKS = (0, X, Y, X | Y)
LOW_MASKS = [
    core | second | first
    for high, low in ((X, Y), (Y, X))
    for core in (0, CORE)
    for second in (0, high)
    for first in (0, low)
]


def swap(part, mask):
    return lax.ppermute(part, AXES, [(device, device ^ mask) for device in range(32)])


def after(value, *earlier):
    return lax.optimization_barrier((value, earlier))[0]


def prepare(place, in_w, out_w, up_w, down_w, vectors, final_norm):
    _, block, features = out_w.shape
    groups = up_w.shape[2] // features
    width, spread = vectors.shape[1], final_norm.shape[0]

    def body(place_ref, in_ref, out_ref, up_ref, down_ref, vec_ref, last_ref, *refs):
        own, rows = refs[:3], refs[3]
        rows[...] = jnp.zeros_like(rows)
        rows[0:2, :width] = vec_ref[...].astype(F32)
        rows[8:9, :spread] = last_ref[...].astype(F32)
        field = rows[0:8, :256]
        field = jnp.where(place_ref[AT_FIELDS] == 0, field, pltpu.roll(field, 64, 1))
        last = rows[8:16, :128]
        chosen = last
        for turn in range(1, 128 // spread):
            turned = pltpu.roll(last, turn * spread, 1)
            chosen = jnp.where(place_ref[AT_FIELDS + 1] == turn * spread, turned, chosen)
        rows[...] = jnp.zeros_like(rows)
        rows[0:1, :256] = field[0:1]
        rows[0:1, 256:512] = field[1:2]
        rows[1:2, :128] = chosen[0:1]
        parts = lambda ref, layer, count: [
            ref[layer, :, features * j : features * (j + 1)] for j in range(count)
        ]
        qkv = [parts(in_ref, layer, 3) for layer in range(2)]
        up = [parts(up_ref, layer, groups) for layer in range(2)]
        down = [
            [down_ref[layer, block * j : block * (j + 1)] for j in range(groups)]
            for layer in range(2)
        ]
        out = [out_ref[layer] for layer in range(2)]
        laid = [
            qkv[0] + [rows[...].astype(BF16)],
            qkv[1][:2] + up[0] + qkv[1][2:] + [out[0]] + down[0],
            up[1] + [out[1]] + down[1],
        ]
        for ref, pieces in zip(own, laid):
            for index, piece in enumerate(pieces):
                ref[index] = piece

    outs = [(count, block, features) for count in (4, 2 * groups + 4, 2 * groups + 1)]
    operands = (in_w, out_w, up_w, down_w, vectors, final_norm[None])
    return pl.pallas_call(
        body,
        grid=(1,),
        out_shape=tuple(jax.ShapeDtypeStruct(shape, BF16) for shape in outs),
        in_specs=[whole(pltpu.SMEM)] + [fixed(part.shape) for part in operands],
        out_specs=tuple(fixed(shape) for shape in outs),
        scratch_shapes=[VMEM((block, features), F32)],
        compiler_params=pltpu.CompilerParams(vmem_limit_bytes=VMEM_LIMIT),
        name="prepare",
    )(place, *operands)


def gather_z(own):
    return [own] + [swap(own, mask) for mask in Z_MASKS[1:]]


def pack_z(place, pieces):
    blocks, *rest = pieces[0].shape

    def body(place_ref, *refs):
        for index in range(4):
            refs[4][:, place_ref[AT_Z] ^ index] = refs[index][...]

    return pl.pallas_call(
        body,
        out_shape=jax.ShapeDtypeStruct((blocks, 4, *rest), BF16),
        in_specs=[whole(pltpu.SMEM)] + [whole()] * 4,
        out_specs=whole(),
        compiler_params=pltpu.CompilerParams(vmem_limit_bytes=SMALL_VMEM),
        name="pack_z",
    )(place, *pieces)


def gather_first(four, cut):
    streams = (four[:cut], Y, X), (four[cut:], X, Y)
    return [(part, swap(part, first), second) for part, first, second in streams]


def gather_second(streams, near):
    return [swap(part, second) for part, (_, _, second) in zip(near, streams)]


def join_two(streams):
    def body(a_ref, b_ref, c_ref, d_ref, out0, out1):
        out0[0], out0[1] = a_ref[...], b_ref[...]
        out1[0], out1[1] = c_ref[...], d_ref[...]

    parts = [part for near, far, _ in streams for part in (near, far)]
    shapes = [(2, *parts[0].shape), (2, *parts[2].shape)]
    return pl.pallas_call(
        body,
        out_shape=tuple(jax.ShapeDtypeStruct(shape, BF16) for shape in shapes),
        in_specs=[whole()] * 4,
        out_specs=(whole(), whole()),
        compiler_params=pltpu.CompilerParams(vmem_limit_bytes=SMALL_VMEM),
        name="join_two",
    )(*parts)


def gather_core(near, far, late):
    near = after(near, far) if late else near
    return [
        part
        for pair in zip(near, far)
        for part in (*pair, *[swap(half, CORE) for half in pair])
    ]


def sum_core(mine, other):
    return hold(mine), swap(other, CORE)


def hold(part):
    def body(in_ref, out_ref, sem):
        copy = pltpu.make_async_copy(in_ref, out_ref, sem)
        copy.start()
        copy.wait()

    return pl.pallas_call(
        body,
        out_shape=jax.ShapeDtypeStruct(part.shape, part.dtype),
        in_specs=[whole(pltpu.HBM)],
        out_specs=whole(),
        scratch_shapes=[pltpu.SemaphoreType.DMA],
        compiler_params=pltpu.CompilerParams(vmem_limit_bytes=SMALL_VMEM),
        cost_estimate=cost(1),
        name="hold",
    )(part)


def sum_plane(place, pairs):
    pairs = [[part.reshape(-1, 4, 4, *part.shape[1:]) for part in pair] for pair in pairs]
    kept, got = zip(*pairs)
    rest = kept[0].shape[3:]
    sizes = [part.shape[0] for part in kept]

    def body(place_ref, *refs):
        outs = refs[2 * len(sizes) :]
        start = 0
        for index, size in enumerate(sizes):
            left, right = refs[index], refs[len(sizes) + index]
            for mask, out in enumerate(outs):
                plane = place_ref[AT_PLANE] ^ mask
                out[start : start + size] = (
                    left[:, :, plane].astype(F32) + right[:, :, plane].astype(F32)
                ).astype(BF16)
            start += size

    return pl.pallas_call(
        body,
        out_shape=(jax.ShapeDtypeStruct((sum(sizes), 4, *rest), BF16),) * 4,
        in_specs=[whole(pltpu.SMEM)] + [whole()] * (2 * len(sizes)),
        out_specs=(whole(),) * 4,
        compiler_params=pltpu.CompilerParams(vmem_limit_bytes=SMALL_VMEM),
        name="sum_plane",
    )(place, *kept, *got)


def send_plane(parts):
    return [parts[0]] + [swap(part, mask) for part, mask in zip(parts[1:], PLANE_MASKS[1:])]


def sum_z(place, parts):
    blocks, _, *rest = parts[0].shape
    count = 3 if blocks % 3 == 0 else 1

    def body(place_ref, *refs):
        for mask in range(4):
            z = place_ref[AT_Z] ^ mask
            total = refs[0][:, z].astype(F32)
            for ref in refs[1:4]:
                total = total + ref[:, z].astype(F32)
            refs[4 + mask][...] = total.astype(BF16)

    return pl.pallas_call(
        body,
        grid=(blocks // count,),
        out_shape=(jax.ShapeDtypeStruct((blocks, *rest), BF16),) * 4,
        in_specs=[whole(pltpu.SMEM)]
        + [pl.BlockSpec((count, 4, *rest), lambda step: (step, 0, 0, 0))] * 4,
        out_specs=(pl.BlockSpec((count, *rest), lambda step: (step, 0, 0)),) * 4,
        compiler_params=pltpu.CompilerParams(vmem_limit_bytes=SMALL_VMEM),
        name="sum_z",
    )(place, *parts)


def send_z(pieces):
    return [pieces[0]] + [swap(piece, mask) for piece, mask in zip(pieces[1:], Z_MASKS[1:])]


def finish(place, ffn1, ffn0, attn0, width, spread):
    _, block, features = ffn1[0].shape
    groups = (ffn1[0].shape[0] - 1) // 2

    def body(place_ref, *refs):
        parts = [refs[:4], refs[4:8], refs[8:12]]
        in_out, out_out, up_out, down_out, vec_out, last_out = refs[12:]

        def total(part, index):
            value = parts[part][0][index].astype(F32)
            for ref in parts[part][1:]:
                value = value + ref[index].astype(F32)
            return value

        for layer, part in ((1, 0), (0, 1)):
            for j in range(groups):
                up_out[layer, :, features * j : features * (j + 1)] = total(part, j)
                down_out[layer, block * j : block * (j + 1)] = total(part, groups + 1 + j)
            out_out[layer] = total(part, groups)
        for layer, part, start in ((1, 1, 2 * groups + 1), (0, 2, 0)):
            for j in range(3):
                in_out[layer, :, features * j : features * (j + 1)] = total(part, start + j)
        rows = total(2, 3)
        for layer in range(2):
            field = rows[0:8, 256 * layer : 256 * layer + 256]
            turned = pltpu.roll(field, 192, 1)
            chosen = jnp.where(place_ref[AT_FIELDS] == 0, field, turned)
            vec_out[layer : layer + 1] = chosen[0:1, :width]
        field = rows[0:8, :128]
        chosen = field
        for turn in range(1, 128 // spread):
            turned = pltpu.roll(field, 128 - turn * spread, 1)
            chosen = jnp.where(place_ref[AT_FIELDS + 1] == turn * spread, turned, chosen)
        last_out[...] = chosen[1:2, :spread]

    shapes = [
        (2, block, 3 * features),
        (2, block, features),
        (2, block, groups * features),
        (2, block * groups, features),
        (2, width),
        (1, spread),
    ]
    return pl.pallas_call(
        body,
        out_shape=tuple(jax.ShapeDtypeStruct(shape, F32) for shape in shapes),
        in_specs=[whole(pltpu.SMEM)] + [whole()] * 12,
        out_specs=tuple(whole() for _ in shapes),
        compiler_params=pltpu.CompilerParams(vmem_limit_bytes=SMALL_VMEM),
        name="finish",
    )(place, *ffn1, *ffn0, *attn0)


def field_of(device, width):
    start = device * width
    return start // 128 * 128, start % 128


def unpack_vectors(order, parts, width, spread):
    def body(order_ref, *refs):
        refs, out, flat, last = refs[:4], *refs[4:]
        flat[...] = jnp.zeros_like(flat)
        last[...] = jnp.zeros_like(last)
        out[...] = jnp.zeros_like(out)
        for index, ref in enumerate(refs):
            for near, z in [(near, z) for near in range(2) for z in range(4)]:
                owner = 8 * z + order_ref[8 + 2 * index + near]
                rows = ref[near, 0, z].astype(F32)
                at = pl.ds(pl.multiple_of(owner * width // 128 * 128, 128), 256)
                for layer in range(2):
                    flat[layer : layer + 1, at] += rows[0:1, 256 * layer : 256 * layer + 256]
                at = pl.ds(pl.multiple_of(owner * spread // 128 * 128, 128), 128)
                last[0:1, at] += rows[1:2, :128]
        for layer in range(2):
            for row in range(12):
                out[layer, row : row + 1] = flat[layer : layer + 1, row * 512 : row * 512 + 512]
            for row in range(2):
                out[layer, 12 + row : 13 + row] = last[0:1, row * 512 : row * 512 + 512]

    features = parts[0].shape[-1]
    at = parts[0].shape[1] - 1
    return pl.pallas_call(
        body,
        grid=(1,),
        out_shape=jax.ShapeDtypeStruct((2, 16, features), F32),
        in_specs=[whole(pltpu.SMEM)]
        + [
            pl.BlockSpec((2, 1, *part.shape[2:]), lambda step: (0, at, 0, 0, 0)) for part in parts
        ],
        out_specs=fixed((2, 16, features)),
        scratch_shapes=[VMEM((8, 12 * features), F32), VMEM((8, 2 * features), F32)],
        compiler_params=pltpu.CompilerParams(vmem_limit_bytes=SMALL_VMEM),
        name="unpack_vectors",
    )(order, *parts)


def pack_vectors(order, attn_rows, ffn_rows, width, spread):
    features = ffn_rows[0].shape[1]

    def body(order_ref, a0, a1, f0, f1, out0, out1, flat, last):
        for layer, (attn, ffn) in enumerate(((a0, f0), (a1, f1))):
            for row in range(12):
                source = attn if row < 2 else ffn
                flat[layer : layer + 1, row * 512 : row * 512 + 512] = source[row : row + 1]
        for row in range(2):
            last[0:1, row * 512 : row * 512 + 512] = f1[12 + row : 13 + row]
        for half, out in enumerate((out0, out1)):
            out[...] = jnp.zeros_like(out)
            core = order_ref[AT_CORE] if half == 0 else 1 - order_ref[AT_CORE]
            for pair in range(16):
                owner = 2 * pair + core
                at = pl.ds(pl.multiple_of(owner * width // 128 * 128, 128), 256)
                fields = [flat[layer : layer + 1, at] for layer in range(2)]
                at = pl.ds(pl.multiple_of(owner * spread // 128 * 128, 128), 128)
                final = jnp.concatenate([last[0:1, at], jnp.zeros((1, 384), F32)], axis=1)
                rows = [jnp.concatenate(fields, axis=1), final, jnp.zeros((BLOCK - 2, 512), F32)]
                out[pair] = jnp.concatenate(rows, axis=0).astype(BF16)

    return pl.pallas_call(
        body,
        out_shape=(jax.ShapeDtypeStruct((16, BLOCK, features), BF16),) * 2,
        in_specs=[whole(pltpu.SMEM)] + [whole()] * 4,
        out_specs=(whole(), whole()),
        scratch_shapes=[VMEM((8, 12 * features), F32), VMEM((8, 2 * features), F32)],
        compiler_params=pltpu.CompilerParams(vmem_limit_bytes=SMALL_VMEM),
        name="pack_vectors",
    )(order, *attn_rows, *ffn_rows)


def total_of(pieces):
    total = pieces[0].astype(F32)
    for piece in pieces[1:]:
        total = total + piece.astype(F32)
    return total


def local(
    main_residual,
    side_residual,
    cotangent,
    lengths,
    input_weight,
    output_weight,
    expand_weight,
    reduce_weight,
    vectors,
    final_norm,
):
    tokens, features = main_residual.shape
    layers = input_weight.shape[0]
    assert lengths.shape[0] == 1 and layers == 2
    per = features // BLOCK
    pairs = features // 128
    half_pairs = pairs // 2
    groups = expand_weight.shape[2] // features
    fast = lax.axis_size(AXES) == 32 and per == 32
    ffn_at = ((2, (1, 1), 2), (0, (0, groups), 0))
    width = vectors.shape[1]
    spread = final_norm.shape[0]

    def vec_rows(all_vectors, final_full):
        return jnp.concatenate(
            [
                all_vectors.reshape(layers, 12, features),
                jnp.broadcast_to(final_full.reshape(1, 2, features), (layers, 2, features)),
                jnp.zeros((layers, 2, features), F32),
            ],
            axis=1,
        )

    if fast:
        me = lax.axis_index(AXES)
        table = [
            [(device ^ mask) & 7 for mask in LOW_MASKS]
            + [device // Z, device // X & 3, device & CORE]
            + [field_of(device, width)[1], field_of(device, spread)[1]]
            for device in range(32)
        ]
        order = jnp.array(table, jnp.int32)[me]
        own = prepare(
            order, input_weight, output_weight, expand_weight, reduce_weight, vectors, final_norm
        )
        z0 = gather_z(own[0])
        z1 = gather_z(after(own[1], z0[1:]))
        two = gather_first(pack_z(order, z0), 2)
        near = join_two(two)
        far = gather_second(two, near)
        attn0 = gather_core(near, far, True)
        vec = unpack_vectors(order, attn0[4:], width, spread)
        four = pack_z(order, after(z1, near))
        two = gather_first(after(four, far[0]), groups + 2)
        two = [(part, after(got, vec), mask) for part, got, mask in two]
        z2 = gather_z(after(own[2], attn0))
        near = join_two(two)
        far = gather_second(two, near)
        x0 = after(main_residual, near)
    else:
        gather = lambda part, axis: lax.all_gather(part, AXES, axis=axis, tiled=True)
        order = jnp.array(LOW_MASKS + [0] * 5, jnp.int32)

        def streams(*two):
            parts = []
            for stream, blocks in enumerate(two):
                joined = jnp.concatenate(blocks, axis=1)
                joined = joined.reshape(4, 8, *joined.shape[1:]).transpose(1, 2, 0, 3, 4)
                lows = LOW_MASKS[8 * stream : 8 * stream + 8]
                parts += [joined[jnp.array(lows[at : at + 2])] for at in range(0, 8, 2)]
            return parts

        vec = vec_rows(gather(vectors, 1).astype(F32), gather(final_norm, 0).astype(F32))
        parts = []
        for layer in range(layers):
            qkv = blocks_of(gather(input_weight[layer], 0), features)
            up = blocks_of(gather(expand_weight[layer], 0), features)
            out = blocks_of(gather(output_weight[layer], 0), features)
            down = gather(reduce_weight[layer], 0).reshape(per, -1, BLOCK, features)
            parts.append((qkv, up, out, down))
        (qkv0, up0, out0, down0), (qkv1, up1, out1, down1) = parts
        attn0 = streams([qkv0[:, :2]], [qkv0[:, 2:]])
        mixed = streams([qkv1[:, :2], up0], [qkv1[:, 2:], out0, down0])
        ffn1 = streams([up1, out1], [down1])
        x0 = main_residual

    e0, ctx0, rinv0, qkv0 = attn_forward(
        lengths, 0, pairs, None, order, x0, vec, attn0, 0, 0
    )
    x0 = main_residual
    if fast:
        far, z2 = after((far, z2), e0)
        mixed = gather_core(near, far, True)
        two = gather_first(pack_z(order, z2), groups + 1)
        x0 = after(x0, *[part for part, _, _ in two])
    xh1, xh2, stat, m1b, hid, m2, m2b, y, qkv1 = ffn_call(
        True, False, False, 0, order, vec, mixed, ffn_at[0], ctx0, (x0, side_residual)
    )
    if fast:
        two = [(part, after(got, m2b), mask) for part, got, mask in two]
        near = join_two(two)
        qkv1 = after(qkv1, near)
        far = gather_second(two, near)
    e1, ctx1, rinv1 = attn_forward(lengths, 0, pairs, qkv1)
    if fast:
        ffn1 = gather_core(near, after(far, e1), False)
    layer_out, grad_side, gm, do, dvec1, *gf1 = ffn_call(
        True, True, True, 1, order, vec, ffn1, ffn_at[1], ctx1, (m2, y, cotangent), rinv1
    )
    if fast:
        f1 = sum_plane(order, [sum_core(*gf1)])
        gm = after(gm, f1)
        f1 = send_plane(f1)
    gm, dvec1a, *gi1 = attn_backward(
        order, 0, pairs, e1, 0, do, qkv1, m2b, gm, mixed, 0
    )
    if fast:
        i1 = (gi1[0], swap(gi1[1], CORE))
        f1 = sum_z(order, after(f1, gm))
        gm = after(gm, f1)
        f1 = send_z(f1)
    gm, do, dvec0, *gf0 = ffn_call(
        False, True, False, 0, order, vec, mixed, ffn_at[0], ctx0,
        (xh1, xh2, stat, m1b, hid, gm, grad_side), rinv0,
    )
    if fast:
        f1, i1 = after((f1, i1), gm)
        f0 = sum_plane(order, [sum_core(*after(gf0, f1)), (hold(i1[0]), i1[1])])
        do = after(do, f0)
        f0 = send_plane(f0)
    dqkv, dvec0a, *gi0 = attn_backward(
        order, 0, pairs, e0, 0, do, qkv0, main_residual, None, None, 0
    )
    if fast:
        rows = pack_vectors(order, (dvec0a, dvec1a), (dvec0, dvec1), width, spread)
        i0 = sum_plane(order, [sum_core(*gi0), sum_core(*rows)])
        f0 = send_z(sum_z(order, after(f0, dqkv)))
        i0 = send_plane(after(i0, f0[0]))
        gm, dqkv = after((gm, dqkv), f0[0], i0[0])
        grad_main = input_gradient(order, dqkv, gm, attn0, 0)
        i0 = send_z(sum_z(order, after(i0, grad_main)))
        grad_in, grad_out, grad_up, grad_down, grad_vec, grad_final = finish(
            order, f1, f0, i0, width, spread
        )
        grad_final = grad_final[0]
    else:
        grad_main = input_gradient(order, dqkv, gm, attn0, 0)
        scatter = lambda part, axis: lax.psum_scatter(
            part, AXES, scatter_dimension=axis, tiled=True
        ).astype(F32)

        def natural(even, odd):
            joined = jnp.stack([even, odd], axis=1)
            return joined.reshape(-1, per, *even.shape[1:]).swapaxes(0, 1)

        both = lambda make: jnp.stack(
            [make(natural(*i), natural(*f)) for i, f in ((gi0, gf0), (gi1, gf1))]
        )
        grad_in = scatter(both(lambda i, f: matrix_of(i)), 1)
        grad_up = scatter(both(lambda i, f: matrix_of(f[:, :groups])), 1)
        grad_out = scatter(both(lambda i, f: matrix_of(f[:, groups : groups + 1])), 1)
        grad_down = scatter(both(lambda i, f: f[:, groups + 1 :].reshape(-1, features)), 1)
        dvec = [
            jnp.concatenate([first[0:2], rest[2:12]]).reshape(-1)
            for first, rest in ((dvec0a, dvec0), (dvec1a, dvec1))
        ]
        grad_vec = scatter(jnp.stack(dvec), 1)
        grad_final = scatter(dvec1[12:14].reshape(-1), 0)
    return (
        layer_out,
        grad_main,
        grad_side,
        grad_in,
        grad_out,
        grad_up,
        grad_down,
        grad_vec,
        grad_final,
    )


def solution(mesh):
    rows = P(AXES, None)
    middle = P(None, AXES, None)
    return jax.shard_map(
        local,
        mesh=mesh,
        in_specs=(rows, rows, rows, rows, middle, middle, middle, middle, P(None, AXES), P(AXES)),
        out_specs=(rows, rows, rows, middle, middle, middle, middle, P(None, AXES), P(AXES)),
        check_vma=False,
    )
```

```python
import functools

import jax
import jax.numpy as jnp
from jax import lax
from jax.experimental import pallas as pl
from jax.experimental.pallas import tpu as pltpu
from jax.sharding import PartitionSpec as P

HEAD_DIM = 64
AXES = ("wide", "narrow")
F32 = jnp.float32
BF16 = jnp.bfloat16
NN = (((1,), (0,)), ((), ()))
NT = (((1,), (1,)), ((), ()))
TN = (((0,), (0,)), ((), ()))
MASKED = -1000000000.0
VMEM_LIMIT = 60 * 2**20
SMALL_VMEM = 24 * 2**20


def cost(microseconds):
    return pl.CostEstimate(
        flops=microseconds * 10**9, bytes_accessed=microseconds * 10**6, transcendentals=0
    )


BLOCK = 16
CHUNK = 512
TILE = 256
ROWS = 64
VMEM = pltpu.VMEM
ANY = pl.ANY


def mm(left, right, dims):
    return lax.dot_general(left, right, dims, preferred_element_type=F32)


def whole(memory=VMEM):
    return pl.BlockSpec(memory_space=memory)


def fixed(shape):
    zeros = (0,) * len(shape)
    return pl.BlockSpec(shape, lambda step: zeros)


def rows_of(tile, width):
    return pl.BlockSpec((tile, width), lambda step: (step, 0))


AT_Z, AT_PLANE, AT_CORE, AT_FIELDS = 16, 17, 18, 19


def each_part(place_ref, weights, stream):
    return [
        (weights[index].at[near], place_ref[2 * index + near])
        for index in range(4 * stream, 4 * stream + 4)
        for near in range(2)
    ]


def wait_all(ref, sem):
    pltpu.make_async_copy(ref, ref, sem).wait()


def fetch_attn(order_ref, weights, at, w_ref, sem, columns):
    for ref, low in each_part(order_ref, weights, 0):
        pltpu.make_async_copy(
            ref.at[pl.ds(at, 2), :, :, columns], w_ref.at[pl.ds(0, 2), :, low], sem
        ).start()
    for ref, low in each_part(order_ref, weights, 1):
        pltpu.make_async_copy(ref.at[at, :, :, columns], w_ref.at[2, :, low], sem).start()


def project(x, w_ref, vec_ref, layer, part):
    features = x.shape[1]
    packed = mm(x, w_ref[part].reshape(features, features), NN)
    if part == 0:
        return (packed + vec_ref[layer, 0:1]).astype(BF16) * BF16(0.125)
    if part == 2:
        packed = packed + vec_ref[layer, 1:2]
    return packed.astype(BF16)


def attn_forward_body(first, count, places, layer, *refs):
    refs = list(refs)
    take = lambda: refs.pop(0)
    bounds_ref = take()
    if places is not None:
        order_ref, x_ref, vec_ref = take(), take(), take()
        weights = [take() for _ in range(8)]
        e_ref, ctx_ref, rinv_ref, qkv_ref, aux_ref, rows_ref, w_ref, sem = refs
        at = pl.program_id(0) + first
    else:
        qkv_ref, e_ref, ctx_ref, rinv_ref, aux_ref, rows_ref = refs
        at = 0
    step = pl.program_id(0)
    tokens = ctx_ref.shape[0]
    lane = lax.broadcasted_iota(jnp.int32, (tokens, 128), 1)
    low_half = lane < HEAD_DIM

    @pl.when(step == 0)
    def _():
        if places is not None:
            features = x_ref.shape[1]
            fetch_attn(order_ref, weights, places, w_ref, sem, pl.ds(0, features))
        token = lax.broadcasted_iota(jnp.int32, (tokens, 128), 0)
        column = lane % HEAD_DIM
        single = bounds_ref[0, 1] == 0
        quarter = tokens // 4
        segment = jnp.where(single, 0, token // quarter)
        inside = jnp.where(single, token, token % quarter)
        own = column == segment
        bound = jnp.where(
            segment == 0,
            bounds_ref[0, 0],
            jnp.where(
                segment == 1,
                bounds_ref[0, 1],
                jnp.where(segment == 2, bounds_ref[0, 2], bounds_ref[0, 3]),
            ),
        )
        alive = own & (inside < bound)
        aux_ref[0] = jnp.where(own, 1.0, 0.0).astype(BF16)
        aux_ref[1] = jnp.where(alive | (column >= 4), 0.0, MASKED).astype(BF16)
        rows_ref[...] = jnp.zeros_like(rows_ref)
        if places is not None:
            wait_all(w_ref, sem)
            x = x_ref[...]
            for part in range(3):
                packed = project(x, w_ref, vec_ref, layer, part)
                for index in range(features // 128):
                    qkv_ref[part, index] = packed[:, index * 128 : (index + 1) * 128]

    query = qkv_ref[0, at]
    key = qkv_ref[1, at]
    value_t = qkv_ref[2, at].T
    ones = jnp.ones((16, tokens), BF16)
    chunk = CHUNK

    def heads(shifted):
        outs, sums = [], []
        for head in range(2):
            inside_head = low_half if head == 0 else ~low_half
            query_aug = jnp.where(inside_head, query, aux_ref[0])
            key_aug = jnp.where(inside_head, key, aux_ref[1])
            value_aug = jnp.concatenate(
                [value_t[head * HEAD_DIM : (head + 1) * HEAD_DIM], ones], axis=0
            )
            parts = []
            for start in range(0, tokens, chunk):
                scores = mm(key_aug, query_aug[start : start + chunk], NT)
                if shifted:
                    scores = scores - jnp.max(scores, axis=0, keepdims=True)
                exponent = jnp.exp(scores).astype(BF16)
                e_ref[head, :, start : start + chunk] = exponent
                mixed = mm(value_aug, exponent, NN)
                total = mixed[HEAD_DIM : HEAD_DIM + 1]
                inverse = 1.0 / total
                rows_ref[pl.ds(step * 2 + head, 1), start : start + chunk] = inverse
                parts.append(mixed[:HEAD_DIM] * inverse)
                sums.append(total)
            outs.append(jnp.concatenate(parts, axis=1))
        ctx_ref[...] = jnp.concatenate(outs, axis=0).T.astype(BF16)
        return jnp.concatenate(sums, axis=1)

    sums = heads(False)
    fits = (jnp.max(sums) <= 2.0**40) & (jnp.min(sums) >= 2.0**-40)

    @pl.when(jnp.logical_not(fits))
    def _():
        heads(True)

    @pl.when(step == pl.num_programs(0) - 1)
    def _():
        inverses = rows_ref[...].T
        high = inverses.astype(BF16).astype(F32)
        low = pltpu.roll(inverses - high, 2 * count, 1)
        rinv_ref[...] = (high + low).astype(BF16)


def attn_forward(bounds, first, count, qkv=None, order=None, x=None, vec=None, weights=(), places=None, layer=0):
    project = places is not None
    if project:
        tokens, features = x.shape
        pairs = features // 128
    else:
        _, pairs, tokens, _ = qkv.shape
    out_shape = [
        jax.ShapeDtypeStruct((2 * count, tokens, tokens), BF16),
        jax.ShapeDtypeStruct((tokens, 128 * count), BF16),
        jax.ShapeDtypeStruct((tokens, 128), BF16),
    ]
    out_specs = [
        pl.BlockSpec((2, tokens, tokens), lambda step: (step, 0, 0)),
        pl.BlockSpec((tokens, 128), lambda step: (0, step)),
        fixed((tokens, 128)),
    ]
    scratch = [VMEM((2, tokens, 128), BF16), VMEM((128, tokens), F32)]
    if project:
        operands = (bounds, order, x, vec, *weights)
        in_specs = [whole(pltpu.SMEM), whole(pltpu.SMEM), fixed(x.shape), fixed(vec.shape)]
        in_specs += [whole(pltpu.HBM)] * len(weights)
        out_shape.append(jax.ShapeDtypeStruct((3, pairs, tokens, 128), BF16))
        out_specs.append(fixed((3, pairs, tokens, 128)))
        scratch += [
            VMEM((3, 4, features // BLOCK // 4, BLOCK, features), BF16),
            pltpu.SemaphoreType.DMA,
        ]
    else:
        operands = (bounds, qkv)
        in_specs = [
            whole(pltpu.SMEM),
            pl.BlockSpec((3, 1, tokens, 128), lambda step: (0, step + first, 0, 0)),
        ]
    return pl.pallas_call(
        functools.partial(attn_forward_body, first, count, places, layer),
        grid=(count,),
        out_shape=tuple(out_shape),
        in_specs=in_specs,
        out_specs=tuple(out_specs),
        scratch_shapes=scratch,
        compiler_params=pltpu.CompilerParams(vmem_limit_bytes=VMEM_LIMIT),
        cost_estimate=cost(14),
        name="attn_forward",
    )(*operands)


def normed(z):
    centered = z - jnp.mean(z, axis=-1, keepdims=True)
    variance = jnp.mean(centered * centered, axis=-1, keepdims=True)
    rstd = lax.rsqrt(variance + 1e-05)
    return centered * rstd, rstd


def norm_back(grad, gain, xhat, rstd):
    scaled = grad * gain
    first = jnp.mean(scaled, axis=-1, keepdims=True)
    second = jnp.mean(scaled * xhat, axis=-1, keepdims=True)
    return rstd * (scaled - first - xhat * second)


GELU_A = 0.7978845608028654
GELU_B = 0.044715


def gelu(hidden, sloped):
    square = hidden * hidden
    tanh = jnp.tanh(hidden * (BF16(GELU_A) + BF16(GELU_A * GELU_B) * square))
    chance = BF16(0.5) + BF16(0.5) * tanh
    active = hidden * chance
    if not sloped:
        return active
    inner = BF16(GELU_A) + BF16(3.0 * GELU_A * GELU_B) * square
    return active, chance + active * (BF16(1.0) - tanh) * inner


def column_sum(ref, row, values):
    ref[row : row + 1] += jnp.sum(values.astype(F32), axis=0, keepdims=True)


def weave(vector_work, matrix_work):
    done = 0
    for index, work in enumerate(vector_work):
        work()
        target = (index + 1) * len(matrix_work) // len(vector_work)
        for matrix in matrix_work[done:target]:
            matrix()
        done = target
    for matrix in matrix_work[done:]:
        matrix()


def ffn_body(mode, layer, places, in_names, out_names, scratch_names, *refs):
    forward, backward, last = mode
    refs = list(refs)
    take = lambda count: [refs.pop(0) for _ in range(count)]
    up_at, (out_stream, out_at), down_at = places
    order_ref, vec_ref = take(2)
    weights = take(8)
    ins = dict(zip(in_names, take(len(in_names))))
    outs = dict(zip(out_names, take(len(out_names))))
    if backward:
        dvec_out, *grads = take(3)
    here = dict(zip(scratch_names, take(len(scratch_names))))
    wo_ref, up_ref, down_ref, sem_w, sem_in, sem_out = take(6)
    if not backward:
        (next_ref,) = take(1)
    assert not refs
    tokens = here["ctx"].shape[0]
    features = vec_ref.shape[2]
    groups = up_ref.shape[0]
    per = features // BLOCK
    wo = lambda: wo_ref[...].reshape(features, features)
    up = lambda j, zs: up_ref[j, zs].reshape(-1, features)
    down = lambda j, part: down_ref[j, part].reshape(-1, features)
    every = slice(None)
    up_halves = [slice(0, 2), slice(2, 4)]
    down_halves = [slice(0, 4), slice(4, 8)]
    wide = features // 2
    half_columns = [slice(0, wide), slice(wide, features)]
    of = lambda j: slice(j * features, (j + 1) * features)
    vec = lambda row: vec_ref[layer, row : row + 1]
    copy_in = {
        name: pltpu.make_async_copy(ref, here[name], sem_in.at[index])
        for index, (name, ref) in enumerate(ins.items())
    }
    sem_of = {name: sem_out.at[index] for index, name in enumerate(outs)}

    def leave(*names, rows=slice(None), columns=None):
        for name in names:
            at = (rows,) if columns is None else (rows, columns)
            if name == "do":
                at = (slice(None), rows)
            if name == "qkv":
                at = (slice(None), slice(None), rows)
            pltpu.make_async_copy(
                here[name].at[at], outs[name].at[at], sem_of[name]
            ).start()

    def leave_all():
        for name, ref in outs.items():
            wait_all(here[name], sem_of[name])

    blocks = [slice(start, start + TILE) for start in range(0, tokens, TILE)]
    chunks = [slice(start, start + ROWS) for start in range(0, tokens, ROWS)]

    def fetch_out(ref, low):
        pltpu.make_async_copy(ref.at[out_at], wo_ref.at[:, low], sem_w.at[0]).start()

    def fetch_up(ref, low):
        pltpu.make_async_copy(
            ref.at[pl.ds(up_at, groups)], up_ref.at[:, :, low], sem_w.at[1]
        ).start()

    def fetch_down(ref, low):
        for block in range(groups):
            pltpu.make_async_copy(
                ref.at[down_at + block], down_ref.at[:, low, block], sem_w.at[2]
            ).start()

    early = ("ctx", "x", "y") if forward else ("gm", "gs", "xh2", "stat")
    for name in early:
        copy_in[name].start()
    for fetch in (fetch_out, fetch_up, fetch_down) if forward else (fetch_down, fetch_up, fetch_out):
        stream = {fetch_out: out_stream, fetch_up: 0, fetch_down: 1}[fetch]
        for ref, low in each_part(order_ref, weights, stream):
            fetch(ref, low)
    if not backward:
        fetch_attn(order_ref, weights, 0, next_ref, sem_w.at[3], pl.ds(0, features))
    for name in in_names:
        if name not in early:
            copy_in[name].start()
    waited = set()

    def need(*names):
        for name in names:
            if name not in waited:
                waited.add(name)
                copy_in[name].wait()

    if backward:
        dvec_out[...] = jnp.zeros_like(dvec_out)
    if forward:
        need("ctx", "x", "y")
        wait_all(wo_ref, sem_w.at[0])
        for rows in blocks:
            branch = mm(here["ctx"][rows], wo(), NN) + vec(2)
            xh1, rstd1 = normed(here["x"][rows].astype(F32) + branch)
            m1 = xh1 * vec(3) + vec(4)
            here["m1"][rows] = m1
            here["m1b"][rows] = m1.astype(BF16)
            here["y_new"][rows] = here["y"][rows].astype(F32) + branch
            here["xh1"][rows] = xh1.astype(BF16)
            here["stat"][rows, :64] = jnp.broadcast_to(rstd1, (TILE, 64))
            if not backward:
                leave("xh1", "m1b", rows=rows)
        wait_all(up_ref, sem_w.at[1])

        def hidden_dots(j):
            def piece(rows):
                here["work"][j % 2, rows] = mm(here["m1b"][rows], up(j, every), NN)

            return [functools.partial(piece, rows) for rows in blocks]

        def activate(j):
            def piece(rows):
                hidden = (here["work"][j % 2, rows] + vec(8 + j)).astype(BF16)
                if backward:
                    active, slope = gelu(hidden, True)
                    here["hid"][rows, of(j)] = slope
                else:
                    active = gelu(hidden, False)
                    here["hid"][rows, of(j)] = hidden
                here["act"][rows, of(j)] = active

            return [functools.partial(piece, rows) for rows in chunks]

        def branch_dots(j):
            def piece(rows):
                part = mm(here["act"][rows, of(j)], down(j, every), NN)
                here["sum"][rows] = part + (vec(5) if j == 0 else here["sum"][rows])

            return [functools.partial(piece, rows) for rows in blocks]

        weave([], hidden_dots(0))
        wait_all(down_ref, sem_w.at[2])
        for j in range(groups):
            matrix = hidden_dots(j + 1) if j + 1 < groups else []
            if j > 0:
                matrix = matrix + branch_dots(j - 1)
            weave(activate(j), matrix)
            if not backward:
                leave("hid", columns=of(j))
        weave([], branch_dots(groups - 1))
        if last:
            need("cot")
        if not backward:
            wait_all(next_ref, sem_w.at[3])
        for rows in blocks:
            xh2, rstd2 = normed(here["m1"][rows] + here["sum"][rows])
            m2 = xh2 * vec(6) + vec(7)
            y = here["y_new"][rows] + here["sum"][rows]
            if not backward:
                here["xh2"][rows] = xh2.astype(BF16)
                here["stat"][rows, 64:] = jnp.broadcast_to(rstd2, (TILE, 64))
                here["m2"][rows] = m2
                here["m2b"][rows] = m2.astype(BF16)
                here["y_new"][rows] = y
                leave("xh2", "stat", "m2", "m2b", "y_new", rows=rows)
                for part in range(3):
                    packed = project(here["m2b"][rows], next_ref, vec_ref, layer + 1, part)
                    for index in range(features // 128):
                        here["qkv"][part, index, rows] = packed[
                            :, index * 128 : (index + 1) * 128
                        ]
                leave("qkv", rows=rows)
                continue
            yh, rstdy = normed(y)
            here["layer_out"][rows] = (m2 + yh * vec(12) + vec(13)).astype(BF16)
            gm = here["cot"][rows].astype(F32)
            gs = norm_back(gm, vec(12), yh, rstdy)
            here["gs"][rows] = gs
            column_sum(dvec_out, 12, gm * yh)
            column_sum(dvec_out, 13, gm)
            column_sum(dvec_out, 6, gm * xh2)
            column_sum(dvec_out, 7, gm)
            dz2 = norm_back(gm, vec(6), xh2, rstd2)
            df = (dz2 + gs).astype(BF16)
            column_sum(dvec_out, 5, df)
            here["df"][rows] = df
            here["sum"][rows] = dz2
            leave("layer_out", "gs", rows=rows)
        if not backward:
            leave_all()
            return
    else:
        need("gm", "gs", "xh2", "stat")
        for rows in blocks:
            gm = here["gm"][rows]
            xh2 = here["xh2"][rows].astype(F32)
            column_sum(dvec_out, 6, gm * xh2)
            column_sum(dvec_out, 7, gm)
            dz2 = norm_back(gm, vec(6), xh2, here["stat"][rows, 64:65])
            df = (dz2 + here["gs"][rows]).astype(BF16)
            column_sum(dvec_out, 5, df)
            here["df"][rows] = df
            here["sum"][rows] = dz2
        wait_all(down_ref, sem_w.at[2])

    def back_dots(j):
        def piece(rows, columns):
            here["work"][j % 2, :, columns] = mm(here["df"][...], down(j, rows), NT)

        return [functools.partial(piece, *part) for part in zip(down_halves, half_columns)]

    def activate_back(j):
        def piece(rows):
            dactive = here["work"][j % 2, rows].astype(BF16)
            slope = here["hid"][rows, of(j)]
            if not forward:
                active, slope = gelu(slope, True)
                here["act"][rows, of(j)] = active
            dhidden = slope * dactive
            here["hid"][rows, of(j)] = dhidden
            column_sum(dvec_out, 8 + j, dhidden)

        return [functools.partial(piece, rows) for rows in chunks]

    def main_dots(j):
        def piece(rows, columns):
            here["sum"][:, columns] += mm(here["hid"][:, of(j)], up(j, rows), NT)

        return [functools.partial(piece, *part) for part in zip(up_halves, half_columns)]

    gup, gdown, gout = here["gup"], here["gdown"], here["gout"]

    def down_grads(j):
        def piece(index, columns):
            rows = slice(j * features + columns.start, j * features + columns.stop)
            gdown[4 * j + 2 * index : 4 * j + 2 * index + 2] = (
                mm(here["act"][:, rows], here["df"][...], TN)
                .astype(BF16)
                .reshape(2, 2, groups, BLOCK, features)
            )

        return [functools.partial(piece, *part) for part in enumerate(half_columns)]

    def up_grads(j):
        def piece(columns):
            source = slice(j * features + columns.start, j * features + columns.stop)
            gup[16 * j : 16 * j + 16, :, :, columns] = (
                mm(here["m1b"][...], here["hid"][:, source], TN)
                .astype(BF16)
                .reshape(16, 2, BLOCK, wide)
            )

        return [functools.partial(piece, columns) for columns in half_columns]

    weave([], back_dots(0))
    if not forward:
        need("hid")
    for j in range(groups):
        if not forward and j == 1:
            wait_all(up_ref, sem_w.at[1])
        matrix = back_dots(j + 1) if j + 1 < groups else []
        if j > 0:
            matrix = matrix + main_dots(j - 1) + down_grads(j - 1)
        weave(activate_back(j), matrix)
    weave([], main_dots(groups - 1))
    need(*in_names)
    if not forward:
        wait_all(wo_ref, sem_w.at[0])

    lane = lax.broadcasted_iota(jnp.int32, (TILE, 128), 1)
    low_half = lane < HEAD_DIM
    column = lane % HEAD_DIM

    def norm_one(rows):
        gm = here["sum"][rows]
        xh1 = here["xh1"][rows].astype(F32)
        column_sum(dvec_out, 3, gm * xh1)
        column_sum(dvec_out, 4, gm)
        dz1 = norm_back(gm, vec(3), xh1, here["stat"][rows, 0:1])
        here["dz1"][rows] = dz1
        da = (dz1 + here["gs"][rows]).astype(BF16)
        column_sum(dvec_out, 2, da)
        here["da"][rows] = da
        leave("dz1", rows=rows)

    heads = features // HEAD_DIM
    iota = lambda shape, axis: lax.broadcasted_iota(jnp.int32, shape, axis)
    if backward:
        mark = lambda picked: jnp.where(picked, 1.0, 0.0).astype(BF16)
        shape = (features, 128)
        place = mark(iota(shape, 1) % HEAD_DIM // 2 == iota(shape, 0) // HEAD_DIM)
        part = iota((128, 128), 0)
        part = jnp.where(part < 2 * heads, part % heads, heads)
        turn = mark(iota((128, 128), 1) % HEAD_DIM // 2 == part)
        shape = (128, features)
        part = iota(shape, 0)
        part = jnp.where(part < 2 * heads, part % heads, heads)
        share = mark(iota(shape, 1) // HEAD_DIM == part)

    def context_one(rows):
        dctx = mm(here["da"][rows], wo(), NT)
        product = dctx * here["ctx"][rows].astype(F32)
        high = product.astype(BF16)
        low = (product - high.astype(F32)).astype(BF16)
        inverse = here["rinv"][rows]
        dots = -(mm(high, place, NN) + mm(low, place, NN)) * mm(inverse, turn, NN)
        high = dots.astype(BF16).astype(F32)
        extra = jnp.where(column % 2 == 0, high, dots - high).astype(BF16)
        scaled = (dctx * mm(inverse, share, NN)).astype(BF16)
        for at in range(heads):
            pair = slice(at // 2 * 128, at // 2 * 128 + 128)
            inside = low_half if at % 2 == 0 else ~low_half
            here["do"][at, rows] = jnp.where(inside, scaled[:, pair], extra)
        leave("do", rows=rows)

    def send(source, sem):
        for index, ref in enumerate(grads):
            core = order_ref[AT_CORE] if index == 0 else 1 - order_ref[AT_CORE]
            for block, count, part in source(core):
                pltpu.make_async_copy(
                    part, ref.at[pl.ds(16 * block, 16 * count)], sem_w.at[sem]
                ).start()

    matrix = down_grads(groups - 1) + up_grads(0)
    weave([functools.partial(norm_one, rows) for rows in blocks], matrix)
    send(
        lambda core: [
            (groups + 1 + block, 1, gdown.at[:, core, block]) for block in range(groups)
        ],
        2,
    )
    matrix = [piece for j in range(1, groups) for piece in up_grads(j)]
    weave([functools.partial(context_one, rows) for rows in blocks], matrix)
    send(lambda core: [(0, groups, gup.at[:, core])], 1)
    gout[...] = (
        mm(here["ctx"][...], here["da"][...], TN)
        .astype(BF16)
        .reshape(16, 2, BLOCK, features)
    )
    send(lambda core: [(groups, 1, gout.at[:, core])], 0)
    wait_all(gup, sem_w.at[1])
    wait_all(gout, sem_w.at[0])
    wait_all(gdown, sem_w.at[2])
    leave_all()


def ffn_call(forward, backward, last, layer, order, vec, weights, places, ctx, tiled, rinv=None):
    tokens, features = ctx.shape
    groups = 4
    width = groups * features
    per = features // BLOCK
    heads = features // HEAD_DIM
    if forward:
        ins = dict(zip(("ctx", "x", "y", "cot"), (ctx, *tiled)))
    else:
        names = ("ctx", "xh1", "xh2", "stat", "m1b", "hid", "gm", "gs")
        ins = dict(zip(names, (ctx, *tiled)))
    if backward:
        ins["rinv"] = rinv
    square, full = (tokens, features), (tokens, width)
    small = (tokens, 128)
    scratch = {name: (value.shape, value.dtype) for name, value in ins.items()}
    scratch["work"] = ((2, *square), F32)
    scratch["sum"] = (square, F32)
    scratch["act"] = (full, BF16)
    if forward:
        scratch.update(
            m1=(square, F32), m1b=(square, BF16), y_new=(square, F32), xh1=(square, BF16),
            stat=(small, F32), hid=(full, BF16),
        )
    if last:
        scratch.update(layer_out=(square, BF16), gs=(square, F32))
    if forward and not backward:
        scratch.update(
            xh2=(square, BF16), m2=(square, F32), m2b=(square, BF16),
            qkv=((3, features // 128, *small), BF16),
        )
        out_names = ["xh1", "xh2", "stat", "m1b", "hid", "m2", "m2b", "y_new", "qkv"]
    else:
        scratch.update(
            df=(square, BF16), dz1=(square, F32), da=(square, BF16), do=((heads, *small), BF16),
            gup=((16 * groups, 2, BLOCK, features), BF16),
            gdown=((16, 2, groups, BLOCK, features), BF16),
            gout=((16, 2, BLOCK, features), BF16),
        )
        out_names = (["layer_out", "gs"] if last else []) + ["dz1", "do"]
    out_shape = [jax.ShapeDtypeStruct(*scratch[name]) for name in out_names]
    out_specs = [whole(ANY)] * len(out_names)
    if backward:
        half = jax.ShapeDtypeStruct((16 * (2 * groups + 1), BLOCK, features), BF16)
        out_shape += [jax.ShapeDtypeStruct((16, features), F32), half, half]
        out_specs += [whole(), whole(ANY), whole(ANY)]
    return pl.pallas_call(
        functools.partial(
            ffn_body, (forward, backward, last), layer, places, tuple(ins), tuple(out_names),
            tuple(scratch),
        ),
        out_shape=tuple(out_shape),
        in_specs=[whole(pltpu.SMEM), whole()] + [whole(pltpu.HBM)] * (8 + len(ins)),
        out_specs=tuple(out_specs),
        scratch_shapes=[VMEM(*kind) for kind in scratch.values()]
        + [
            VMEM((4, 8, BLOCK, features), BF16),
            VMEM((groups, 4, 8, BLOCK, features), BF16),
            VMEM((4, 8, groups, BLOCK, features), BF16),
            pltpu.SemaphoreType.DMA((4,)),
            pltpu.SemaphoreType.DMA((len(ins),)),
            pltpu.SemaphoreType.DMA((len(out_names),)),
        ]
        + ([] if backward else [VMEM((3, 4, 8, BLOCK, features), BF16)]),
        compiler_params=pltpu.CompilerParams(vmem_limit_bytes=VMEM_LIMIT),
        cost_estimate=cost(6 * forward + 12 * backward),
        name="ffn_" + ("f" if forward else "") + ("b" if backward else ""),
    )(order, vec, *weights, *ins.values())


def attn_backward_body(
    first,
    count,
    places,
    whole_step,
    order_ref,
    e_ref,
    do_ref,
    qkv_ref,
    x_ref,
    gm_ref,
    *refs,
):
    if whole_step:
        weights, refs = refs[:8], refs[8:]
        gm_out, dvec_out, *grads, w_ref, dqkv_s, ds_s, g_s, sem, sem_g = refs
    else:
        dqkv_s, dvec_out, *grads, ds_s, g_s, sem_g = refs
    step = pl.program_id(0)
    tokens, features = x_ref.shape
    lane = lax.broadcasted_iota(jnp.int32, (tokens, 128), 1)
    low_half = lane < HEAD_DIM
    column = lane % HEAD_DIM
    width = 128 * count

    if whole_step:

        @pl.when(step == 0)
        def _():
            fetch_attn(order_ref, weights, places, w_ref, sem, pl.ds(first * 128, width))

    query = qkv_ref[0, 0]
    key_t = qkv_ref[1, 0].T
    value = qkv_ref[2, 0]
    chunk = CHUNK
    dquery, dkey, dvalue = [], [], []
    for head in range(2):
        inside = low_half if head == 0 else ~low_half
        ones = jnp.where(column // 2 == 2 * (step + first) + head, 1.0, 0.0).astype(BF16)
        value_aug = jnp.where(inside, value, ones)
        key_head = key_t[head * HEAD_DIM : (head + 1) * HEAD_DIM]
        parts = []
        for start in range(0, tokens, chunk):
            columns = slice(start, start + chunk)
            dchances = mm(value_aug, do_ref[head, columns], NT)
            dscores = (e_ref[head, :, columns].astype(F32) * dchances).astype(BF16)
            ds_s[head, :, columns] = dscores
            parts.append(mm(key_head, dscores, NN))
        dquery.append(jnp.concatenate(parts, axis=1))
        dkey.append(mm(ds_s[head], query, NN))
        dvalue.append(mm(e_ref[head], do_ref[head], NN))
    here = pl.ds(pl.multiple_of(step * 128, 128), 128)
    dqkv_s[0, :, here] = (jnp.concatenate(dquery, axis=0).T * 0.125).astype(BF16)
    dqkv_s[1, :, here] = jnp.where(low_half, dkey[0], dkey[1]).astype(BF16)
    dqkv_s[2, :, here] = jnp.where(low_half, dvalue[0], dvalue[1]).astype(BF16)

    @pl.when(step == count - 1)
    def _():
        x = x_ref[...]
        for part in range(3):
            g_s[16 * part : 16 * part + 16] = (
                mm(x, dqkv_s[part], TN).astype(BF16).reshape((16, 2, BLOCK, width))
            )
        for index, ref in enumerate(grads):
            core = order_ref[AT_CORE] if index == 0 else 1 - order_ref[AT_CORE]
            pltpu.make_async_copy(g_s.at[:, core], ref, sem_g).start()
        if whole_step:
            wait_all(w_ref, sem)
            gm = gm_ref[...]
            for part in range(3):
                gm = gm + mm(dqkv_s[part], w_ref[part].reshape(features, width), NT)
            gm_out[...] = gm
        dvec_out[...] = jnp.zeros_like(dvec_out)
        column_sum(dvec_out, 0, dqkv_s[0])
        column_sum(dvec_out, 1, dqkv_s[2])
        wait_all(g_s, sem_g)


def attn_backward(order, first, count, e, e_first, do, qkv, x, gm, weights, places):
    tokens, features = x.shape
    width = 128 * count
    half = jax.ShapeDtypeStruct((16 * 3, BLOCK, width), BF16)
    whole_step = weights is not None
    operands = [order, e, do, qkv, x] + ([gm, *weights] if whole_step else [x])
    in_specs = [
        whole(pltpu.SMEM),
        pl.BlockSpec((2, tokens, tokens), lambda step: (step + e_first, 0, 0)),
        pl.BlockSpec((2, tokens, 128), lambda step: (step + first, 0, 0)),
        pl.BlockSpec((3, 1, tokens, 128), lambda step: (0, step + first, 0, 0)),
        fixed(x.shape),
    ]
    scratch = [
        VMEM((2, tokens, tokens), BF16),
        VMEM((16 * 3, 2, BLOCK, width), BF16),
    ]
    if whole_step:
        in_specs += [fixed(gm.shape)] + [whole(pltpu.HBM)] * len(weights)
        result = jax.ShapeDtypeStruct((tokens, features), F32)
        scratch = [VMEM((3, 4, 8, BLOCK, width), BF16), VMEM((3, tokens, width), BF16)] + scratch
        scratch.append(pltpu.SemaphoreType.DMA)
    else:
        in_specs.append(whole(ANY))
        result = jax.ShapeDtypeStruct((3, tokens, width), BF16)
    return pl.pallas_call(
        functools.partial(attn_backward_body, first, count, places, whole_step),
        grid=(count,),
        out_shape=(result, jax.ShapeDtypeStruct((8, width), F32), half, half),
        in_specs=in_specs,
        out_specs=(fixed(result.shape), fixed((8, width))) + (whole(ANY),) * 2,
        scratch_shapes=scratch + [pltpu.SemaphoreType.DMA],
        compiler_params=pltpu.CompilerParams(vmem_limit_bytes=VMEM_LIMIT),
        cost_estimate=cost(26),
        name="attn_backward",
    )(*operands)


def input_gradient(order, dqkv, dz, weights, places):
    tokens, features = dz.shape
    tile = tokens // 4

    def body(order_ref, dqkv_ref, dz_ref, *refs):
        parts, (out, w_ref, sem) = refs[:8], refs[8:]

        @pl.when(pl.program_id(0) == 0)
        def _():
            fetch_attn(order_ref, parts, places, w_ref, sem, pl.ds(0, features))
            wait_all(w_ref, sem)

        total = dz_ref[...]
        for part in range(3):
            total = total + mm(dqkv_ref[part], w_ref[part].reshape(features, features), NT)
        out[...] = total

    return pl.pallas_call(
        body,
        grid=(4,),
        out_shape=jax.ShapeDtypeStruct((tokens, features), F32),
        in_specs=[
            whole(pltpu.SMEM),
            pl.BlockSpec((3, tile, features), lambda step: (0, step, 0)),
            rows_of(tile, features),
        ]
        + [whole(pltpu.HBM)] * len(weights),
        out_specs=rows_of(tile, features),
        scratch_shapes=[
            VMEM((3, 4, 8, BLOCK, features), BF16),
            pltpu.SemaphoreType.DMA,
        ],
        compiler_params=pltpu.CompilerParams(vmem_limit_bytes=VMEM_LIMIT),
        cost_estimate=cost(4),
        name="input_gradient",
    )(order, dqkv, dz, *weights)


def blocks_of(matrix, features):
    rows, columns = matrix.shape
    shaped = matrix.reshape(rows // BLOCK, BLOCK, columns // features, features)
    return shaped.transpose(0, 2, 1, 3)


def matrix_of(blocks):
    rows, columns, block, features = blocks.shape
    return blocks.transpose(0, 2, 1, 3).reshape(rows * block, columns * features)


CORE, X, Y, Z = 1, 2, 4, 8
Z_MASKS = (0, Z, 2 * Z, 3 * Z)
PLANE_MASKS = (0, X, Y, X | Y)
LOW_MASKS = [
    core | second | first
    for high, low in ((X, Y), (Y, X))
    for core in (0, CORE)
    for second in (0, high)
    for first in (0, low)
]


def swap(part, mask):
    return lax.ppermute(part, AXES, [(device, device ^ mask) for device in range(32)])


def after(value, *earlier):
    return lax.optimization_barrier((value, earlier))[0]


def prepare(place, in_w, out_w, up_w, down_w, vectors, final_norm):
    _, block, features = out_w.shape
    groups = up_w.shape[2] // features
    width, spread = vectors.shape[1], final_norm.shape[0]

    def body(place_ref, in_ref, out_ref, up_ref, down_ref, vec_ref, last_ref, *refs):
        own, rows = refs[:3], refs[3]
        rows[...] = jnp.zeros_like(rows)
        rows[0:2, :width] = vec_ref[...].astype(F32)
        rows[8:9, :spread] = last_ref[...].astype(F32)
        field = rows[0:8, :256]
        field = jnp.where(place_ref[AT_FIELDS] == 0, field, pltpu.roll(field, 64, 1))
        last = rows[8:16, :128]
        chosen = last
        for turn in range(1, 128 // spread):
            turned = pltpu.roll(last, turn * spread, 1)
            chosen = jnp.where(place_ref[AT_FIELDS + 1] == turn * spread, turned, chosen)
        rows[...] = jnp.zeros_like(rows)
        rows[0:1, :256] = field[0:1]
        rows[0:1, 256:512] = field[1:2]
        rows[1:2, :128] = chosen[0:1]
        parts = lambda ref, layer, count: [
            ref[layer, :, features * j : features * (j + 1)] for j in range(count)
        ]
        qkv = [parts(in_ref, layer, 3) for layer in range(2)]
        up = [parts(up_ref, layer, groups) for layer in range(2)]
        down = [
            [down_ref[layer, block * j : block * (j + 1)] for j in range(groups)]
            for layer in range(2)
        ]
        out = [out_ref[layer] for layer in range(2)]
        laid = [
            qkv[0] + [rows[...].astype(BF16)],
            qkv[1][:2] + up[0] + qkv[1][2:] + [out[0]] + down[0],
            up[1] + [out[1]] + down[1],
        ]
        for ref, pieces in zip(own, laid):
            for index, piece in enumerate(pieces):
                ref[index] = piece

    outs = [(count, block, features) for count in (4, 2 * groups + 4, 2 * groups + 1)]
    operands = (in_w, out_w, up_w, down_w, vectors, final_norm[None])
    return pl.pallas_call(
        body,
        grid=(1,),
        out_shape=tuple(jax.ShapeDtypeStruct(shape, BF16) for shape in outs),
        in_specs=[whole(pltpu.SMEM)] + [fixed(part.shape) for part in operands],
        out_specs=tuple(fixed(shape) for shape in outs),
        scratch_shapes=[VMEM((block, features), F32)],
        compiler_params=pltpu.CompilerParams(vmem_limit_bytes=VMEM_LIMIT),
        name="prepare",
    )(place, *operands)


def gather_z(own):
    return [hold(own)] + [swap(own, mask) for mask in Z_MASKS[1:]]


def pack_z(place, pieces):
    blocks, *rest = pieces[0].shape

    def body(place_ref, *refs):
        for index in range(4):
            refs[4][:, place_ref[AT_Z] ^ index] = refs[index][...]

    return pl.pallas_call(
        body,
        out_shape=jax.ShapeDtypeStruct((blocks, 4, *rest), BF16),
        in_specs=[whole(pltpu.SMEM)] + [whole()] * 4,
        out_specs=whole(),
        compiler_params=pltpu.CompilerParams(vmem_limit_bytes=SMALL_VMEM),
        name="pack_z",
    )(place, *pieces)


def gather_first(four, cut):
    streams = (four[:cut], Y, X), (four[cut:], X, Y)
    return [(part, swap(part, first), second) for part, first, second in streams]


def gather_second(streams, near):
    return [swap(part, second) for part, (_, _, second) in zip(near, streams)]


def join_two(streams):
    def body(a_ref, b_ref, c_ref, d_ref, out0, out1):
        out0[0], out0[1] = a_ref[...], b_ref[...]
        out1[0], out1[1] = c_ref[...], d_ref[...]

    parts = [part for near, far, _ in streams for part in (near, far)]
    shapes = [(2, *parts[0].shape), (2, *parts[2].shape)]
    return pl.pallas_call(
        body,
        out_shape=tuple(jax.ShapeDtypeStruct(shape, BF16) for shape in shapes),
        in_specs=[whole()] * 4,
        out_specs=(whole(), whole()),
        compiler_params=pltpu.CompilerParams(vmem_limit_bytes=SMALL_VMEM),
        name="join_two",
    )(*parts)


def gather_core(near, far, late):
    near = after(near, far) if late else near
    return [
        part
        for pair in zip(near, far)
        for part in (*pair, *[swap(half, CORE) for half in pair])
    ]


def sum_core(mine, other):
    return hold(mine), swap(other, CORE)


def hold(part):
    def body(in_ref, out_ref, sem):
        copy = pltpu.make_async_copy(in_ref, out_ref, sem)
        copy.start()
        copy.wait()

    return pl.pallas_call(
        body,
        out_shape=jax.ShapeDtypeStruct(part.shape, part.dtype),
        in_specs=[whole(pltpu.HBM)],
        out_specs=whole(),
        scratch_shapes=[pltpu.SemaphoreType.DMA],
        compiler_params=pltpu.CompilerParams(vmem_limit_bytes=SMALL_VMEM),
        cost_estimate=cost(1),
        name="hold",
    )(part)


def sum_plane(place, pairs):
    pairs = [[part.reshape(-1, 4, 4, *part.shape[1:]) for part in pair] for pair in pairs]
    kept, got = zip(*pairs)
    rest = kept[0].shape[3:]
    sizes = [part.shape[0] for part in kept]

    def body(place_ref, *refs):
        outs = refs[2 * len(sizes) :]
        start = 0
        for index, size in enumerate(sizes):
            left, right = refs[index], refs[len(sizes) + index]
            for mask, out in enumerate(outs):
                plane = place_ref[AT_PLANE] ^ mask
                out[start : start + size] = (
                    left[:, :, plane].astype(F32) + right[:, :, plane].astype(F32)
                ).astype(BF16)
            start += size

    return pl.pallas_call(
        body,
        out_shape=(jax.ShapeDtypeStruct((sum(sizes), 4, *rest), BF16),) * 4,
        in_specs=[whole(pltpu.SMEM)] + [whole()] * (2 * len(sizes)),
        out_specs=(whole(),) * 4,
        compiler_params=pltpu.CompilerParams(vmem_limit_bytes=SMALL_VMEM),
        name="sum_plane",
    )(place, *kept, *got)


def send_plane(parts):
    return [parts[0]] + [swap(part, mask) for part, mask in zip(parts[1:], PLANE_MASKS[1:])]


def sum_z(place, parts):
    blocks, _, *rest = parts[0].shape
    count = 3 if blocks % 3 == 0 else 1

    def body(place_ref, *refs):
        for mask in range(4):
            z = place_ref[AT_Z] ^ mask
            total = refs[0][:, z].astype(F32)
            for ref in refs[1:4]:
                total = total + ref[:, z].astype(F32)
            refs[4 + mask][...] = total.astype(BF16)

    return pl.pallas_call(
        body,
        grid=(blocks // count,),
        out_shape=(jax.ShapeDtypeStruct((blocks, *rest), BF16),) * 4,
        in_specs=[whole(pltpu.SMEM)]
        + [pl.BlockSpec((count, 4, *rest), lambda step: (step, 0, 0, 0))] * 4,
        out_specs=(pl.BlockSpec((count, *rest), lambda step: (step, 0, 0)),) * 4,
        compiler_params=pltpu.CompilerParams(vmem_limit_bytes=SMALL_VMEM),
        name="sum_z",
    )(place, *parts)


def send_z(pieces):
    return [pieces[0]] + [swap(piece, mask) for piece, mask in zip(pieces[1:], Z_MASKS[1:])]


def finish(place, ffn1, ffn0, attn0, width, spread):
    _, block, features = ffn1[0].shape
    groups = (ffn1[0].shape[0] - 1) // 2

    def body(place_ref, *refs):
        parts = [refs[:4], refs[4:8], refs[8:12]]
        in_out, out_out, up_out, down_out, vec_out, last_out = refs[12:]

        def total(part, index):
            value = parts[part][0][index].astype(F32)
            for ref in parts[part][1:]:
                value = value + ref[index].astype(F32)
            return value

        for layer, part in ((1, 0), (0, 1)):
            for j in range(groups):
                up_out[layer, :, features * j : features * (j + 1)] = total(part, j)
                down_out[layer, block * j : block * (j + 1)] = total(part, groups + 1 + j)
            out_out[layer] = total(part, groups)
        for layer, part, start in ((1, 1, 2 * groups + 1), (0, 2, 0)):
            for j in range(3):
                in_out[layer, :, features * j : features * (j + 1)] = total(part, start + j)
        rows = total(2, 3)
        for layer in range(2):
            field = rows[0:8, 256 * layer : 256 * layer + 256]
            turned = pltpu.roll(field, 192, 1)
            chosen = jnp.where(place_ref[AT_FIELDS] == 0, field, turned)
            vec_out[layer : layer + 1] = chosen[0:1, :width]
        field = rows[0:8, :128]
        chosen = field
        for turn in range(1, 128 // spread):
            turned = pltpu.roll(field, 128 - turn * spread, 1)
            chosen = jnp.where(place_ref[AT_FIELDS + 1] == turn * spread, turned, chosen)
        last_out[...] = chosen[1:2, :spread]

    shapes = [
        (2, block, 3 * features),
        (2, block, features),
        (2, block, groups * features),
        (2, block * groups, features),
        (2, width),
        (1, spread),
    ]
    return pl.pallas_call(
        body,
        out_shape=tuple(jax.ShapeDtypeStruct(shape, F32) for shape in shapes),
        in_specs=[whole(pltpu.SMEM)] + [whole()] * 12,
        out_specs=tuple(whole() for _ in shapes),
        compiler_params=pltpu.CompilerParams(vmem_limit_bytes=SMALL_VMEM),
        name="finish",
    )(place, *ffn1, *ffn0, *attn0)


def field_of(device, width):
    start = device * width
    return start // 128 * 128, start % 128


def unpack_vectors(order, parts, width, spread):
    def body(order_ref, *refs):
        refs, out, flat, last = refs[:4], *refs[4:]
        flat[...] = jnp.zeros_like(flat)
        last[...] = jnp.zeros_like(last)
        out[...] = jnp.zeros_like(out)
        for index, ref in enumerate(refs):
            for near, z in [(near, z) for near in range(2) for z in range(4)]:
                owner = 8 * z + order_ref[8 + 2 * index + near]
                rows = ref[near, 0, z].astype(F32)
                at = pl.ds(pl.multiple_of(owner * width // 128 * 128, 128), 256)
                for layer in range(2):
                    flat[layer : layer + 1, at] += rows[0:1, 256 * layer : 256 * layer + 256]
                at = pl.ds(pl.multiple_of(owner * spread // 128 * 128, 128), 128)
                last[0:1, at] += rows[1:2, :128]
        for layer in range(2):
            for row in range(12):
                out[layer, row : row + 1] = flat[layer : layer + 1, row * 512 : row * 512 + 512]
            for row in range(2):
                out[layer, 12 + row : 13 + row] = last[0:1, row * 512 : row * 512 + 512]

    features = parts[0].shape[-1]
    at = parts[0].shape[1] - 1
    return pl.pallas_call(
        body,
        grid=(1,),
        out_shape=jax.ShapeDtypeStruct((2, 16, features), F32),
        in_specs=[whole(pltpu.SMEM)]
        + [
            pl.BlockSpec((2, 1, *part.shape[2:]), lambda step: (0, at, 0, 0, 0)) for part in parts
        ],
        out_specs=fixed((2, 16, features)),
        scratch_shapes=[VMEM((8, 12 * features), F32), VMEM((8, 2 * features), F32)],
        compiler_params=pltpu.CompilerParams(vmem_limit_bytes=SMALL_VMEM),
        name="unpack_vectors",
    )(order, *parts)


def pack_vectors(order, attn_rows, ffn_rows, width, spread):
    features = ffn_rows[0].shape[1]

    def body(order_ref, a0, a1, f0, f1, out0, out1, flat, last):
        for layer, (attn, ffn) in enumerate(((a0, f0), (a1, f1))):
            for row in range(12):
                source = attn if row < 2 else ffn
                flat[layer : layer + 1, row * 512 : row * 512 + 512] = source[row : row + 1]
        for row in range(2):
            last[0:1, row * 512 : row * 512 + 512] = f1[12 + row : 13 + row]
        for half, out in enumerate((out0, out1)):
            out[...] = jnp.zeros_like(out)
            core = order_ref[AT_CORE] if half == 0 else 1 - order_ref[AT_CORE]
            for pair in range(16):
                owner = 2 * pair + core
                at = pl.ds(pl.multiple_of(owner * width // 128 * 128, 128), 256)
                fields = [flat[layer : layer + 1, at] for layer in range(2)]
                at = pl.ds(pl.multiple_of(owner * spread // 128 * 128, 128), 128)
                final = jnp.concatenate([last[0:1, at], jnp.zeros((1, 384), F32)], axis=1)
                rows = [jnp.concatenate(fields, axis=1), final, jnp.zeros((BLOCK - 2, 512), F32)]
                out[pair] = jnp.concatenate(rows, axis=0).astype(BF16)

    return pl.pallas_call(
        body,
        out_shape=(jax.ShapeDtypeStruct((16, BLOCK, features), BF16),) * 2,
        in_specs=[whole(pltpu.SMEM)] + [whole()] * 4,
        out_specs=(whole(), whole()),
        scratch_shapes=[VMEM((8, 12 * features), F32), VMEM((8, 2 * features), F32)],
        compiler_params=pltpu.CompilerParams(vmem_limit_bytes=SMALL_VMEM),
        name="pack_vectors",
    )(order, *attn_rows, *ffn_rows)


def total_of(pieces):
    total = pieces[0].astype(F32)
    for piece in pieces[1:]:
        total = total + piece.astype(F32)
    return total


def local(
    main_residual,
    side_residual,
    cotangent,
    lengths,
    input_weight,
    output_weight,
    expand_weight,
    reduce_weight,
    vectors,
    final_norm,
):
    tokens, features = main_residual.shape
    layers = input_weight.shape[0]
    assert lengths.shape[0] == 1 and layers == 2
    per = features // BLOCK
    pairs = features // 128
    half_pairs = pairs // 2
    groups = expand_weight.shape[2] // features
    fast = lax.axis_size(AXES) == 32 and per == 32
    ffn_at = ((2, (1, 1), 2), (0, (0, groups), 0))
    width = vectors.shape[1]
    spread = final_norm.shape[0]

    def vec_rows(all_vectors, final_full):
        return jnp.concatenate(
            [
                all_vectors.reshape(layers, 12, features),
                jnp.broadcast_to(final_full.reshape(1, 2, features), (layers, 2, features)),
                jnp.zeros((layers, 2, features), F32),
            ],
            axis=1,
        )

    if fast:
        me = lax.axis_index(AXES)
        table = [
            [(device ^ mask) & 7 for mask in LOW_MASKS]
            + [device // Z, device // X & 3, device & CORE]
            + [field_of(device, width)[1], field_of(device, spread)[1]]
            for device in range(32)
        ]
        order = jnp.array(table, jnp.int32)[me]
        own = prepare(
            order, input_weight, output_weight, expand_weight, reduce_weight, vectors, final_norm
        )
        z0 = gather_z(own[0])
        z1 = gather_z(after(own[1], z0[1:]))
        two = gather_first(pack_z(order, z0), 2)
        near = join_two(two)
        far = gather_second(two, near)
        attn0 = gather_core(near, far, True)
        vec = unpack_vectors(order, attn0[4:], width, spread)
        four = pack_z(order, after(z1, near))
        two = gather_first(after(four, far[0]), groups + 2)
        two = [(part, after(got, vec), mask) for part, got, mask in two]
        z2 = gather_z(after(own[2], attn0))
        near = join_two(two)
        far = gather_second(two, near)
        x0 = after(main_residual, near)
    else:
        gather = lambda part, axis: lax.all_gather(part, AXES, axis=axis, tiled=True)
        order = jnp.array(LOW_MASKS + [0] * 5, jnp.int32)

        def streams(*two):
            parts = []
            for stream, blocks in enumerate(two):
                joined = jnp.concatenate(blocks, axis=1)
                joined = joined.reshape(4, 8, *joined.shape[1:]).transpose(1, 2, 0, 3, 4)
                lows = LOW_MASKS[8 * stream : 8 * stream + 8]
                parts += [joined[jnp.array(lows[at : at + 2])] for at in range(0, 8, 2)]
            return parts

        vec = vec_rows(gather(vectors, 1).astype(F32), gather(final_norm, 0).astype(F32))
        parts = []
        for layer in range(layers):
            qkv = blocks_of(gather(input_weight[layer], 0), features)
            up = blocks_of(gather(expand_weight[layer], 0), features)
            out = blocks_of(gather(output_weight[layer], 0), features)
            down = gather(reduce_weight[layer], 0).reshape(per, -1, BLOCK, features)
            parts.append((qkv, up, out, down))
        (qkv0, up0, out0, down0), (qkv1, up1, out1, down1) = parts
        attn0 = streams([qkv0[:, :2]], [qkv0[:, 2:]])
        mixed = streams([qkv1[:, :2], up0], [qkv1[:, 2:], out0, down0])
        ffn1 = streams([up1, out1], [down1])
        x0 = main_residual

    e0, ctx0, rinv0, qkv0 = attn_forward(
        lengths, 0, pairs, None, order, x0, vec, attn0, 0, 0
    )
    x0 = main_residual
    if fast:
        far, z2 = after((far, z2), e0)
        mixed = gather_core(near, far, True)
        two = gather_first(pack_z(order, z2), groups + 1)
        x0 = after(x0, *[part for part, _, _ in two])
    xh1, xh2, stat, m1b, hid, m2, m2b, y, qkv1 = ffn_call(
        True, False, False, 0, order, vec, mixed, ffn_at[0], ctx0, (x0, side_residual)
    )
    if fast:
        two = [(part, after(got, m2b), mask) for part, got, mask in two]
        near = join_two(two)
        qkv1 = after(qkv1, near)
        far = gather_second(two, near)
    e1, ctx1, rinv1 = attn_forward(lengths, 0, pairs, qkv1)
    if fast:
        ffn1 = gather_core(near, after(far, e1), False)
    layer_out, grad_side, gm, do, dvec1, *gf1 = ffn_call(
        True, True, True, 1, order, vec, ffn1, ffn_at[1], ctx1, (m2, y, cotangent), rinv1
    )
    if fast:
        f1 = sum_plane(order, [sum_core(*gf1)])
        gm = after(gm, f1)
        f1 = send_plane(f1)
    gm, dvec1a, *gi1 = attn_backward(
        order, 0, pairs, e1, 0, do, qkv1, m2b, gm, mixed, 0
    )
    if fast:
        i1 = (gi1[0], swap(gi1[1], CORE))
        f1 = sum_z(order, after(f1, gm))
        gm = after(gm, f1)
        f1 = send_z(f1)
    gm, do, dvec0, *gf0 = ffn_call(
        False, True, False, 0, order, vec, mixed, ffn_at[0], ctx0,
        (xh1, xh2, stat, m1b, hid, gm, grad_side), rinv0,
    )
    if fast:
        f1, i1 = after((f1, i1), gm)
        f0 = sum_plane(order, [sum_core(*after(gf0, f1)), (hold(i1[0]), i1[1])])
        do = after(do, f0)
        f0 = send_plane(f0)
    dqkv, dvec0a, *gi0 = attn_backward(
        order, 0, pairs, e0, 0, do, qkv0, main_residual, None, None, 0
    )
    if fast:
        rows = pack_vectors(order, (dvec0a, dvec1a), (dvec0, dvec1), width, spread)
        i0 = [sum_core(*gi0), sum_core(*rows)]
        f0 = send_z(sum_z(order, after(f0, dqkv)))
        i0 = send_plane(sum_plane(order, after(i0, f0[0])))
        gm, dqkv = after((gm, dqkv), f0[0], i0[0])
        grad_main = input_gradient(order, dqkv, gm, attn0, 0)
        i0 = send_z(sum_z(order, after(i0, grad_main)))
        grad_in, grad_out, grad_up, grad_down, grad_vec, grad_final = finish(
            order, f1, f0, i0, width, spread
        )
        grad_final = grad_final[0]
    else:
        grad_main = input_gradient(order, dqkv, gm, attn0, 0)
        scatter = lambda part, axis: lax.psum_scatter(
            part, AXES, scatter_dimension=axis, tiled=True
        ).astype(F32)

        def natural(even, odd):
            joined = jnp.stack([even, odd], axis=1)
            return joined.reshape(-1, per, *even.shape[1:]).swapaxes(0, 1)

        both = lambda make: jnp.stack(
            [make(natural(*i), natural(*f)) for i, f in ((gi0, gf0), (gi1, gf1))]
        )
        grad_in = scatter(both(lambda i, f: matrix_of(i)), 1)
        grad_up = scatter(both(lambda i, f: matrix_of(f[:, :groups])), 1)
        grad_out = scatter(both(lambda i, f: matrix_of(f[:, groups : groups + 1])), 1)
        grad_down = scatter(both(lambda i, f: f[:, groups + 1 :].reshape(-1, features)), 1)
        dvec = [
            jnp.concatenate([first[0:2], rest[2:12]]).reshape(-1)
            for first, rest in ((dvec0a, dvec0), (dvec1a, dvec1))
        ]
        grad_vec = scatter(jnp.stack(dvec), 1)
        grad_final = scatter(dvec1[12:14].reshape(-1), 0)
    return (
        layer_out,
        grad_main,
        grad_side,
        grad_in,
        grad_out,
        grad_up,
        grad_down,
        grad_vec,
        grad_final,
    )


def solution(mesh):
    rows = P(AXES, None)
    middle = P(None, AXES, None)
    return jax.shard_map(
        local,
        mesh=mesh,
        in_specs=(rows, rows, rows, rows, middle, middle, middle, middle, P(None, AXES), P(AXES)),
        out_specs=(rows, rows, rows, middle, middle, middle, middle, P(None, AXES), P(AXES)),
        check_vma=False,
    )
```

```python
import functools

import jax
import jax.numpy as jnp
from jax import lax
from jax.experimental import pallas as pl
from jax.experimental.pallas import tpu as pltpu
from jax.sharding import PartitionSpec as P

HEAD_DIM = 64
AXES = ("wide", "narrow")
F32 = jnp.float32
BF16 = jnp.bfloat16
NN = (((1,), (0,)), ((), ()))
NT = (((1,), (1,)), ((), ()))
TN = (((0,), (0,)), ((), ()))
MASKED = -1000000000.0
VMEM_LIMIT = 60 * 2**20
SMALL_VMEM = 24 * 2**20


def cost(microseconds):
    return pl.CostEstimate(
        flops=microseconds * 10**9, bytes_accessed=microseconds * 10**6, transcendentals=0
    )


BLOCK = 16
CHUNK = 512
TILE = 256
ROWS = 64
VMEM = pltpu.VMEM
ANY = pl.ANY


def mm(left, right, dims):
    return lax.dot_general(left, right, dims, preferred_element_type=F32)


def whole(memory=VMEM):
    return pl.BlockSpec(memory_space=memory)


def fixed(shape):
    zeros = (0,) * len(shape)
    return pl.BlockSpec(shape, lambda step: zeros)


def rows_of(tile, width):
    return pl.BlockSpec((tile, width), lambda step: (step, 0))


AT_Z, AT_PLANE, AT_CORE, AT_FIELDS = 16, 17, 18, 19


def each_part(place_ref, weights, stream):
    return [
        (weights[index].at[near], place_ref[2 * index + near])
        for index in range(4 * stream, 4 * stream + 4)
        for near in range(2)
    ]


def wait_all(ref, sem):
    pltpu.make_async_copy(ref, ref, sem).wait()


def fetch_attn(order_ref, weights, at, w_ref, sem, columns):
    for ref, low in each_part(order_ref, weights, 0):
        pltpu.make_async_copy(
            ref.at[pl.ds(at, 2), :, :, columns], w_ref.at[pl.ds(0, 2), :, low], sem
        ).start()
    for ref, low in each_part(order_ref, weights, 1):
        pltpu.make_async_copy(ref.at[at, :, :, columns], w_ref.at[2, :, low], sem).start()


def project(x, w_ref, vec_ref, layer, part):
    features = x.shape[1]
    packed = mm(x, w_ref[part].reshape(features, features), NN)
    if part == 0:
        return (packed + vec_ref[layer, 0:1]).astype(BF16) * BF16(0.125)
    if part == 2:
        packed = packed + vec_ref[layer, 1:2]
    return packed.astype(BF16)


def attn_forward_body(first, count, places, layer, *refs):
    refs = list(refs)
    take = lambda: refs.pop(0)
    bounds_ref = take()
    if places is not None:
        order_ref, x_ref, vec_ref = take(), take(), take()
        weights = [take() for _ in range(8)]
        e_ref, ctx_ref, rinv_ref, qkv_ref, aux_ref, rows_ref, w_ref, sem = refs
        at = pl.program_id(0) + first
    else:
        qkv_ref, e_ref, ctx_ref, rinv_ref, aux_ref, rows_ref = refs
        at = 0
    step = pl.program_id(0)
    tokens = ctx_ref.shape[0]
    lane = lax.broadcasted_iota(jnp.int32, (tokens, 128), 1)
    low_half = lane < HEAD_DIM

    @pl.when(step == 0)
    def _():
        if places is not None:
            features = x_ref.shape[1]
            fetch_attn(order_ref, weights, places, w_ref, sem, pl.ds(0, features))
        token = lax.broadcasted_iota(jnp.int32, (tokens, 128), 0)
        column = lane % HEAD_DIM
        single = bounds_ref[0, 1] == 0
        quarter = tokens // 4
        segment = jnp.where(single, 0, token // quarter)
        inside = jnp.where(single, token, token % quarter)
        own = column == segment
        bound = jnp.where(
            segment == 0,
            bounds_ref[0, 0],
            jnp.where(
                segment == 1,
                bounds_ref[0, 1],
                jnp.where(segment == 2, bounds_ref[0, 2], bounds_ref[0, 3]),
            ),
        )
        alive = own & (inside < bound)
        aux_ref[0] = jnp.where(own, 1.0, 0.0).astype(BF16)
        aux_ref[1] = jnp.where(alive | (column >= 4), 0.0, MASKED).astype(BF16)
        rows_ref[...] = jnp.zeros_like(rows_ref)
        if places is not None:
            wait_all(w_ref, sem)
            x = x_ref[...]
            for part in range(3):
                packed = project(x, w_ref, vec_ref, layer, part)
                for index in range(features // 128):
                    qkv_ref[part, index] = packed[:, index * 128 : (index + 1) * 128]

    query = qkv_ref[0, at]
    key = qkv_ref[1, at]
    value_t = qkv_ref[2, at].T
    ones = jnp.ones((16, tokens), BF16)
    chunk = CHUNK

    def heads(shifted):
        outs, sums = [], []
        for head in range(2):
            inside_head = low_half if head == 0 else ~low_half
            query_aug = jnp.where(inside_head, query, aux_ref[0])
            key_aug = jnp.where(inside_head, key, aux_ref[1])
            value_aug = jnp.concatenate(
                [value_t[head * HEAD_DIM : (head + 1) * HEAD_DIM], ones], axis=0
            )
            parts = []
            for start in range(0, tokens, chunk):
                scores = mm(key_aug, query_aug[start : start + chunk], NT)
                if shifted:
                    scores = scores - jnp.max(scores, axis=0, keepdims=True)
                exponent = jnp.exp(scores).astype(BF16)
                e_ref[head, :, start : start + chunk] = exponent
                mixed = mm(value_aug, exponent, NN)
                total = mixed[HEAD_DIM : HEAD_DIM + 1]
                inverse = 1.0 / total
                rows_ref[pl.ds(step * 2 + head, 1), start : start + chunk] = inverse
                parts.append(mixed[:HEAD_DIM] * inverse)
                sums.append(total)
            outs.append(jnp.concatenate(parts, axis=1))
        ctx_ref[...] = jnp.concatenate(outs, axis=0).T.astype(BF16)
        return jnp.concatenate(sums, axis=1)

    sums = heads(False)
    fits = (jnp.max(sums) <= 2.0**40) & (jnp.min(sums) >= 2.0**-40)

    @pl.when(jnp.logical_not(fits))
    def _():
        heads(True)

    @pl.when(step == pl.num_programs(0) - 1)
    def _():
        inverses = rows_ref[...].T
        high = inverses.astype(BF16).astype(F32)
        low = pltpu.roll(inverses - high, 2 * count, 1)
        rinv_ref[...] = (high + low).astype(BF16)


def attn_forward(bounds, first, count, qkv=None, order=None, x=None, vec=None, weights=(), places=None, layer=0):
    project = places is not None
    if project:
        tokens, features = x.shape
        pairs = features // 128
    else:
        _, pairs, tokens, _ = qkv.shape
    out_shape = [
        jax.ShapeDtypeStruct((2 * count, tokens, tokens), BF16),
        jax.ShapeDtypeStruct((tokens, 128 * count), BF16),
        jax.ShapeDtypeStruct((tokens, 128), BF16),
    ]
    out_specs = [
        pl.BlockSpec((2, tokens, tokens), lambda step: (step, 0, 0)),
        pl.BlockSpec((tokens, 128), lambda step: (0, step)),
        fixed((tokens, 128)),
    ]
    scratch = [VMEM((2, tokens, 128), BF16), VMEM((128, tokens), F32)]
    if project:
        operands = (bounds, order, x, vec, *weights)
        in_specs = [whole(pltpu.SMEM), whole(pltpu.SMEM), fixed(x.shape), fixed(vec.shape)]
        in_specs += [whole(pltpu.HBM)] * len(weights)
        out_shape.append(jax.ShapeDtypeStruct((3, pairs, tokens, 128), BF16))
        out_specs.append(fixed((3, pairs, tokens, 128)))
        scratch += [
            VMEM((3, 4, features // BLOCK // 4, BLOCK, features), BF16),
            pltpu.SemaphoreType.DMA,
        ]
    else:
        operands = (bounds, qkv)
        in_specs = [
            whole(pltpu.SMEM),
            pl.BlockSpec((3, 1, tokens, 128), lambda step: (0, step + first, 0, 0)),
        ]
    return pl.pallas_call(
        functools.partial(attn_forward_body, first, count, places, layer),
        grid=(count,),
        out_shape=tuple(out_shape),
        in_specs=in_specs,
        out_specs=tuple(out_specs),
        scratch_shapes=scratch,
        compiler_params=pltpu.CompilerParams(vmem_limit_bytes=VMEM_LIMIT),
        cost_estimate=cost(14),
        name="attn_forward",
    )(*operands)


def normed(z):
    centered = z - jnp.mean(z, axis=-1, keepdims=True)
    variance = jnp.mean(centered * centered, axis=-1, keepdims=True)
    rstd = lax.rsqrt(variance + 1e-05)
    return centered * rstd, rstd


def norm_back(grad, gain, xhat, rstd):
    scaled = grad * gain
    first = jnp.mean(scaled, axis=-1, keepdims=True)
    second = jnp.mean(scaled * xhat, axis=-1, keepdims=True)
    return rstd * (scaled - first - xhat * second)


GELU_A = 0.7978845608028654
GELU_B = 0.044715


def gelu(hidden, sloped):
    square = hidden * hidden
    tanh = jnp.tanh(hidden * (BF16(GELU_A) + BF16(GELU_A * GELU_B) * square))
    chance = BF16(0.5) + BF16(0.5) * tanh
    active = hidden * chance
    if not sloped:
        return active
    inner = BF16(GELU_A) + BF16(3.0 * GELU_A * GELU_B) * square
    return active, chance + active * (BF16(1.0) - tanh) * inner


def column_sum(ref, row, values):
    ref[row : row + 1] += jnp.sum(values.astype(F32), axis=0, keepdims=True)


def weave(vector_work, matrix_work):
    done = 0
    for index, work in enumerate(vector_work):
        work()
        target = (index + 1) * len(matrix_work) // len(vector_work)
        for matrix in matrix_work[done:target]:
            matrix()
        done = target
    for matrix in matrix_work[done:]:
        matrix()


def ffn_body(mode, layer, places, in_names, out_names, scratch_names, *refs):
    forward, backward, last = mode
    refs = list(refs)
    take = lambda count: [refs.pop(0) for _ in range(count)]
    up_at, (out_stream, out_at), down_at = places
    order_ref, vec_ref = take(2)
    weights = take(8)
    ins = dict(zip(in_names, take(len(in_names))))
    outs = dict(zip(out_names, take(len(out_names))))
    if backward:
        dvec_out, *grads = take(3)
    here = dict(zip(scratch_names, take(len(scratch_names))))
    wo_ref, up_ref, down_ref, sem_w, sem_in, sem_out = take(6)
    if not backward:
        (next_ref,) = take(1)
    assert not refs
    tokens = here["ctx"].shape[0]
    features = vec_ref.shape[2]
    groups = up_ref.shape[0]
    per = features // BLOCK
    wo = lambda: wo_ref[...].reshape(features, features)
    up = lambda j, zs: up_ref[j, zs].reshape(-1, features)
    down = lambda j, part: down_ref[j, part].reshape(-1, features)
    every = slice(None)
    up_halves = [slice(0, 2), slice(2, 4)]
    down_halves = [slice(0, 4), slice(4, 8)]
    wide = features // 2
    half_columns = [slice(0, wide), slice(wide, features)]
    of = lambda j: slice(j * features, (j + 1) * features)
    vec = lambda row: vec_ref[layer, row : row + 1]
    copy_in = {
        name: pltpu.make_async_copy(ref, here[name], sem_in.at[index])
        for index, (name, ref) in enumerate(ins.items())
    }
    sem_of = {name: sem_out.at[index] for index, name in enumerate(outs)}

    def leave(*names, rows=slice(None), columns=None):
        for name in names:
            at = (rows,) if columns is None else (rows, columns)
            if name == "do":
                at = (slice(None), rows)
            if name == "qkv":
                at = (slice(None), slice(None), rows)
            pltpu.make_async_copy(
                here[name].at[at], outs[name].at[at], sem_of[name]
            ).start()

    def leave_all():
        for name, ref in outs.items():
            wait_all(here[name], sem_of[name])

    blocks = [slice(start, start + TILE) for start in range(0, tokens, TILE)]
    chunks = [slice(start, start + ROWS) for start in range(0, tokens, ROWS)]

    def fetch_out(ref, low):
        pltpu.make_async_copy(ref.at[out_at], wo_ref.at[:, low], sem_w.at[0]).start()

    def fetch_up(ref, low):
        pltpu.make_async_copy(
            ref.at[pl.ds(up_at, groups)], up_ref.at[:, :, low], sem_w.at[1]
        ).start()

    def fetch_down(ref, low):
        for block in range(groups):
            pltpu.make_async_copy(
                ref.at[down_at + block], down_ref.at[:, low, block], sem_w.at[2]
            ).start()

    early = ("ctx", "x", "y") if forward else ("gm", "gs", "xh2", "stat")
    for name in early:
        copy_in[name].start()
    for fetch in (fetch_out, fetch_up, fetch_down) if forward else (fetch_down, fetch_up, fetch_out):
        stream = {fetch_out: out_stream, fetch_up: 0, fetch_down: 1}[fetch]
        for ref, low in each_part(order_ref, weights, stream):
            fetch(ref, low)
    if not backward:
        fetch_attn(order_ref, weights, 0, next_ref, sem_w.at[3], pl.ds(0, features))
    for name in in_names:
        if name not in early:
            copy_in[name].start()
    waited = set()

    def need(*names):
        for name in names:
            if name not in waited:
                waited.add(name)
                copy_in[name].wait()

    if backward:
        dvec_out[...] = jnp.zeros_like(dvec_out)
    if forward:
        need("ctx", "x", "y")
        wait_all(wo_ref, sem_w.at[0])
        for rows in blocks:
            branch = mm(here["ctx"][rows], wo(), NN) + vec(2)
            xh1, rstd1 = normed(here["x"][rows].astype(F32) + branch)
            m1 = xh1 * vec(3) + vec(4)
            here["m1"][rows] = m1
            here["m1b"][rows] = m1.astype(BF16)
            here["y_new"][rows] = here["y"][rows].astype(F32) + branch
            here["xh1"][rows] = xh1.astype(BF16)
            here["stat"][rows, :64] = jnp.broadcast_to(rstd1, (TILE, 64))
            if not backward:
                leave("xh1", "m1b", rows=rows)
        wait_all(up_ref, sem_w.at[1])

        def hidden_dots(j):
            def piece(rows):
                here["work"][j % 2, rows] = mm(here["m1b"][rows], up(j, every), NN)

            return [functools.partial(piece, rows) for rows in blocks]

        def activate(j):
            def piece(rows):
                hidden = (here["work"][j % 2, rows] + vec(8 + j)).astype(BF16)
                if backward:
                    active, slope = gelu(hidden, True)
                    here["hid"][rows, of(j)] = slope
                else:
                    active = gelu(hidden, False)
                    here["hid"][rows, of(j)] = hidden
                here["act"][rows, of(j)] = active

            return [functools.partial(piece, rows) for rows in chunks]

        def branch_dots(j):
            def piece(rows):
                part = mm(here["act"][rows, of(j)], down(j, every), NN)
                here["sum"][rows] = part + (vec(5) if j == 0 else here["sum"][rows])

            return [functools.partial(piece, rows) for rows in blocks]

        weave([], hidden_dots(0))
        wait_all(down_ref, sem_w.at[2])
        for j in range(groups):
            matrix = hidden_dots(j + 1) if j + 1 < groups else []
            if j > 0:
                matrix = matrix + branch_dots(j - 1)
            weave(activate(j), matrix)
            if not backward:
                leave("hid", columns=of(j))
        weave([], branch_dots(groups - 1))
        if last:
            need("cot")
        if not backward:
            wait_all(next_ref, sem_w.at[3])
        for rows in blocks:
            xh2, rstd2 = normed(here["m1"][rows] + here["sum"][rows])
            m2 = xh2 * vec(6) + vec(7)
            y = here["y_new"][rows] + here["sum"][rows]
            if not backward:
                here["xh2"][rows] = xh2.astype(BF16)
                here["stat"][rows, 64:] = jnp.broadcast_to(rstd2, (TILE, 64))
                here["m2"][rows] = m2
                here["m2b"][rows] = m2.astype(BF16)
                here["y_new"][rows] = y
                leave("xh2", "stat", "m2", "m2b", "y_new", rows=rows)
                continue
            yh, rstdy = normed(y)
            here["layer_out"][rows] = (m2 + yh * vec(12) + vec(13)).astype(BF16)
            gm = here["cot"][rows].astype(F32)
            gs = norm_back(gm, vec(12), yh, rstdy)
            here["gs"][rows] = gs
            column_sum(dvec_out, 12, gm * yh)
            column_sum(dvec_out, 13, gm)
            column_sum(dvec_out, 6, gm * xh2)
            column_sum(dvec_out, 7, gm)
            dz2 = norm_back(gm, vec(6), xh2, rstd2)
            df = (dz2 + gs).astype(BF16)
            column_sum(dvec_out, 5, df)
            here["df"][rows] = df
            here["sum"][rows] = dz2
            leave("layer_out", "gs", rows=rows)
        if not backward:
            for part in range(3):
                packed = project(here["m2b"][...], next_ref, vec_ref, layer + 1, part)
                for index in range(features // 128):
                    here["qkv"][part, index] = packed[:, index * 128 : (index + 1) * 128]
            leave("qkv")
            leave_all()
            return
    else:
        need("gm", "gs", "xh2", "stat")
        for rows in blocks:
            gm = here["gm"][rows]
            xh2 = here["xh2"][rows].astype(F32)
            column_sum(dvec_out, 6, gm * xh2)
            column_sum(dvec_out, 7, gm)
            dz2 = norm_back(gm, vec(6), xh2, here["stat"][rows, 64:65])
            df = (dz2 + here["gs"][rows]).astype(BF16)
            column_sum(dvec_out, 5, df)
            here["df"][rows] = df
            here["sum"][rows] = dz2
        wait_all(down_ref, sem_w.at[2])

    def back_dots(j):
        def piece(rows, columns):
            here["work"][j % 2, :, columns] = mm(here["df"][...], down(j, rows), NT)

        return [functools.partial(piece, *part) for part in zip(down_halves, half_columns)]

    def activate_back(j):
        def piece(rows):
            dactive = here["work"][j % 2, rows].astype(BF16)
            slope = here["hid"][rows, of(j)]
            if not forward:
                active, slope = gelu(slope, True)
                here["act"][rows, of(j)] = active
            dhidden = slope * dactive
            here["hid"][rows, of(j)] = dhidden
            column_sum(dvec_out, 8 + j, dhidden)

        return [functools.partial(piece, rows) for rows in chunks]

    def main_dots(j):
        def piece(rows, columns):
            here["sum"][:, columns] += mm(here["hid"][:, of(j)], up(j, rows), NT)

        return [functools.partial(piece, *part) for part in zip(up_halves, half_columns)]

    gup, gdown, gout = here["gup"], here["gdown"], here["gout"]

    def down_grads(j):
        def piece(index, columns):
            rows = slice(j * features + columns.start, j * features + columns.stop)
            gdown[4 * j + 2 * index : 4 * j + 2 * index + 2] = (
                mm(here["act"][:, rows], here["df"][...], TN)
                .astype(BF16)
                .reshape(2, 2, groups, BLOCK, features)
            )

        return [functools.partial(piece, *part) for part in enumerate(half_columns)]

    def up_grads(j):
        def piece(columns):
            source = slice(j * features + columns.start, j * features + columns.stop)
            gup[16 * j : 16 * j + 16, :, :, columns] = (
                mm(here["m1b"][...], here["hid"][:, source], TN)
                .astype(BF16)
                .reshape(16, 2, BLOCK, wide)
            )

        return [functools.partial(piece, columns) for columns in half_columns]

    weave([], back_dots(0))
    if not forward:
        need("hid")
    for j in range(groups):
        if not forward and j == 1:
            wait_all(up_ref, sem_w.at[1])
        matrix = back_dots(j + 1) if j + 1 < groups else []
        if j > 0:
            matrix = matrix + main_dots(j - 1) + down_grads(j - 1)
        weave(activate_back(j), matrix)
    weave([], main_dots(groups - 1))
    need(*in_names)
    if not forward:
        wait_all(wo_ref, sem_w.at[0])

    lane = lax.broadcasted_iota(jnp.int32, (TILE, 128), 1)
    low_half = lane < HEAD_DIM
    column = lane % HEAD_DIM

    def norm_one(rows):
        gm = here["sum"][rows]
        xh1 = here["xh1"][rows].astype(F32)
        column_sum(dvec_out, 3, gm * xh1)
        column_sum(dvec_out, 4, gm)
        dz1 = norm_back(gm, vec(3), xh1, here["stat"][rows, 0:1])
        here["dz1"][rows] = dz1
        da = (dz1 + here["gs"][rows]).astype(BF16)
        column_sum(dvec_out, 2, da)
        here["da"][rows] = da
        leave("dz1", rows=rows)

    heads = features // HEAD_DIM
    iota = lambda shape, axis: lax.broadcasted_iota(jnp.int32, shape, axis)
    if backward:
        mark = lambda picked: jnp.where(picked, 1.0, 0.0).astype(BF16)
        shape = (features, 128)
        place = mark(iota(shape, 1) % HEAD_DIM // 2 == iota(shape, 0) // HEAD_DIM)
        part = iota((128, 128), 0)
        part = jnp.where(part < 2 * heads, part % heads, heads)
        turn = mark(iota((128, 128), 1) % HEAD_DIM // 2 == part)
        shape = (128, features)
        part = iota(shape, 0)
        part = jnp.where(part < 2 * heads, part % heads, heads)
        share = mark(iota(shape, 1) // HEAD_DIM == part)

    def context_one(rows):
        dctx = mm(here["da"][rows], wo(), NT)
        product = dctx * here["ctx"][rows].astype(F32)
        high = product.astype(BF16)
        low = (product - high.astype(F32)).astype(BF16)
        inverse = here["rinv"][rows]
        dots = -(mm(high, place, NN) + mm(low, place, NN)) * mm(inverse, turn, NN)
        high = dots.astype(BF16).astype(F32)
        extra = jnp.where(column % 2 == 0, high, dots - high).astype(BF16)
        scaled = (dctx * mm(inverse, share, NN)).astype(BF16)
        for at in range(heads):
            pair = slice(at // 2 * 128, at // 2 * 128 + 128)
            inside = low_half if at % 2 == 0 else ~low_half
            here["do"][at, rows] = jnp.where(inside, scaled[:, pair], extra)
        leave("do", rows=rows)

    def send(source, sem):
        for index, ref in enumerate(grads):
            core = order_ref[AT_CORE] if index == 0 else 1 - order_ref[AT_CORE]
            for block, count, part in source(core):
                pltpu.make_async_copy(
                    part, ref.at[pl.ds(16 * block, 16 * count)], sem_w.at[sem]
                ).start()

    matrix = down_grads(groups - 1) + up_grads(0)
    weave([functools.partial(norm_one, rows) for rows in blocks], matrix)
    send(
        lambda core: [
            (groups + 1 + block, 1, gdown.at[:, core, block]) for block in range(groups)
        ],
        2,
    )
    matrix = [piece for j in range(1, groups) for piece in up_grads(j)]
    weave([functools.partial(context_one, rows) for rows in blocks], matrix)
    send(lambda core: [(0, groups, gup.at[:, core])], 1)
    gout[...] = (
        mm(here["ctx"][...], here["da"][...], TN)
        .astype(BF16)
        .reshape(16, 2, BLOCK, features)
    )
    send(lambda core: [(groups, 1, gout.at[:, core])], 0)
    wait_all(gup, sem_w.at[1])
    wait_all(gout, sem_w.at[0])
    wait_all(gdown, sem_w.at[2])
    leave_all()


def ffn_call(forward, backward, last, layer, order, vec, weights, places, ctx, tiled, rinv=None):
    tokens, features = ctx.shape
    groups = 4
    width = groups * features
    per = features // BLOCK
    heads = features // HEAD_DIM
    if forward:
        ins = dict(zip(("ctx", "x", "y", "cot"), (ctx, *tiled)))
    else:
        names = ("ctx", "xh1", "xh2", "stat", "m1b", "hid", "gm", "gs")
        ins = dict(zip(names, (ctx, *tiled)))
    if backward:
        ins["rinv"] = rinv
    square, full = (tokens, features), (tokens, width)
    small = (tokens, 128)
    scratch = {name: (value.shape, value.dtype) for name, value in ins.items()}
    scratch["work"] = ((2, *square), F32)
    scratch["sum"] = (square, F32)
    scratch["act"] = (full, BF16)
    if forward:
        scratch.update(
            m1=(square, F32), m1b=(square, BF16), y_new=(square, F32), xh1=(square, BF16),
            stat=(small, F32), hid=(full, BF16),
        )
    if last:
        scratch.update(layer_out=(square, BF16), gs=(square, F32))
    if forward and not backward:
        scratch.update(
            xh2=(square, BF16), m2=(square, F32), m2b=(square, BF16),
            qkv=((3, features // 128, *small), BF16),
        )
        out_names = ["xh1", "xh2", "stat", "m1b", "hid", "m2", "m2b", "y_new", "qkv"]
    else:
        scratch.update(
            df=(square, BF16), dz1=(square, F32), da=(square, BF16), do=((heads, *small), BF16),
            gup=((16 * groups, 2, BLOCK, features), BF16),
            gdown=((16, 2, groups, BLOCK, features), BF16),
            gout=((16, 2, BLOCK, features), BF16),
        )
        out_names = (["layer_out", "gs"] if last else []) + ["dz1", "do"]
    out_shape = [jax.ShapeDtypeStruct(*scratch[name]) for name in out_names]
    out_specs = [whole(ANY)] * len(out_names)
    if backward:
        half = jax.ShapeDtypeStruct((16 * (2 * groups + 1), BLOCK, features), BF16)
        out_shape += [jax.ShapeDtypeStruct((16, features), F32), half, half]
        out_specs += [whole(), whole(ANY), whole(ANY)]
    return pl.pallas_call(
        functools.partial(
            ffn_body, (forward, backward, last), layer, places, tuple(ins), tuple(out_names),
            tuple(scratch),
        ),
        out_shape=tuple(out_shape),
        in_specs=[whole(pltpu.SMEM), whole()] + [whole(pltpu.HBM)] * (8 + len(ins)),
        out_specs=tuple(out_specs),
        scratch_shapes=[VMEM(*kind) for kind in scratch.values()]
        + [
            VMEM((4, 8, BLOCK, features), BF16),
            VMEM((groups, 4, 8, BLOCK, features), BF16),
            VMEM((4, 8, groups, BLOCK, features), BF16),
            pltpu.SemaphoreType.DMA((4,)),
            pltpu.SemaphoreType.DMA((len(ins),)),
            pltpu.SemaphoreType.DMA((len(out_names),)),
        ]
        + ([] if backward else [VMEM((3, 4, 8, BLOCK, features), BF16)]),
        compiler_params=pltpu.CompilerParams(vmem_limit_bytes=VMEM_LIMIT),
        cost_estimate=cost(6 * forward + 12 * backward),
        name="ffn_" + ("f" if forward else "") + ("b" if backward else ""),
    )(order, vec, *weights, *ins.values())


def attn_backward_body(
    first,
    count,
    places,
    whole_step,
    order_ref,
    e_ref,
    do_ref,
    qkv_ref,
    x_ref,
    gm_ref,
    *refs,
):
    if whole_step:
        weights, refs = refs[:8], refs[8:]
        gm_out, dvec_out, *grads, w_ref, dqkv_s, ds_s, g_s, sem, sem_g = refs
    else:
        dqkv_s, dvec_out, *grads, ds_s, g_s, sem_g = refs
    step = pl.program_id(0)
    tokens, features = x_ref.shape
    lane = lax.broadcasted_iota(jnp.int32, (tokens, 128), 1)
    low_half = lane < HEAD_DIM
    column = lane % HEAD_DIM
    width = 128 * count

    if whole_step:

        @pl.when(step == 0)
        def _():
            fetch_attn(order_ref, weights, places, w_ref, sem, pl.ds(first * 128, width))

    query = qkv_ref[0, 0]
    key_t = qkv_ref[1, 0].T
    value = qkv_ref[2, 0]
    chunk = CHUNK
    dquery, dkey, dvalue = [], [], []
    for head in range(2):
        inside = low_half if head == 0 else ~low_half
        ones = jnp.where(column // 2 == 2 * (step + first) + head, 1.0, 0.0).astype(BF16)
        value_aug = jnp.where(inside, value, ones)
        key_head = key_t[head * HEAD_DIM : (head + 1) * HEAD_DIM]
        parts = []
        for start in range(0, tokens, chunk):
            columns = slice(start, start + chunk)
            dchances = mm(value_aug, do_ref[head, columns], NT)
            dscores = (e_ref[head, :, columns].astype(F32) * dchances).astype(BF16)
            ds_s[head, :, columns] = dscores
            parts.append(mm(key_head, dscores, NN))
        dquery.append(jnp.concatenate(parts, axis=1))
        dkey.append(mm(ds_s[head], query, NN))
        dvalue.append(mm(e_ref[head], do_ref[head], NN))
    here = pl.ds(pl.multiple_of(step * 128, 128), 128)
    dqkv_s[0, :, here] = (jnp.concatenate(dquery, axis=0).T * 0.125).astype(BF16)
    dqkv_s[1, :, here] = jnp.where(low_half, dkey[0], dkey[1]).astype(BF16)
    dqkv_s[2, :, here] = jnp.where(low_half, dvalue[0], dvalue[1]).astype(BF16)

    @pl.when(step == count - 1)
    def _():
        x = x_ref[...]
        for part in range(3):
            g_s[16 * part : 16 * part + 16] = (
                mm(x, dqkv_s[part], TN).astype(BF16).reshape((16, 2, BLOCK, width))
            )
        for index, ref in enumerate(grads):
            core = order_ref[AT_CORE] if index == 0 else 1 - order_ref[AT_CORE]
            pltpu.make_async_copy(g_s.at[:, core], ref, sem_g).start()
        if whole_step:
            wait_all(w_ref, sem)
            gm = gm_ref[...]
            for part in range(3):
                gm = gm + mm(dqkv_s[part], w_ref[part].reshape(features, width), NT)
            gm_out[...] = gm
        dvec_out[...] = jnp.zeros_like(dvec_out)
        column_sum(dvec_out, 0, dqkv_s[0])
        column_sum(dvec_out, 1, dqkv_s[2])
        wait_all(g_s, sem_g)


def attn_backward(order, first, count, e, e_first, do, qkv, x, gm, weights, places):
    tokens, features = x.shape
    width = 128 * count
    half = jax.ShapeDtypeStruct((16 * 3, BLOCK, width), BF16)
    whole_step = weights is not None
    operands = [order, e, do, qkv, x] + ([gm, *weights] if whole_step else [x])
    in_specs = [
        whole(pltpu.SMEM),
        pl.BlockSpec((2, tokens, tokens), lambda step: (step + e_first, 0, 0)),
        pl.BlockSpec((2, tokens, 128), lambda step: (step + first, 0, 0)),
        pl.BlockSpec((3, 1, tokens, 128), lambda step: (0, step + first, 0, 0)),
        fixed(x.shape),
    ]
    scratch = [
        VMEM((2, tokens, tokens), BF16),
        VMEM((16 * 3, 2, BLOCK, width), BF16),
    ]
    if whole_step:
        in_specs += [fixed(gm.shape)] + [whole(pltpu.HBM)] * len(weights)
        result = jax.ShapeDtypeStruct((tokens, features), F32)
        scratch = [VMEM((3, 4, 8, BLOCK, width), BF16), VMEM((3, tokens, width), BF16)] + scratch
        scratch.append(pltpu.SemaphoreType.DMA)
    else:
        in_specs.append(whole(ANY))
        result = jax.ShapeDtypeStruct((3, tokens, width), BF16)
    return pl.pallas_call(
        functools.partial(attn_backward_body, first, count, places, whole_step),
        grid=(count,),
        out_shape=(result, jax.ShapeDtypeStruct((8, width), F32), half, half),
        in_specs=in_specs,
        out_specs=(fixed(result.shape), fixed((8, width))) + (whole(ANY),) * 2,
        scratch_shapes=scratch + [pltpu.SemaphoreType.DMA],
        compiler_params=pltpu.CompilerParams(vmem_limit_bytes=VMEM_LIMIT),
        cost_estimate=cost(26),
        name="attn_backward",
    )(*operands)


def input_gradient(order, dqkv, dz, weights, places):
    tokens, features = dz.shape
    tile = tokens // 4

    def body(order_ref, dqkv_ref, dz_ref, *refs):
        parts, (out, w_ref, sem) = refs[:8], refs[8:]

        @pl.when(pl.program_id(0) == 0)
        def _():
            fetch_attn(order_ref, parts, places, w_ref, sem, pl.ds(0, features))
            wait_all(w_ref, sem)

        total = dz_ref[...]
        for part in range(3):
            total = total + mm(dqkv_ref[part], w_ref[part].reshape(features, features), NT)
        out[...] = total

    return pl.pallas_call(
        body,
        grid=(4,),
        out_shape=jax.ShapeDtypeStruct((tokens, features), F32),
        in_specs=[
            whole(pltpu.SMEM),
            pl.BlockSpec((3, tile, features), lambda step: (0, step, 0)),
            rows_of(tile, features),
        ]
        + [whole(pltpu.HBM)] * len(weights),
        out_specs=rows_of(tile, features),
        scratch_shapes=[
            VMEM((3, 4, 8, BLOCK, features), BF16),
            pltpu.SemaphoreType.DMA,
        ],
        compiler_params=pltpu.CompilerParams(vmem_limit_bytes=VMEM_LIMIT),
        cost_estimate=cost(4),
        name="input_gradient",
    )(order, dqkv, dz, *weights)


def blocks_of(matrix, features):
    rows, columns = matrix.shape
    shaped = matrix.reshape(rows // BLOCK, BLOCK, columns // features, features)
    return shaped.transpose(0, 2, 1, 3)


def matrix_of(blocks):
    rows, columns, block, features = blocks.shape
    return blocks.transpose(0, 2, 1, 3).reshape(rows * block, columns * features)


CORE, X, Y, Z = 1, 2, 4, 8
Z_MASKS = (0, Z, 2 * Z, 3 * Z)
PLANE_MASKS = (0, X, Y, X | Y)
LOW_MASKS = [
    core | second | first
    for high, low in ((X, Y), (Y, X))
    for core in (0, CORE)
    for second in (0, high)
    for first in (0, low)
]


def swap(part, mask):
    return lax.ppermute(part, AXES, [(device, device ^ mask) for device in range(32)])


def after(value, *earlier):
    return lax.optimization_barrier((value, earlier))[0]


def prepare(place, in_w, out_w, up_w, down_w, vectors, final_norm):
    _, block, features = out_w.shape
    groups = up_w.shape[2] // features
    width, spread = vectors.shape[1], final_norm.shape[0]

    def body(place_ref, in_ref, out_ref, up_ref, down_ref, vec_ref, last_ref, *refs):
        own, rows = refs[:3], refs[3]
        rows[...] = jnp.zeros_like(rows)
        rows[0:2, :width] = vec_ref[...].astype(F32)
        rows[8:9, :spread] = last_ref[...].astype(F32)
        field = rows[0:8, :256]
        field = jnp.where(place_ref[AT_FIELDS] == 0, field, pltpu.roll(field, 64, 1))
        last = rows[8:16, :128]
        chosen = last
        for turn in range(1, 128 // spread):
            turned = pltpu.roll(last, turn * spread, 1)
            chosen = jnp.where(place_ref[AT_FIELDS + 1] == turn * spread, turned, chosen)
        rows[...] = jnp.zeros_like(rows)
        rows[0:1, :256] = field[0:1]
        rows[0:1, 256:512] = field[1:2]
        rows[1:2, :128] = chosen[0:1]
        parts = lambda ref, layer, count: [
            ref[layer, :, features * j : features * (j + 1)] for j in range(count)
        ]
        qkv = [parts(in_ref, layer, 3) for layer in range(2)]
        up = [parts(up_ref, layer, groups) for layer in range(2)]
        down = [
            [down_ref[layer, block * j : block * (j + 1)] for j in range(groups)]
            for layer in range(2)
        ]
        out = [out_ref[layer] for layer in range(2)]
        laid = [
            qkv[0] + [rows[...].astype(BF16)],
            qkv[1][:2] + up[0] + qkv[1][2:] + [out[0]] + down[0],
            up[1] + [out[1]] + down[1],
        ]
        for ref, pieces in zip(own, laid):
            for index, piece in enumerate(pieces):
                ref[index] = piece

    outs = [(count, block, features) for count in (4, 2 * groups + 4, 2 * groups + 1)]
    operands = (in_w, out_w, up_w, down_w, vectors, final_norm[None])
    return pl.pallas_call(
        body,
        grid=(1,),
        out_shape=tuple(jax.ShapeDtypeStruct(shape, BF16) for shape in outs),
        in_specs=[whole(pltpu.SMEM)] + [fixed(part.shape) for part in operands],
        out_specs=tuple(fixed(shape) for shape in outs),
        scratch_shapes=[VMEM((block, features), F32)],
        compiler_params=pltpu.CompilerParams(vmem_limit_bytes=VMEM_LIMIT),
        name="prepare",
    )(place, *operands)


def gather_z(own):
    return [hold(own)] + [swap(own, mask) for mask in Z_MASKS[1:]]


def pack_z(place, pieces):
    blocks, *rest = pieces[0].shape

    def body(place_ref, *refs):
        for index in range(4):
            refs[4][:, place_ref[AT_Z] ^ index] = refs[index][...]

    return pl.pallas_call(
        body,
        out_shape=jax.ShapeDtypeStruct((blocks, 4, *rest), BF16),
        in_specs=[whole(pltpu.SMEM)] + [whole()] * 4,
        out_specs=whole(),
        compiler_params=pltpu.CompilerParams(vmem_limit_bytes=SMALL_VMEM),
        name="pack_z",
    )(place, *pieces)


def gather_first(four, cut):
    streams = (four[:cut], Y, X), (four[cut:], X, Y)
    return [(part, swap(part, first), second) for part, first, second in streams]


def gather_second(streams, near):
    return [swap(part, second) for part, (_, _, second) in zip(near, streams)]


def join_two(streams):
    def body(a_ref, b_ref, c_ref, d_ref, out0, out1):
        out0[0], out0[1] = a_ref[...], b_ref[...]
        out1[0], out1[1] = c_ref[...], d_ref[...]

    parts = [part for near, far, _ in streams for part in (near, far)]
    shapes = [(2, *parts[0].shape), (2, *parts[2].shape)]
    return pl.pallas_call(
        body,
        out_shape=tuple(jax.ShapeDtypeStruct(shape, BF16) for shape in shapes),
        in_specs=[whole()] * 4,
        out_specs=(whole(), whole()),
        compiler_params=pltpu.CompilerParams(vmem_limit_bytes=SMALL_VMEM),
        name="join_two",
    )(*parts)


def gather_core(near, far, late):
    near = after(near, far) if late else near
    return [
        part
        for pair in zip(near, far)
        for part in (*pair, *[swap(half, CORE) for half in pair])
    ]


def sum_core(mine, other):
    return hold(mine), swap(other, CORE)


def hold(part):
    def body(in_ref, out_ref, sem):
        copy = pltpu.make_async_copy(in_ref, out_ref, sem)
        copy.start()
        copy.wait()

    return pl.pallas_call(
        body,
        out_shape=jax.ShapeDtypeStruct(part.shape, part.dtype),
        in_specs=[whole(pltpu.HBM)],
        out_specs=whole(),
        scratch_shapes=[pltpu.SemaphoreType.DMA],
        compiler_params=pltpu.CompilerParams(vmem_limit_bytes=SMALL_VMEM),
        cost_estimate=cost(1),
        name="hold",
    )(part)


def sum_plane(place, pairs):
    pairs = [[part.reshape(-1, 4, 4, *part.shape[1:]) for part in pair] for pair in pairs]
    kept, got = zip(*pairs)
    rest = kept[0].shape[3:]
    sizes = [part.shape[0] for part in kept]

    def body(place_ref, *refs):
        outs = refs[2 * len(sizes) :]
        start = 0
        for index, size in enumerate(sizes):
            left, right = refs[index], refs[len(sizes) + index]
            for mask, out in enumerate(outs):
                plane = place_ref[AT_PLANE] ^ mask
                out[start : start + size] = (
                    left[:, :, plane].astype(F32) + right[:, :, plane].astype(F32)
                ).astype(BF16)
            start += size

    return pl.pallas_call(
        body,
        out_shape=(jax.ShapeDtypeStruct((sum(sizes), 4, *rest), BF16),) * 4,
        in_specs=[whole(pltpu.SMEM)] + [whole()] * (2 * len(sizes)),
        out_specs=(whole(),) * 4,
        compiler_params=pltpu.CompilerParams(vmem_limit_bytes=SMALL_VMEM),
        name="sum_plane",
    )(place, *kept, *got)


def send_plane(parts):
    return [parts[0]] + [swap(part, mask) for part, mask in zip(parts[1:], PLANE_MASKS[1:])]


def sum_z(place, parts):
    blocks, _, *rest = parts[0].shape
    count = 3 if blocks % 3 == 0 else 1

    def body(place_ref, *refs):
        for mask in range(4):
            z = place_ref[AT_Z] ^ mask
            total = refs[0][:, z].astype(F32)
            for ref in refs[1:4]:
                total = total + ref[:, z].astype(F32)
            refs[4 + mask][...] = total.astype(BF16)

    return pl.pallas_call(
        body,
        grid=(blocks // count,),
        out_shape=(jax.ShapeDtypeStruct((blocks, *rest), BF16),) * 4,
        in_specs=[whole(pltpu.SMEM)]
        + [pl.BlockSpec((count, 4, *rest), lambda step: (step, 0, 0, 0))] * 4,
        out_specs=(pl.BlockSpec((count, *rest), lambda step: (step, 0, 0)),) * 4,
        compiler_params=pltpu.CompilerParams(vmem_limit_bytes=SMALL_VMEM),
        name="sum_z",
    )(place, *parts)


def send_z(pieces):
    return [pieces[0]] + [swap(piece, mask) for piece, mask in zip(pieces[1:], Z_MASKS[1:])]


def finish(place, ffn1, ffn0, attn0, width, spread):
    _, block, features = ffn1[0].shape
    groups = (ffn1[0].shape[0] - 1) // 2

    def body(place_ref, *refs):
        parts = [refs[:4], refs[4:8], refs[8:12]]
        in_out, out_out, up_out, down_out, vec_out, last_out = refs[12:]

        def total(part, index):
            value = parts[part][0][index].astype(F32)
            for ref in parts[part][1:]:
                value = value + ref[index].astype(F32)
            return value

        for layer, part in ((1, 0), (0, 1)):
            for j in range(groups):
                up_out[layer, :, features * j : features * (j + 1)] = total(part, j)
                down_out[layer, block * j : block * (j + 1)] = total(part, groups + 1 + j)
            out_out[layer] = total(part, groups)
        for layer, part, start in ((1, 1, 2 * groups + 1), (0, 2, 0)):
            for j in range(3):
                in_out[layer, :, features * j : features * (j + 1)] = total(part, start + j)
        rows = total(2, 3)
        for layer in range(2):
            field = rows[0:8, 256 * layer : 256 * layer + 256]
            turned = pltpu.roll(field, 192, 1)
            chosen = jnp.where(place_ref[AT_FIELDS] == 0, field, turned)
            vec_out[layer : layer + 1] = chosen[0:1, :width]
        field = rows[0:8, :128]
        chosen = field
        for turn in range(1, 128 // spread):
            turned = pltpu.roll(field, 128 - turn * spread, 1)
            chosen = jnp.where(place_ref[AT_FIELDS + 1] == turn * spread, turned, chosen)
        last_out[...] = chosen[1:2, :spread]

    shapes = [
        (2, block, 3 * features),
        (2, block, features),
        (2, block, groups * features),
        (2, block * groups, features),
        (2, width),
        (1, spread),
    ]
    return pl.pallas_call(
        body,
        out_shape=tuple(jax.ShapeDtypeStruct(shape, F32) for shape in shapes),
        in_specs=[whole(pltpu.SMEM)] + [whole()] * 12,
        out_specs=tuple(whole() for _ in shapes),
        compiler_params=pltpu.CompilerParams(vmem_limit_bytes=SMALL_VMEM),
        name="finish",
    )(place, *ffn1, *ffn0, *attn0)


def field_of(device, width):
    start = device * width
    return start // 128 * 128, start % 128


def unpack_vectors(order, parts, width, spread):
    def body(order_ref, *refs):
        refs, out, flat, last = refs[:4], *refs[4:]
        flat[...] = jnp.zeros_like(flat)
        last[...] = jnp.zeros_like(last)
        out[...] = jnp.zeros_like(out)
        for index, ref in enumerate(refs):
            for near, z in [(near, z) for near in range(2) for z in range(4)]:
                owner = 8 * z + order_ref[8 + 2 * index + near]
                rows = ref[near, 0, z].astype(F32)
                at = pl.ds(pl.multiple_of(owner * width // 128 * 128, 128), 256)
                for layer in range(2):
                    flat[layer : layer + 1, at] += rows[0:1, 256 * layer : 256 * layer + 256]
                at = pl.ds(pl.multiple_of(owner * spread // 128 * 128, 128), 128)
                last[0:1, at] += rows[1:2, :128]
        for layer in range(2):
            for row in range(12):
                out[layer, row : row + 1] = flat[layer : layer + 1, row * 512 : row * 512 + 512]
            for row in range(2):
                out[layer, 12 + row : 13 + row] = last[0:1, row * 512 : row * 512 + 512]

    features = parts[0].shape[-1]
    at = parts[0].shape[1] - 1
    return pl.pallas_call(
        body,
        grid=(1,),
        out_shape=jax.ShapeDtypeStruct((2, 16, features), F32),
        in_specs=[whole(pltpu.SMEM)]
        + [
            pl.BlockSpec((2, 1, *part.shape[2:]), lambda step: (0, at, 0, 0, 0)) for part in parts
        ],
        out_specs=fixed((2, 16, features)),
        scratch_shapes=[VMEM((8, 12 * features), F32), VMEM((8, 2 * features), F32)],
        compiler_params=pltpu.CompilerParams(vmem_limit_bytes=SMALL_VMEM),
        name="unpack_vectors",
    )(order, *parts)


def pack_vectors(order, attn_rows, ffn_rows, width, spread):
    features = ffn_rows[0].shape[1]

    def body(order_ref, a0, a1, f0, f1, out0, out1, flat, last):
        for layer, (attn, ffn) in enumerate(((a0, f0), (a1, f1))):
            for row in range(12):
                source = attn if row < 2 else ffn
                flat[layer : layer + 1, row * 512 : row * 512 + 512] = source[row : row + 1]
        for row in range(2):
            last[0:1, row * 512 : row * 512 + 512] = f1[12 + row : 13 + row]
        for half, out in enumerate((out0, out1)):
            out[...] = jnp.zeros_like(out)
            core = order_ref[AT_CORE] if half == 0 else 1 - order_ref[AT_CORE]
            for pair in range(16):
                owner = 2 * pair + core
                at = pl.ds(pl.multiple_of(owner * width // 128 * 128, 128), 256)
                fields = [flat[layer : layer + 1, at] for layer in range(2)]
                at = pl.ds(pl.multiple_of(owner * spread // 128 * 128, 128), 128)
                final = jnp.concatenate([last[0:1, at], jnp.zeros((1, 384), F32)], axis=1)
                rows = [jnp.concatenate(fields, axis=1), final, jnp.zeros((BLOCK - 2, 512), F32)]
                out[pair] = jnp.concatenate(rows, axis=0).astype(BF16)

    return pl.pallas_call(
        body,
        out_shape=(jax.ShapeDtypeStruct((16, BLOCK, features), BF16),) * 2,
        in_specs=[whole(pltpu.SMEM)] + [whole()] * 4,
        out_specs=(whole(), whole()),
        scratch_shapes=[VMEM((8, 12 * features), F32), VMEM((8, 2 * features), F32)],
        compiler_params=pltpu.CompilerParams(vmem_limit_bytes=SMALL_VMEM),
        name="pack_vectors",
    )(order, *attn_rows, *ffn_rows)


def total_of(pieces):
    total = pieces[0].astype(F32)
    for piece in pieces[1:]:
        total = total + piece.astype(F32)
    return total


def local(
    main_residual,
    side_residual,
    cotangent,
    lengths,
    input_weight,
    output_weight,
    expand_weight,
    reduce_weight,
    vectors,
    final_norm,
):
    tokens, features = main_residual.shape
    layers = input_weight.shape[0]
    assert lengths.shape[0] == 1 and layers == 2
    per = features // BLOCK
    pairs = features // 128
    half_pairs = pairs // 2
    groups = expand_weight.shape[2] // features
    fast = lax.axis_size(AXES) == 32 and per == 32
    ffn_at = ((2, (1, 1), 2), (0, (0, groups), 0))
    width = vectors.shape[1]
    spread = final_norm.shape[0]

    def vec_rows(all_vectors, final_full):
        return jnp.concatenate(
            [
                all_vectors.reshape(layers, 12, features),
                jnp.broadcast_to(final_full.reshape(1, 2, features), (layers, 2, features)),
                jnp.zeros((layers, 2, features), F32),
            ],
            axis=1,
        )

    if fast:
        me = lax.axis_index(AXES)
        table = [
            [(device ^ mask) & 7 for mask in LOW_MASKS]
            + [device // Z, device // X & 3, device & CORE]
            + [field_of(device, width)[1], field_of(device, spread)[1]]
            for device in range(32)
        ]
        order = jnp.array(table, jnp.int32)[me]
        own = prepare(
            order, input_weight, output_weight, expand_weight, reduce_weight, vectors, final_norm
        )
        z0 = gather_z(own[0])
        z1 = gather_z(after(own[1], z0[1:]))
        two = gather_first(pack_z(order, z0), 2)
        near = join_two(two)
        far = gather_second(two, near)
        attn0 = gather_core(near, far, True)
        vec = unpack_vectors(order, attn0[4:], width, spread)
        four = pack_z(order, after(z1, near))
        two = gather_first(after(four, far[0]), groups + 2)
        two = [(part, after(got, vec), mask) for part, got, mask in two]
        z2 = gather_z(after(own[2], attn0))
        near = join_two(two)
        far = gather_second(two, near)
        x0 = after(main_residual, near)
    else:
        gather = lambda part, axis: lax.all_gather(part, AXES, axis=axis, tiled=True)
        order = jnp.array(LOW_MASKS + [0] * 5, jnp.int32)

        def streams(*two):
            parts = []
            for stream, blocks in enumerate(two):
                joined = jnp.concatenate(blocks, axis=1)
                joined = joined.reshape(4, 8, *joined.shape[1:]).transpose(1, 2, 0, 3, 4)
                lows = LOW_MASKS[8 * stream : 8 * stream + 8]
                parts += [joined[jnp.array(lows[at : at + 2])] for at in range(0, 8, 2)]
            return parts

        vec = vec_rows(gather(vectors, 1).astype(F32), gather(final_norm, 0).astype(F32))
        parts = []
        for layer in range(layers):
            qkv = blocks_of(gather(input_weight[layer], 0), features)
            up = blocks_of(gather(expand_weight[layer], 0), features)
            out = blocks_of(gather(output_weight[layer], 0), features)
            down = gather(reduce_weight[layer], 0).reshape(per, -1, BLOCK, features)
            parts.append((qkv, up, out, down))
        (qkv0, up0, out0, down0), (qkv1, up1, out1, down1) = parts
        attn0 = streams([qkv0[:, :2]], [qkv0[:, 2:]])
        mixed = streams([qkv1[:, :2], up0], [qkv1[:, 2:], out0, down0])
        ffn1 = streams([up1, out1], [down1])
        x0 = main_residual

    e0, ctx0, rinv0, qkv0 = attn_forward(
        lengths, 0, pairs, None, order, x0, vec, attn0, 0, 0
    )
    x0 = main_residual
    if fast:
        far, z2 = after((far, z2), e0)
        mixed = gather_core(near, far, True)
        two = gather_first(pack_z(order, z2), groups + 1)
        x0 = after(x0, *[part for part, _, _ in two])
    xh1, xh2, stat, m1b, hid, m2, m2b, y, qkv1 = ffn_call(
        True, False, False, 0, order, vec, mixed, ffn_at[0], ctx0, (x0, side_residual)
    )
    if fast:
        two = [(part, after(got, m2b), mask) for part, got, mask in two]
        near = join_two(two)
        qkv1 = after(qkv1, near)
        far = gather_second(two, near)
    e1, ctx1, rinv1 = attn_forward(lengths, 0, pairs, qkv1)
    if fast:
        ffn1 = gather_core(near, after(far, e1), False)
    layer_out, grad_side, gm, do, dvec1, *gf1 = ffn_call(
        True, True, True, 1, order, vec, ffn1, ffn_at[1], ctx1, (m2, y, cotangent), rinv1
    )
    if fast:
        f1 = sum_plane(order, [sum_core(*gf1)])
        gm = after(gm, f1)
        f1 = send_plane(f1)
    gm, dvec1a, *gi1 = attn_backward(
        order, 0, pairs, e1, 0, do, qkv1, m2b, gm, mixed, 0
    )
    if fast:
        i1 = (gi1[0], swap(gi1[1], CORE))
        f1 = sum_z(order, after(f1, gm))
        gm = after(gm, f1)
        f1 = send_z(f1)
    gm, do, dvec0, *gf0 = ffn_call(
        False, True, False, 0, order, vec, mixed, ffn_at[0], ctx0,
        (xh1, xh2, stat, m1b, hid, gm, grad_side), rinv0,
    )
    if fast:
        f1, i1 = after((f1, i1), gm)
        f0 = sum_plane(order, [sum_core(*after(gf0, f1)), (hold(i1[0]), i1[1])])
        do = after(do, f0)
        f0 = send_plane(f0)
    dqkv, dvec0a, *gi0 = attn_backward(
        order, 0, pairs, e0, 0, do, qkv0, main_residual, None, None, 0
    )
    if fast:
        rows = pack_vectors(order, (dvec0a, dvec1a), (dvec0, dvec1), width, spread)
        i0 = [sum_core(*gi0), sum_core(*rows)]
        f0 = send_z(sum_z(order, after(f0, dqkv)))
        i0 = send_plane(sum_plane(order, after(i0, f0[0])))
        gm, dqkv = after((gm, dqkv), f0[0], i0[0])
        grad_main = input_gradient(order, dqkv, gm, attn0, 0)
        i0 = send_z(sum_z(order, after(i0, grad_main)))
        grad_in, grad_out, grad_up, grad_down, grad_vec, grad_final = finish(
            order, f1, f0, i0, width, spread
        )
        grad_final = grad_final[0]
    else:
        grad_main = input_gradient(order, dqkv, gm, attn0, 0)
        scatter = lambda part, axis: lax.psum_scatter(
            part, AXES, scatter_dimension=axis, tiled=True
        ).astype(F32)

        def natural(even, odd):
            joined = jnp.stack([even, odd], axis=1)
            return joined.reshape(-1, per, *even.shape[1:]).swapaxes(0, 1)

        both = lambda make: jnp.stack(
            [make(natural(*i), natural(*f)) for i, f in ((gi0, gf0), (gi1, gf1))]
        )
        grad_in = scatter(both(lambda i, f: matrix_of(i)), 1)
        grad_up = scatter(both(lambda i, f: matrix_of(f[:, :groups])), 1)
        grad_out = scatter(both(lambda i, f: matrix_of(f[:, groups : groups + 1])), 1)
        grad_down = scatter(both(lambda i, f: f[:, groups + 1 :].reshape(-1, features)), 1)
        dvec = [
            jnp.concatenate([first[0:2], rest[2:12]]).reshape(-1)
            for first, rest in ((dvec0a, dvec0), (dvec1a, dvec1))
        ]
        grad_vec = scatter(jnp.stack(dvec), 1)
        grad_final = scatter(dvec1[12:14].reshape(-1), 0)
    return (
        layer_out,
        grad_main,
        grad_side,
        grad_in,
        grad_out,
        grad_up,
        grad_down,
        grad_vec,
        grad_final,
    )


def solution(mesh):
    rows = P(AXES, None)
    middle = P(None, AXES, None)
    return jax.shard_map(
        local,
        mesh=mesh,
        in_specs=(rows, rows, rows, rows, middle, middle, middle, middle, P(None, AXES), P(AXES)),
        out_specs=(rows, rows, rows, middle, middle, middle, middle, P(None, AXES), P(AXES)),
        check_vma=False,
    )
```
